128 devices in a mesh: dp: 16 (over y, x), ctx: 8 (over z, core).
Axes of the slice: x: 4, y: 4, z: 4, core: 2. Of those that a mesh axis runs over, the one named last changes fastest.
Arguments:
- tokens: bfloat16 [16, 1024, 2048], P('dp', 'ctx'), may hold values from -6 to 6
- cotangent: bfloat16 [16, 1024, 2048], P('dp', 'ctx'), may hold values from -6 to 6
- w_query: float32 [2048, 2048], P('dp', 'ctx'), may hold values from -0.125 to 0.125
- query_first: float32 [2048, 2048], P('dp', 'ctx'), may hold values from -80 to 80
- query_second: float32 [2048, 2048], P('dp', 'ctx'), may hold values from 868.352 to 3440.64
- w_key: float32 [2048, 256], P(('dp', 'ctx')), may hold values from -0.125 to 0.125
- key_first: float32 [2048, 256], P(('dp', 'ctx')), may hold values from -256 to 256
- key_second: float32 [2048, 256], P(('dp', 'ctx')), may hold values from 6946.816 to 27525.12
- w_value: float32 [2048, 256], P(('dp', 'ctx')), may hold values from -0.125 to 0.125
- value_first: float32 [2048, 256], P(('dp', 'ctx')), may hold values from -256 to 256
- value_second: float32 [2048, 256], P(('dp', 'ctx')), may hold values from 6946.816 to 27525.12
- w_out: float32 [2048, 2048], P('ctx', 'dp'), may hold values from -1 to 1
- out_first: float32 [2048, 2048], P('ctx', 'dp'), may hold values from -4 to 4
- out_second: float32 [2048, 2048], P('ctx', 'dp'), may hold values from 1.696 to 6.72
- w_gate: float32 [2048, 5632], P('dp', 'ctx'), may hold values from -0.125 to 0.125
- gate_first: float32 [2048, 5632], P('dp', 'ctx'), may hold values from -40 to 40
- gate_second: float32 [2048, 5632], P('dp', 'ctx'), may hold values from 212.992 to 868.352
- w_up: float32 [2048, 5632], P('dp', 'ctx'), may hold values from -0.125 to 0.125
- up_first: float32 [2048, 5632], P('dp', 'ctx'), may hold values from -40 to 40
- up_second: float32 [2048, 5632], P('dp', 'ctx'), may hold values from 212.992 to 868.352
- w_down: float32 [5632, 2048], P('ctx', 'dp'), may hold values from -0.078125 to 0.078125
- down_first: float32 [5632, 2048], P('ctx', 'dp'), may hold values from -40 to 40
- down_second: float32 [5632, 2048], P('ctx', 'dp'), may hold values from 212.992 to 868.352
- norm_gains: float32 [2, 2048], P(None, ('dp', 'ctx')), may hold values from 0.5 to 1.5
- gains_first: float32 [2, 2048], P(None, ('dp', 'ctx')), may hold values from -80 to 80
- gains_second: float32 [2, 2048], P(None, ('dp', 'ctx')), may hold values from 868.352 to 3440.64
Outputs:
- output: bfloat16 [16, 1024, 2048], P('dp', 'ctx')
- input_grad: bfloat16 [16, 1024, 2048], P('dp', 'ctx')
- query_new: float32 [2048, 2048], P('dp', 'ctx')
- query_first_new: float32 [2048, 2048], P('dp', 'ctx')
- query_second_new: float32 [2048, 2048], P('dp', 'ctx')
- key_new: float32 [2048, 256], P(('dp', 'ctx'))
- key_first_new: float32 [2048, 256], P(('dp', 'ctx'))
- key_second_new: float32 [2048, 256], P(('dp', 'ctx'))
- value_new: float32 [2048, 256], P(('dp', 'ctx'))
- value_first_new: float32 [2048, 256], P(('dp', 'ctx'))
- value_second_new: float32 [2048, 256], P(('dp', 'ctx'))
- out_new: float32 [2048, 2048], P('ctx', 'dp')
- out_first_new: float32 [2048, 2048], P('ctx', 'dp')
- out_second_new: float32 [2048, 2048], P('ctx', 'dp')
- gate_new: float32 [2048, 5632], P('dp', 'ctx')
- gate_first_new: float32 [2048, 5632], P('dp', 'ctx')
- gate_second_new: float32 [2048, 5632], P('dp', 'ctx')
- up_new: float32 [2048, 5632], P('dp', 'ctx')
- up_first_new: float32 [2048, 5632], P('dp', 'ctx')
- up_second_new: float32 [2048, 5632], P('dp', 'ctx')
- down_new: float32 [5632, 2048], P('ctx', 'dp')
- down_first_new: float32 [5632, 2048], P('ctx', 'dp')
- down_second_new: float32 [5632, 2048], P('ctx', 'dp')
- gains_new: float32 [2, 2048], P(None, ('dp', 'ctx'))
- gains_first_new: float32 [2, 2048], P(None, ('dp', 'ctx'))
- gains_second_new: float32 [2, 2048], P(None, ('dp', 'ctx'))
The draws below stay inside these ranges and needn't reach their ends.
All inputs are finite; a program needn't handle non-finite values.
Results may differ from the reference program's by a relative error of at most 0.025.
Values may be sent and summed in bfloat16 or wider, within the bound.
No kernel may reach another device: no remote copies, remote signals or barrier semaphores. Data moves between devices by JAX's collectives and lax.ppermute only.
A program may use at most 128 MiB of HBM per device.

```python
import math
import jax
import jax.numpy as jnp
from jax import lax

D = 2048
HEADS = 32
KV_HEADS = 4
HD = 64
FF = 5632
SEQ_LEN = 1024
STEP = 10
BATCH = 16
KVW = 256
N_DP = 16


def level_of(own_key, shape, shards, least, high):
    factor_of, own = 1.0, jax.random.fold_in(own_key, 6)
    for dim, blocks in shards:
        draws = jnp.exp(jax.random.uniform(jax.random.fold_in(own, dim), (blocks,), jnp.float32, least / len(shards), high / len(shards)))
        factor_of = factor_of * jnp.repeat(draws, shape[dim] // blocks).reshape([-1 if axis == dim else 1 for axis in range(len(shape))])
    return factor_of


def normal_values(rng, shape, deviation, reach, shards=(), kind=jnp.bfloat16):
    array = deviation * jax.random.normal(rng, shape, jnp.float32)
    if shards:
        array = array * level_of(rng, shape, shards, -0.22, 0.18)
    return jnp.clip(array, -reach, reach).astype(kind)


def setup_inputs(seed: int = 0) -> dict:
    splits = jax.random.split(jax.random.key(seed), 27)
    tokens = normal_values(splits[0], (BATCH, SEQ_LEN, D), 1.0, 6.0, ((0, 16), (1, 8)))
    cotangent = normal_values(splits[1], (BATCH, SEQ_LEN, D), 1.0, 6.0, ((0, 16), (1, 8)))
    w_query = normal_values(splits[2], (D, D), D ** -0.5, 0.125, ((0, 16), (1, 8)), jnp.float32)
    query_first = normal_values(splits[3], (D, D), (0.11 * (N_DP * SEQ_LEN) ** 0.5), 80.0, ((0, 16), (1, 8)), jnp.float32)
    query_second = jnp.clip(jnp.exp(math.log(3440.64) - 1.3768156 * jax.random.uniform(splits[4], (D, D), jnp.float32) ** level_of(splits[4], (D, D), ((0, 16), (1, 8)), -0.2, 0.2)), 868.352, 3440.64)
    w_key = normal_values(splits[5], (D, KVW), D ** -0.5, 0.125, ((0, 128),), jnp.float32)
    key_first = normal_values(splits[6], (D, KVW), (0.11 * ((HEADS // KV_HEADS) * N_DP * SEQ_LEN) ** 0.5), 256.0, ((0, 128),), jnp.float32)
    key_second = jnp.clip(jnp.exp(math.log(27525.12) - 1.3768156 * jax.random.uniform(splits[7], (D, KVW), jnp.float32) ** level_of(splits[7], (D, KVW), ((0, 128),), -0.2, 0.2)), 6946.816, 27525.12)
    w_value = normal_values(splits[8], (D, KVW), D ** -0.5, 0.125, ((0, 128),), jnp.float32)
    value_first = normal_values(splits[9], (D, KVW), (0.11 * ((HEADS // KV_HEADS) * N_DP * SEQ_LEN) ** 0.5), 256.0, ((0, 128),), jnp.float32)
    value_second = jnp.clip(jnp.exp(math.log(27525.12) - 1.3768156 * jax.random.uniform(splits[10], (D, KVW), jnp.float32) ** level_of(splits[10], (D, KVW), ((0, 128),), -0.2, 0.2)), 6946.816, 27525.12)
    w_out = normal_values(splits[11], (D, D), (max(1, 16 * D // SEQ_LEN)) ** -0.5, 1.0, ((0, 8), (1, 16)), jnp.float32)
    out_first = normal_values(splits[12], (D, D), (0.11 * (2 * N_DP) ** 0.5), 4.0, ((0, 8), (1, 16)), jnp.float32)
    out_second = jnp.clip(jnp.exp(math.log(6.72) - 1.3768156 * jax.random.uniform(splits[13], (D, D), jnp.float32) ** level_of(splits[13], (D, D), ((0, 8), (1, 16)), -0.2, 0.2)), 1.696, 6.72)
    w_gate = normal_values(splits[14], (D, FF), D ** -0.5, 0.125, ((0, 16), (1, 8)), jnp.float32)
    gate_first = normal_values(splits[15], (D, FF), (0.055 * (N_DP * SEQ_LEN) ** 0.5), 40.0, ((0, 16), (1, 8)), jnp.float32)
    gate_second = jnp.clip(jnp.exp(math.log(868.352) - 1.40534252 * jax.random.uniform(splits[16], (D, FF), jnp.float32) ** level_of(splits[16], (D, FF), ((0, 16), (1, 8)), -0.2, 0.2)), 212.992, 868.352)
    w_up = normal_values(splits[17], (D, FF), D ** -0.5, 0.125, ((0, 16), (1, 8)), jnp.float32)
    up_first = normal_values(splits[18], (D, FF), (0.055 * (N_DP * SEQ_LEN) ** 0.5), 40.0, ((0, 16), (1, 8)), jnp.float32)
    up_second = jnp.clip(jnp.exp(math.log(868.352) - 1.40534252 * jax.random.uniform(splits[19], (D, FF), jnp.float32) ** level_of(splits[19], (D, FF), ((0, 16), (1, 8)), -0.2, 0.2)), 212.992, 868.352)
    w_down = normal_values(splits[20], (FF, D), FF ** -0.5, 0.078125, ((0, 8), (1, 16)), jnp.float32)
    down_first = normal_values(splits[21], (FF, D), (0.055 * (N_DP * SEQ_LEN) ** 0.5), 40.0, ((0, 8), (1, 16)), jnp.float32)
    down_second = jnp.clip(jnp.exp(math.log(868.352) - 1.40534252 * jax.random.uniform(splits[22], (FF, D), jnp.float32) ** level_of(splits[22], (FF, D), ((0, 8), (1, 16)), -0.2, 0.2)), 212.992, 868.352)
    norm_gains = jnp.clip(1.0 + 0.1 * jax.random.normal(splits[23], (2, D), jnp.float32), 0.5, 1.5)
    gains_first = normal_values(splits[24], (2, D), (0.11 * (N_DP * SEQ_LEN) ** 0.5), 80.0, ((1, 128),), jnp.float32)
    gains_second = jnp.clip(jnp.exp(math.log(3440.64) - 1.3768156 * jax.random.uniform(splits[25], (2, D), jnp.float32) ** level_of(splits[25], (2, D), ((1, 128),), -0.2, 0.2)), 868.352, 3440.64)
    return {"tokens": tokens, "cotangent": cotangent, "w_query": w_query, "query_first": query_first, "query_second": query_second, "w_key": w_key, "key_first": key_first, "key_second": key_second, "w_value": w_value, "value_first": value_first, "value_second": value_second, "w_out": w_out, "out_first": out_first, "out_second": out_second, "w_gate": w_gate, "gate_first": gate_first, "gate_second": gate_second, "w_up": w_up, "up_first": up_first, "up_second": up_second, "w_down": w_down, "down_first": down_first, "down_second": down_second, "norm_gains": norm_gains, "gains_first": gains_first, "gains_second": gains_second}


EPS = 1e-05
BETA_ONE = 0.9
BETA_TWO = 0.95
ADAM_EPS = 1e-08
DECAY = 0.1
HIGHEST = lax.Precision.HIGHEST

@jax.custom_vjp
def low(v):
    return lax.optimization_barrier(v.astype(jnp.bfloat16)).astype(jnp.float32)

@jax.custom_vjp
def low_back(v):
    return v

def low_keep(v):
    return (low(v), None)

def low_pass(kept, grad):
    return (grad,)

def back_keep(v):
    return (v, None)

def back_low(kept, grad):
    return (low(grad),)
low.defvjp(low_keep, low_pass)
low_back.defvjp(back_keep, back_low)

def tables(positions):
    half_width = HD // 2
    frequency = 10000.0 ** (-2.0 * jnp.arange(half_width).astype(jnp.float32) / HD)
    angles = positions.astype(jnp.float32)[:, None] * frequency[None, :]
    return (jnp.cos(angles)[:, None, :], jnp.sin(angles)[:, None, :])

def rotate(inputs, cos_table, sine_table):
    half_width = inputs.shape[-1] // 2
    first_half = inputs[..., :half_width]
    second_half = inputs[..., half_width:]
    return jnp.concatenate([first_half * cos_table - second_half * sine_table, second_half * cos_table + first_half * sine_table], axis=-1)

def normed(inputs, gain_row):
    inv_rms = lax.rsqrt(lax.optimization_barrier(jnp.mean(inputs * inputs, axis=-1, keepdims=True)) + EPS)
    return inputs * inv_rms * gain_row

def matmul(left, right):
    return jnp.dot(left, right, precision=HIGHEST)

def layer_sequence(sequence, w_query, w_key, w_value, w_out, w_gate, w_up, w_down, norm_gains):
    length = sequence.shape[0]
    group_size = HEADS // KV_HEADS
    cos_table, sine_table = tables(jnp.arange(length))
    normed_in = low(normed(sequence, norm_gains[0]))
    query = low_back(matmul(normed_in, w_query)).reshape(length, HEADS, HD)
    key_proj = low_back(matmul(normed_in, w_key)).reshape(length, KV_HEADS, HD)
    values = low(low_back(matmul(normed_in, w_value))).reshape(length, KV_HEADS, HD)
    query = low(rotate(query, cos_table, sine_table)).reshape(length, KV_HEADS, group_size, HD)
    key_proj = low(rotate(key_proj, cos_table, sine_table))
    scores = jnp.einsum('qkgd,skd->kgqs', query, key_proj, precision=HIGHEST)
    scores = low_back(scores * HD ** (-0.5))
    causal = jnp.arange(length)[:, None] >= jnp.arange(length)[None, :]
    scores = jnp.where(causal, scores, -1e+30)
    row_max = lax.optimization_barrier(jnp.max(scores, axis=-1, keepdims=True))
    exponent = jnp.exp(scores - row_max)
    probabilities = low(exponent / lax.optimization_barrier(jnp.sum(exponent, axis=-1, keepdims=True)))
    attended = jnp.einsum('kgqs,skd->qkgd', probabilities, values, precision=HIGHEST).reshape(length, HEADS * HD)
    attended = low(low_back(attended))
    middle = sequence + low_back(matmul(attended, w_out))
    normed_mid = low(normed(middle, norm_gains[1]))
    gate_proj = low_back(matmul(normed_mid, w_gate))
    up_proj = low_back(matmul(normed_mid, w_up))
    hidden = low(jax.nn.silu(gate_proj) * up_proj)
    return middle + low_back(matmul(hidden, w_down))

def forward(inputs, w_query, w_key, w_value, w_out, w_gate, w_up, w_down, norm_gains):
    low_query = low(w_query)
    low_key = low(w_key)
    low_value = low(w_value)
    low_out = low(w_out)
    low_gate = low(w_gate)
    low_up = low(w_up)
    low_down = low(w_down)
    low_gains = low(norm_gains)

    def per_sequence(sequence):
        return layer_sequence(sequence, low_query, low_key, low_value, low_out, low_gate, low_up, low_down, low_gains)
    return lax.map(jax.checkpoint(per_sequence), inputs)

def adamw_step(weight, first, second, gradient, rate, decay):
    first_new = BETA_ONE * first + (1.0 - BETA_ONE) * gradient
    second_new = BETA_TWO * second + (1.0 - BETA_TWO) * gradient * gradient
    first_hat = first_new / (1.0 - BETA_ONE ** STEP)
    second_hat = second_new / (1.0 - BETA_TWO ** STEP)
    weight_new = weight - rate * (first_hat / (jnp.sqrt(second_hat) + ADAM_EPS) + decay * weight)
    return (weight_new, first_new, second_new)

def reference(tokens, cotangent, w_query, query_first, query_second, w_key, key_first, key_second, w_value, value_first, value_second, w_out, out_first, out_second, w_gate, gate_first, gate_second, w_up, up_first, up_second, w_down, down_first, down_second, norm_gains, gains_first, gains_second):
    result, pullback = jax.vjp(forward, tokens.astype(jnp.float32), w_query, w_key, w_value, w_out, w_gate, w_up, w_down, norm_gains)
    gradients = pullback(cotangent.astype(jnp.float32))
    wide_rate = 2.0 * D ** (-0.5)
    out_rate = 2.0 * max(1, 16 * D // SEQ_LEN) ** (-0.5)
    down_rate = 2.0 * FF ** (-0.5)
    query_new, query_first_new, query_second_new = adamw_step(w_query, query_first, query_second, gradients[1], wide_rate, DECAY)
    key_new, key_first_new, key_second_new = adamw_step(w_key, key_first, key_second, gradients[2], wide_rate, DECAY)
    value_new, value_first_new, value_second_new = adamw_step(w_value, value_first, value_second, gradients[3], wide_rate, DECAY)
    out_new, out_first_new, out_second_new = adamw_step(w_out, out_first, out_second, gradients[4], out_rate, DECAY)
    gate_new, gate_first_new, gate_second_new = adamw_step(w_gate, gate_first, gate_second, gradients[5], wide_rate, DECAY)
    up_new, up_first_new, up_second_new = adamw_step(w_up, up_first, up_second, gradients[6], wide_rate, DECAY)
    down_new, down_first_new, down_second_new = adamw_step(w_down, down_first, down_second, gradients[7], down_rate, DECAY)
    gains_new, gains_first_new, gains_second_new = adamw_step(norm_gains, gains_first, gains_second, gradients[8], 0.3, 0.0)
    return (result.astype(jnp.bfloat16), gradients[0].astype(jnp.bfloat16), query_new, query_first_new, query_second_new, key_new, key_first_new, key_second_new, value_new, value_first_new, value_second_new, out_new, out_first_new, out_second_new, gate_new, gate_first_new, gate_second_new, up_new, up_first_new, up_second_new, down_new, down_first_new, down_second_new, gains_new, gains_first_new, gains_second_new)
```

```python
import functools

import jax
import jax.numpy as jnp
from jax import lax
from jax.experimental import pallas as pl
from jax.experimental.pallas import tpu as pltpu
from jax.sharding import Mesh
from jax.sharding import PartitionSpec as P

D = 2048
HEADS = 32
KV_HEADS = 4
HD = 64
FF = 5632
SEQ_LEN = 1024
STEP = 10

EPS = 1e-05
BETA_ONE = 0.9
BETA_TWO = 0.95
ADAM_EPS = 1e-08
DECAY = 0.1

ROWS = 128
HID = FF // 8
TILES = 6
PAD = TILES * 128
QW = 256
AW = 384
BF = jnp.bfloat16
F32 = jnp.float32
MIB = 2**20


def params(limit=56, **more):
    return pltpu.CompilerParams(vmem_limit_bytes=limit * MIB, **more)


def cost(flops, nbytes, trans=0):
    return pl.CostEstimate(flops=int(flops), bytes_accessed=int(nbytes), transcendentals=int(trans))


def dot(left, right):
    return jnp.dot(left, right, preferred_element_type=F32)


def dot_cols(left, right):
    return lax.dot_general(left, right, (((1,), (1,)), ((), ())), preferred_element_type=F32)


def dot_rows(left, right):
    return lax.dot_general(left, right, (((0,), (0,)), ((), ())), preferred_element_type=F32)


def swap_halves(v):
    width = v.shape[-1]
    lane = lax.broadcasted_iota(jnp.int32, v.shape, v.ndim - 1)
    return jnp.where(
        lane % HD < HD // 2,
        pltpu.roll(v, width - HD // 2, v.ndim - 1),
        pltpu.roll(v, HD // 2, v.ndim - 1),
    )


def ring(axis, k):
    return functools.partial(
        lax.ppermute, axis_name=axis, perm=[(i, (i + k) % 4) for i in range(4)]
    )


def other_core(v):
    return lax.ppermute(v, "core", [(0, 1), (1, 0)])


def spread(v):
    own = [v, ring("z", 1)(v), ring("z", 2)(v), ring("z", 3)(v)]
    return own + [other_core(t) for t in own]


def gather_axis(v, axis):
    me = lax.axis_index(axis)
    out = lax.dynamic_update_index_in_dim(jnp.zeros((4,) + v.shape, v.dtype), v, me, 0)
    for k in (1, 3, 2):
        out = lax.dynamic_update_index_in_dim(out, ring(axis, k)(v), (me - k) % 4, 0)
    return out


def scatter_axis(v, axis):
    me = lax.axis_index(axis)
    part = lambda k: lax.dynamic_index_in_dim(v, (me + k) % 4, 0, False)
    total = part(0).astype(F32)
    for k in (1, 3, 2):
        total = total + ring(axis, k)(part(k)).astype(F32)
    return total


def natural(parts, axis):
    me = lax.axis_index(axis)
    turned = jnp.stack([parts[3], parts[2], parts[1], parts[0]])
    return lax.dynamic_slice_in_dim(jnp.concatenate([turned, turned]), 3 - me, 4, 0)


def load_blocks(where, blocks, held, sems):
    step = pl.program_id(0)

    def copy(i, k, half, source):
        return pltpu.make_async_copy(
            source, held.at[k, pl.ds(pl.multiple_of(half * ROWS, ROWS), ROWS)], sems.at[i]
        )

    @pl.when(step == 0)
    def _():
        for k in range(4):
            copy(k, k, where[4], blocks[k]).start()
            copy(4 + k, k, 1 - where[4], blocks[4 + k]).start()

    copy(step, step, where[4], blocks[0]).wait()
    copy(4 + step, step, 1 - where[4], blocks[4]).wait()
    return held[step]


HELD = [pltpu.VMEM((4, 2 * ROWS, D), BF), pltpu.SemaphoreType.DMA((8,))]
ANY8 = [pl.BlockSpec(memory_space=pl.ANY)] * 8


def by_block(width):
    return pl.BlockSpec((2 * ROWS, width), lambda i, where: (where[i], 0))


def whole(*shape):
    return pl.BlockSpec(shape, lambda i, *_: (0,) * len(shape))


def blocks_call(kernel, where, blocks, operands, in_specs, out_widths, flops):
    outs = [jax.ShapeDtypeStruct((SEQ_LEN, w), t) for w, t in out_widths]
    nbytes = 4 * 2**20 + sum(o.size * o.dtype.itemsize for o in outs)
    nbytes += sum(o.size * o.dtype.itemsize for o in operands)
    return pl.pallas_call(
        kernel,
        grid_spec=pltpu.PrefetchScalarGridSpec(
            num_scalar_prefetch=1,
            grid=(4,),
            in_specs=ANY8 + in_specs,
            out_specs=[by_block(w) for w, _ in out_widths],
            scratch_shapes=HELD,
        ),
        out_shape=outs,
        compiler_params=params(),
        cost_estimate=cost(flops, nbytes),
    )(where, *blocks, *operands)


def first_kernel(where, *refs):
    blocks, (w, tcos, tsin, unit_out, q_out, kv_out, held, sems) = refs[:8], refs[8:]
    x = load_blocks(where, blocks, held, sems).astype(F32)
    inv = lax.rsqrt(jnp.mean(x * x, axis=-1, keepdims=True) + EPS)
    unit = (x * inv).astype(BF)
    unit_out[...] = unit
    y = dot(unit, w[...])
    cos, sin = tcos[...], tsin[...]
    for j in range(2):
        part = y[:, j * 128 : (j + 1) * 128]
        q_out[:, j * 128 : (j + 1) * 128] = (part * cos + swap_halves(part) * sin).astype(BF)
    part = y[:, 256:384]
    is_key = lax.broadcasted_iota(jnp.int32, part.shape, 1) < HD
    kv_out[...] = jnp.where(is_key, part * cos + swap_halves(part) * sin, part).astype(BF)


def first_call(where, blocks, w, tcos, tsin):
    return blocks_call(
        first_kernel,
        where,
        blocks,
        (w, tcos, tsin),
        [whole(D, AW), by_block(128), by_block(128)],
        [(D, BF), (QW, BF), (128, BF)],
        2 * SEQ_LEN * D * AW,
    )


def hidden_grad_kernel(where, *refs):
    blocks, (w, all_out, grad_out, held, sems) = refs[:8], refs[8:]
    x = load_blocks(where, blocks, held, sems)
    all_out[...] = x
    grad_out[...] = dot(x, w[...])


def hidden_grad_call(where, blocks, w):
    return blocks_call(
        hidden_grad_kernel,
        where,
        blocks,
        (w,),
        [pl.BlockSpec((D, PAD), lambda i, *_: (0, 2))],
        [(D, BF), (PAD, F32)],
        2 * SEQ_LEN * D * PAD,
    )


def middle_kernel(where, *refs):
    blocks, (w, hg, all_out, hidden_out, grads_out, held, sems) = refs[:8], refs[8:]
    x = load_blocks(where, blocks, held, sems)
    all_out[...] = x
    for j in range(TILES):
        y = dot(x, w[:, 256 * j : 256 * (j + 1)])
        gate, up = y[:, :128], y[:, 128:]
        sigma = jax.nn.sigmoid(gate)
        swish = gate * sigma
        back = hg[:, 128 * j : 128 * (j + 1)]
        hidden_out[:, 128 * j : 128 * (j + 1)] = (swish * up).astype(BF)
        grads_out[:, 256 * j : 256 * j + 128] = (
            back * up * (sigma * (1.0 + gate * (1.0 - sigma)))
        ).astype(BF)
        grads_out[:, 256 * j + 128 : 256 * (j + 1)] = (back * swish).astype(BF)


def middle_call(where, blocks, w, hg):
    return blocks_call(
        middle_kernel,
        where,
        blocks,
        (w, hg),
        [whole(D, 2 * PAD), by_block(PAD)],
        [(D, BF), (PAD, BF), (2 * PAD, BF)],
        2 * SEQ_LEN * D * 2 * PAD,
    )


def mixed_grad_kernel(where, *refs):
    blocks, (w, all_out, grad_out, held, sems) = refs[:8], refs[8:]
    x = load_blocks(where, blocks, held, sems)
    all_out[...] = x
    grad_out[...] = dot(x, w[...]).astype(BF)


def mixed_grad_call(where, blocks, w):
    return blocks_call(
        mixed_grad_kernel,
        where,
        blocks,
        (w,),
        [whole(D, QW)],
        [(D, BF), (QW, BF)],
        2 * SEQ_LEN * D * QW,
    )


def partial_kernel(has_addend, has_unit, n_out, order, a, w, *refs):
    refs = list(refs)
    addend = refs.pop(0) if has_addend else None
    unit = refs.pop(0) if has_unit else None
    outs = [refs.pop(0) for _ in range(n_out)]
    gain_out = refs.pop(0) if has_unit else None
    picked = refs.pop(0)

    def block(k):
        return pl.ds(pl.multiple_of(order[k] * ROWS, ROWS), ROWS)

    @pl.when(pl.program_id(0) == 0)
    def _():
        for k in range(4):
            picked[k * ROWS : (k + 1) * ROWS] = a[block(k)]

    y = dot_cols(picked[...], w[...])
    if has_unit:
        total = jnp.zeros((1, y.shape[1]), F32)
        for k in range(4):
            total += jnp.sum(
                y[k * ROWS : (k + 1) * ROWS] * unit[block(k)].astype(F32), axis=0, keepdims=True
            )
        gain_out[...] = total
    if has_addend:
        y = y + addend[...].astype(F32)
    y = y.astype(BF)
    if n_out == 1:
        outs[0][...] = y
    else:
        for k in range(4):
            outs[k][...] = y[k * ROWS : (k + 1) * ROWS]


def partial_call(order, a, w, col, addend=None, unit=None):
    depth, tile = a.shape[1], 256
    in_specs = [
        whole(SEQ_LEN, depth),
        pl.BlockSpec((tile, depth), lambda i, *_: (i, col)),
    ]
    operands = [a, w]
    n_out, rows = 1, 4 * ROWS
    if addend is not None:
        n_out, rows = 4, ROWS
        in_specs.append(pl.BlockSpec((4 * ROWS, tile), lambda i, *_: (0, i)))
        operands.append(addend)
    out_specs = [pl.BlockSpec((rows, tile), lambda i, *_: (0, i))] * n_out
    out_shape = [jax.ShapeDtypeStruct((rows, D), BF)] * n_out
    if unit is not None:
        in_specs.append(pl.BlockSpec((SEQ_LEN, tile), lambda i, *_: (0, i)))
        operands.append(unit)
        out_specs = out_specs + [pl.BlockSpec((1, tile), lambda i, *_: (0, i))]
        out_shape = out_shape + [jax.ShapeDtypeStruct((1, D), F32)]
    return pl.pallas_call(
        functools.partial(partial_kernel, addend is not None, unit is not None, n_out),
        grid_spec=pltpu.PrefetchScalarGridSpec(
            num_scalar_prefetch=1,
            grid=(D // tile,),
            in_specs=in_specs,
            out_specs=out_specs,
            scratch_shapes=[pltpu.VMEM((4 * ROWS, depth), BF)],
        ),
        out_shape=out_shape,
        compiler_params=params(),
        cost_estimate=cost(
            2 * 4 * ROWS * D * depth, 2 * depth * (D + 512) + (2 + 2 * (n_out == 4)) * MIB
        ),
    )(order, *operands)


def scores_of(q, k, diagonal):
    s = dot_cols(q, k)
    if diagonal:
        row = lax.broadcasted_iota(jnp.int32, s.shape, 0) % ROWS
        s = jnp.where(row >= lax.broadcasted_iota(jnp.int32, s.shape, 1), s, -1e30)
    return s


def stack_heads(v):
    return jnp.concatenate([v[:, HD * h : HD * (h + 1)] for h in range(4)], axis=0)


def lay_heads(v):
    return jnp.concatenate([v[ROWS * h : ROWS * (h + 1)] for h in range(4)], axis=1)


def attend_kernel(q, kv, out, lse):
    key, value = kv[:, :HD], kv[:, HD:]
    lane = lax.broadcasted_iota(jnp.int32, (ROWS, 128), 1)
    for b in range(8):
        rows = slice(b * ROWS, (b + 1) * ROWS)
        mine = stack_heads(q[rows] * HD**-0.5)
        pieces = [(scores_of(mine, key[rows], True), value[rows])]
        if b:
            pieces.append((scores_of(mine, key[: b * ROWS], False), value[: b * ROWS]))
        top = functools.reduce(
            jnp.maximum, [jnp.max(s, axis=-1, keepdims=True) for s, _ in pieces]
        )
        total, mixed = 0.0, 0.0
        for s, v in pieces:
            p = jnp.exp(s - top)
            total = total + jnp.sum(p, axis=-1, keepdims=True)
            mixed = mixed + dot(p.astype(BF), v)
        out[rows] = lay_heads(mixed / total).astype(BF)
        log_total = top + jnp.log(total)
        spread_out = jnp.zeros((ROWS, 128), F32)
        for h in range(4):
            spread_out = jnp.where(lane == h, log_total[ROWS * h : ROWS * (h + 1)], spread_out)
        lse[rows] = spread_out


def attend_call(q, kv):
    return pl.pallas_call(
        attend_kernel,
        out_shape=[
            jax.ShapeDtypeStruct((SEQ_LEN, QW), BF),
            jax.ShapeDtypeStruct((SEQ_LEN, 128), F32),
        ],
        compiler_params=params(),
        cost_estimate=cost(4e9, 2 * MIB, 2 * MIB),
    )(q, kv)


def attend_back_kernel(q, kv, lse, mixed_grad, tcos, tsin, q_grad, kv_grad, held):
    key, value = kv[:, :HD], kv[:, HD:]
    held[...] = jnp.zeros_like(held)
    for b in range(8):
        rows = slice(b * ROWS, (b + 1) * ROWS)
        mine = stack_heads(q[rows] * HD**-0.5)
        grad = stack_heads(mixed_grad[rows])
        log_total = jnp.concatenate([lse[rows, h : h + 1] for h in range(4)], axis=0)
        pieces = [(rows, True)] + ([(slice(0, b * ROWS), False)] if b else [])
        probs, back = [], []
        inner = 0.0
        for cols, diagonal in pieces:
            p = jnp.exp(scores_of(mine, key[cols], diagonal) - log_total)
            g = dot_cols(grad, value[cols])
            inner = inner + jnp.sum(p * g, axis=-1, keepdims=True)
            probs.append(p)
            back.append(g)
        total = 0.0
        for (cols, _), p, g in zip(pieces, probs, back):
            s_grad = (p * (g - inner)).astype(BF)
            total = total + dot(s_grad, key[cols])
            held[:HD, cols] += dot_rows(mine, s_grad)
            held[HD:, cols] += dot_rows(grad, p.astype(BF))
        wide = lay_heads(total * HD**-0.5)
        cos, sin = tcos[rows], tsin[rows]
        for j in range(2):
            part = wide[:, 128 * j : 128 * (j + 1)]
            q_grad[rows, 128 * j : 128 * (j + 1)] = (part * cos - swap_halves(part) * sin).astype(
                BF
            )
    kv_grad[...] = held[...].T


def attend_back_call(q, kv, lse, mixed_grad, tcos, tsin):
    return pl.pallas_call(
        attend_back_kernel,
        out_shape=[
            jax.ShapeDtypeStruct((SEQ_LEN, QW), BF),
            jax.ShapeDtypeStruct((SEQ_LEN, 128), F32),
        ],
        scratch_shapes=[pltpu.VMEM((128, SEQ_LEN), F32)],
        compiler_params=params(),
        cost_estimate=cost(8e9, 4 * MIB, 2 * MIB),
    )(q, kv, lse, mixed_grad, tcos, tsin)


def wgrad_kernel(n, *refs):
    out = refs[-1]
    at = 0
    for j in range(n):
        x, g = refs[2 * j], refs[2 * j + 1]
        width = g.shape[1]
        out[:, at : at + width] = dot_rows(x[...], g[...]).astype(BF)
        at += width


def wgrad_call(*pairs):
    tile = 256
    in_specs, operands, width = [], [], 0
    for x, g in pairs:
        in_specs += [
            pl.BlockSpec((SEQ_LEN, tile), lambda i: (0, i)),
            pl.BlockSpec(g.shape, lambda i: (0, 0)),
        ]
        operands += [x, g]
        width += g.shape[1]
    return pl.pallas_call(
        functools.partial(wgrad_kernel, len(pairs)),
        grid=(D // tile,),
        in_specs=in_specs,
        out_specs=pl.BlockSpec((tile, width), lambda i: (i, 0)),
        out_shape=jax.ShapeDtypeStruct((D, width), BF),
        compiler_params=params(),
        cost_estimate=cost(
            2 * SEQ_LEN * D * width, 4 * MIB * len(pairs) + 2 * width * (SEQ_LEN + D)
        ),
    )(*operands)


def adamw_step(weight, first, second, gradient, rate, decay):
    first_new = BETA_ONE * first + (1.0 - BETA_ONE) * gradient
    second_new = BETA_TWO * second + (1.0 - BETA_TWO) * gradient * gradient
    first_hat = first_new / (1.0 - BETA_ONE**STEP)
    second_hat = second_new / (1.0 - BETA_TWO**STEP)
    weight_new = weight - rate * (first_hat / (jnp.sqrt(second_hat) + ADAM_EPS) + decay * weight)
    return (weight_new, first_new, second_new)


def rotary():
    positions = jnp.arange(SEQ_LEN).astype(F32)
    frequency = 10000.0 ** (-2.0 * jnp.arange(HD // 2).astype(F32) / HD)
    angles = positions[:, None] * frequency[None, :]
    cos, sin = jnp.cos(angles), jnp.sin(angles)
    return (
        jnp.concatenate([cos] * 4, axis=1),
        jnp.concatenate([-sin, sin, -sin, sin], axis=1),
    )


def pad_hidden(v):
    return jnp.pad(v, ((0, 0), (0, PAD - HID)))


def shards(
    tokens,
    cotangent,
    w_query,
    query_first,
    query_second,
    w_key,
    key_first,
    key_second,
    w_value,
    value_first,
    value_second,
    w_out,
    out_first,
    out_second,
    w_gate,
    gate_first,
    gate_second,
    w_up,
    up_first,
    up_second,
    w_down,
    down_first,
    down_second,
    norm_gains,
    gains_first,
    gains_second,
):
    z, core = lax.axis_index("z"), lax.axis_index("core")
    away = jnp.arange(4)
    where = jnp.concatenate([(z - away) % 4, core[None]]).astype(jnp.int32)
    mine_order = (2 * ((z + away) % 4) + core).astype(jnp.int32)
    other_order = (2 * ((z + away) % 4) + 1 - core).astype(jnp.int32)
    is_zero = core == 0

    small = jnp.concatenate(
        [
            w_key.astype(BF).reshape(16, 4, HD),
            w_value.astype(BF).reshape(16, 4, HD),
            jnp.broadcast_to(
                jnp.pad(norm_gains.astype(BF).T, ((0, 0), (0, 126)))[:, None, :], (16, 4, 128)
            ),
        ],
        axis=2,
    ).transpose(1, 0, 2)
    got = []
    for k in range(4):
        piece = lax.dynamic_index_in_dim(small, (z + k) % 4, 0, False)
        got.append(ring("z", k)(piece) if k else piece)
    got = natural(got, "z")
    across = other_core(got)
    kv_rows = jnp.stack(
        [jnp.where(is_zero, got, across), jnp.where(is_zero, across, got)], axis=1
    ).reshape(128, 256)
    gain_one = kv_rows[:, 128:129].astype(F32)
    gain_two = kv_rows[:, 129:130].astype(F32)

    w_attend = jnp.concatenate([w_query.astype(BF), kv_rows[:, :128]], axis=1)
    w_attend = (w_attend.astype(F32) * gain_one).astype(BF)
    w_mixed = w_out.astype(BF).T
    gate_tiles = pad_hidden(w_gate.astype(BF)).reshape(128, TILES, 1, 128)
    up_tiles = pad_hidden(w_up.astype(BF)).reshape(128, TILES, 1, 128)
    w_wide = jnp.concatenate([gate_tiles, up_tiles], axis=2).reshape(128, 2 * PAD)
    w_wide = (w_wide.astype(F32) * gain_two).astype(BF)
    w_ffn = jnp.concatenate([w_wide, pad_hidden(w_down.astype(BF).T)], axis=1)

    all_ffn = lax.all_gather(w_ffn, ("y", "x"), axis=0, tiled=True)
    all_attend = gather_axis(gather_axis(w_attend, "x"), "y").reshape(D, AW)
    all_mixed = (
        gather_axis(gather_axis(w_mixed, "y"), "x").transpose(1, 0, 2, 3).reshape(D, QW)
    )

    tcos, tsin = rotary()
    blocks = spread(tokens[0])
    unit_all, query, key_value = first_call(where, blocks, all_attend, tcos, tsin)
    attended, lse = attend_call(query, key_value)

    def reduce_rows(a, w, col, unit=None):
        other = partial_call(other_order, a, w, col, unit=unit)
        mine = partial_call(mine_order, a, w, col, addend=other_core(other[0]), unit=unit)
        total = mine[0].astype(F32)
        for k in (2, 1, 3):
            total = total + ring("z", k)(mine[k]).astype(F32)
        return total, (other[1] + mine[4] if unit is not None else None)

    x = tokens[0].astype(F32)
    inv_first = lax.rsqrt(jnp.mean(x * x, axis=-1, keepdims=True) + EPS)
    unit_first = x * inv_first

    mixed, _ = reduce_rows(attended, all_mixed, 0)
    middle = x + mixed
    inv_second = lax.rsqrt(jnp.mean(middle * middle, axis=-1, keepdims=True) + EPS)
    unit_second = middle * inv_second

    hidden_grad_blocks = spread(cotangent[0])
    grad_all, hidden_grad = hidden_grad_call(where, hidden_grad_blocks, all_ffn)

    mid_all, hidden, wide_grad = middle_call(
        where, spread(unit_second.astype(BF)), all_ffn, hidden_grad
    )
    mid_back, _ = reduce_rows(wide_grad, all_ffn, 0)
    ffn_wgrad = wgrad_call((mid_all, wide_grad), (grad_all, hidden))
    ffn_sum = lax.psum_scatter(ffn_wgrad, ("y", "x"), scatter_dimension=0, tiled=True)
    down_rows, _ = reduce_rows(hidden, all_ffn, 2)
    output = middle + down_rows

    slope = mid_back * unit_second
    gain_two_row = jnp.sum(slope, axis=0)
    middle_grad = cotangent[0].astype(F32) + inv_second * (
        mid_back - unit_second * jnp.mean(slope, axis=-1, keepdims=True)
    )
    mid_grad_all, mixed_grad = mixed_grad_call(where, spread(middle_grad.astype(BF)), all_mixed)
    out_wgrad = wgrad_call((mid_grad_all, attended)).reshape(4, 4, 128, QW)
    out_sum = scatter_axis(scatter_axis(out_wgrad, "y").astype(BF), "x")

    query_grad, kv_grad = attend_back_call(query, key_value, lse, mixed_grad, tcos, tsin)
    key_part, value_part = kv_grad[:, :HD], kv_grad[:, HD:]
    kept = jnp.where(is_zero, key_part, value_part)
    sent = jnp.where(is_zero, value_part, key_part).astype(BF)
    kept = kept + other_core(sent).astype(F32)
    half = HD // 2
    turned = jnp.concatenate([kept[:, half:], kept[:, :half]], axis=1)
    kept = jnp.where(is_zero, kept * tcos[:, :HD] - turned * tsin[:, :HD], kept).astype(BF)
    none = jnp.zeros_like(kept)
    attend_grad = jnp.concatenate(
        [query_grad, jnp.where(is_zero, kept, none), jnp.where(is_zero, none, kept)], axis=1
    )
    in_back, gain_one_row = reduce_rows(attend_grad, all_attend, 0, unit=unit_all)
    slope = in_back * unit_first
    input_grad = middle_grad + inv_first * (
        in_back - unit_first * jnp.mean(slope, axis=-1, keepdims=True)
    )

    attend_wgrad = wgrad_call((unit_all, attend_grad))
    gain_rows = jnp.stack([gain_one_row[0], gain_two_row])
    gain_high = gain_rows.astype(BF)
    gain_low = (gain_rows - gain_high.astype(F32)).astype(BF)
    gain_cols = jnp.pad(jnp.concatenate([gain_high, gain_low]).T, ((0, 0), (0, HD - 4)))
    tail = attend_wgrad[:, QW:]
    tail = jnp.where(
        is_zero,
        jnp.concatenate([tail[:, :HD], gain_cols], axis=1),
        jnp.concatenate([gain_cols, tail[:, HD:]], axis=1),
    )
    attend_wgrad = jnp.concatenate([attend_wgrad[:, :QW], tail], axis=1).reshape(4, 4, 128, AW)
    attend_sum = scatter_axis(
        scatter_axis(attend_wgrad.transpose(1, 0, 2, 3), "x").astype(BF), "y"
    )

    tail = attend_sum[:, QW:]
    tail_kv = jnp.where(is_zero, tail[:, :HD], tail[:, HD:]) * gain_one
    tail_gain = jnp.where(is_zero, tail[:, HD:], tail[:, :HD])
    tail = jnp.concatenate([tail_kv, tail_gain], axis=1).reshape(4, 32, 128)
    got = []
    for k in range(4):
        piece = lax.dynamic_index_in_dim(tail, (z + k) % 4, 0, False)
        got.append(ring("z", k)(piece) if k else piece)
    got = natural(got, "z")
    kv_mine = got[:, :, :HD].transpose(1, 0, 2).reshape(2, 16, 4 * HD)
    gain_mine = jnp.sum(got[:, :, HD:], axis=0).reshape(2, 16, HD)
    tail = jnp.concatenate([kv_mine, gain_mine], axis=2)
    own = lax.dynamic_index_in_dim(tail, core, 0, False)
    across = other_core(lax.dynamic_index_in_dim(tail, 1 - core, 0, False))
    key_sum = jnp.where(is_zero, own[:, : 4 * HD], across[:, : 4 * HD])
    value_sum = jnp.where(is_zero, across[:, : 4 * HD], own[:, : 4 * HD])
    gain_sum = own[:, 4 * HD : 4 * HD + 4] + across[:, 4 * HD : 4 * HD + 4]
    gains_sum = (gain_sum[:, :2] + gain_sum[:, 2:4]).T / norm_gains.astype(BF).astype(F32)

    query_sum = attend_sum[:, :QW] * gain_one
    wide_sum = ffn_sum[:, : 2 * PAD].astype(F32) * gain_two
    wide_sum = wide_sum.reshape(128, TILES, 2, 128)
    gate_sum = wide_sum[:, :, 0].reshape(128, PAD)[:, :HID]
    up_sum = wide_sum[:, :, 1].reshape(128, PAD)[:, :HID]
    down_sum = ffn_sum[:, 2 * PAD : 2 * PAD + HID].astype(F32).T

    wide_rate = 2.0 * D ** (-0.5)
    out_rate = 2.0 * max(1, 16 * D // SEQ_LEN) ** (-0.5)
    down_rate = 2.0 * FF ** (-0.5)
    return (
        output.astype(BF)[None],
        input_grad.astype(BF)[None],
        *adamw_step(w_query, query_first, query_second, query_sum, wide_rate, DECAY),
        *adamw_step(w_key, key_first, key_second, key_sum, wide_rate, DECAY),
        *adamw_step(w_value, value_first, value_second, value_sum, wide_rate, DECAY),
        *adamw_step(w_out, out_first, out_second, out_sum.T, out_rate, DECAY),
        *adamw_step(w_gate, gate_first, gate_second, gate_sum, wide_rate, DECAY),
        *adamw_step(w_up, up_first, up_second, up_sum, wide_rate, DECAY),
        *adamw_step(w_down, down_first, down_second, down_sum, down_rate, DECAY),
        *adamw_step(norm_gains, gains_first, gains_second, gains_sum, 0.3, 0.0),
    )


def solution(mesh):
    dp, ctx = ("y", "x"), ("z", "core")
    fine = Mesh(mesh.devices.reshape(4, 4, 4, 2), dp + ctx)
    act, col, row = P(dp, ctx, None), P(dp, ctx), P(ctx, dp)
    flat, gains = P(dp + ctx, None), P(None, dp + ctx)
    weights = (col,) * 3 + (flat,) * 6 + (row,) * 3 + (col,) * 6 + (row,) * 3 + (gains,) * 3
    return jax.shard_map(
        shards,
        mesh=fine,
        in_specs=(act, act) + weights,
        out_specs=(act, act) + weights,
        check_vma=False,
    )
```

```python
import functools

import jax
import jax.numpy as jnp
from jax import lax
from jax.experimental import pallas as pl
from jax.experimental.pallas import tpu as pltpu
from jax.sharding import Mesh
from jax.sharding import PartitionSpec as P

D = 2048
HEADS = 32
KV_HEADS = 4
HD = 64
FF = 5632
SEQ_LEN = 1024
STEP = 10

EPS = 1e-05
BETA_ONE = 0.9
BETA_TWO = 0.95
ADAM_EPS = 1e-08
DECAY = 0.1

ROWS = 128
HID = FF // 8
TILES = 6
PAD = TILES * 128
QW = 256
AW = 384
BF = jnp.bfloat16
F32 = jnp.float32
MIB = 2**20


def params(limit=56, **more):
    return pltpu.CompilerParams(vmem_limit_bytes=limit * MIB, **more)


def cost(flops, nbytes, trans=0):
    return pl.CostEstimate(flops=int(flops), bytes_accessed=int(nbytes), transcendentals=int(trans))


def dot(left, right):
    return jnp.dot(left, right, preferred_element_type=F32)


def dot_cols(left, right):
    return lax.dot_general(left, right, (((1,), (1,)), ((), ())), preferred_element_type=F32)


def dot_rows(left, right):
    return lax.dot_general(left, right, (((0,), (0,)), ((), ())), preferred_element_type=F32)


def swap_halves(v):
    width = v.shape[-1]
    lane = lax.broadcasted_iota(jnp.int32, v.shape, v.ndim - 1)
    return jnp.where(
        lane % HD < HD // 2,
        pltpu.roll(v, width - HD // 2, v.ndim - 1),
        pltpu.roll(v, HD // 2, v.ndim - 1),
    )


def ring(axis, k):
    return functools.partial(
        lax.ppermute, axis_name=axis, perm=[(i, (i + k) % 4) for i in range(4)]
    )


def other_core(v):
    return lax.ppermute(v, "core", [(0, 1), (1, 0)])


def spread_z(v):
    return [v, ring("z", 1)(v), ring("z", 2)(v), ring("z", 3)(v)]


def spread(v):
    own = spread_z(v)
    return own + [other_core(t) for t in own]


def came(v, axis):
    return [v] + [ring(axis, k)(v) for k in (1, 2, 3)]


def swap_blocks(v, axes):
    return lax.all_to_all(v, axes, split_axis=0, concat_axis=0, tiled=True)


ANY = pl.BlockSpec(memory_space=pl.ANY)
HELD = [pltpu.VMEM((4, 2 * ROWS, D), BF), pltpu.SemaphoreType.DMA((8,))]


def load_blocks(halves, blocks, held, sems):
    step = pl.program_id(0)

    def copy(i, k, half, source):
        return pltpu.make_async_copy(
            source, held.at[k, pl.ds(pl.multiple_of(half * ROWS, ROWS), ROWS)], sems.at[i]
        )

    @pl.when(step == 0)
    def _():
        for k in range(4):
            copy(k, k, halves[0], blocks[k]).start()
            copy(4 + k, k, halves[1], blocks[4 + k]).start()

    copy(step, step, halves[0], blocks[0]).wait()
    copy(4 + step, step, halves[1], blocks[4]).wait()
    return held.at[step]


def by_block(width):
    return pl.BlockSpec((2 * ROWS, width), lambda i, where: (where[i], 0))


def by_step(width):
    return pl.BlockSpec((ROWS, width), lambda i, *_: (i, 0))


def whole(*shape):
    return pl.BlockSpec(shape, lambda i, *_: (0,) * len(shape))


def shape_of(shape, kind=BF):
    return jax.ShapeDtypeStruct(shape, kind)


def blocks_call(
    kernel, where, blocks, operands, in_specs, out_specs, outs, flops, behind=(), through=(), scratch=None
):
    n_in, n_out, n_more = 8 + len(operands), len(outs), len(behind) + len(through)

    def body(where, *refs):
        refs = list(refs)
        del refs[n_in + n_more + n_out : n_in + n_more + n_out + len(through)]
        del refs[n_in : n_in + n_more]
        kernel(where, *refs)

    nbytes = 4 * MIB + sum(o.size * o.dtype.itemsize for o in outs)
    nbytes += sum(o.size * o.dtype.itemsize for o in operands)
    first = 1 + n_in + len(behind)
    return pl.pallas_call(
        body,
        grid_spec=pltpu.PrefetchScalarGridSpec(
            num_scalar_prefetch=1,
            grid=(4,),
            in_specs=[ANY] * 8 + in_specs + [ANY] * n_more,
            out_specs=out_specs + [ANY] * len(through),
            scratch_shapes=scratch or HELD,
        ),
        out_shape=outs + [shape_of(v.shape, v.dtype) for v in through],
        input_output_aliases={first + i: n_out + i for i in range(len(through))},
        compiler_params=params(),
        cost_estimate=cost(flops, nbytes),
        name=kernel.__name__,
    )(where, *blocks, *operands, *behind, *through)


def assemble_call(axis, pieces, behind=()):
    order = ((lax.axis_index(axis) - jnp.arange(4)) % 4).astype(jnp.int32)

    def assemble_kernel(order, *refs):
        for k in range(4):
            refs[-1][order[k]] = refs[k][...]

    shape = pieces[0].shape
    return pl.pallas_call(
        assemble_kernel,
        grid_spec=pltpu.PrefetchScalarGridSpec(
            num_scalar_prefetch=1,
            grid=(1,),
            in_specs=[whole(*shape)] * 4 + [ANY] * len(behind),
            out_specs=whole(4, *shape),
        ),
        out_shape=shape_of((4,) + shape, pieces[0].dtype),
        compiler_params=params(),
        cost_estimate=cost(0, 16 * pieces[0].size),
        name="assemble_kernel",
    )(order, *pieces, *behind)


def weights_kernel(order, *refs):
    for k in range(4):
        rows = pl.ds(pl.multiple_of(order[k] * 512, 512), 512)
        piece = refs[k][...].reshape(512, AW + QW)
        refs[4][rows] = piece[:, :AW]
        refs[5][rows] = piece[:, AW:]


def weights_call(pieces):
    order = ((lax.axis_index("y") - jnp.arange(4)) % 4).astype(jnp.int32)
    return pl.pallas_call(
        weights_kernel,
        grid_spec=pltpu.PrefetchScalarGridSpec(
            num_scalar_prefetch=1,
            grid=(1,),
            in_specs=[whole(*pieces[0].shape)] * 4,
            out_specs=[whole(D, AW), whole(D, QW)],
        ),
        out_shape=[shape_of((D, AW)), shape_of((D, QW))],
        compiler_params=params(),
        cost_estimate=cost(0, 5 * MIB),
        name="weights_kernel",
    )(order, *pieces)


def attend_weights_kernel(kvg, query, mixed, out):
    gain = kvg[:, 128:129].astype(F32)
    out[:, :QW] = (query[...].astype(BF).astype(F32) * gain).astype(BF)
    out[:, QW:AW] = (kvg[:, :128].astype(F32) * gain).astype(BF)
    out[:, AW:] = mixed[...].T.astype(BF)


def attend_weights_call(kvg, query, mixed):
    return pl.pallas_call(
        attend_weights_kernel,
        out_shape=shape_of((ROWS, AW + QW)),
        compiler_params=params(),
        cost_estimate=cost(0, MIB),
        name="attend_weights_kernel",
    )(kvg, query, mixed)


def ffn_weights_kernel(kvg, gate, up, down, *refs):
    out = refs[-1]
    gain = kvg[:, 129:130].astype(F32)
    for j in range(TILES):
        n = min(128, HID - 128 * j)
        for s, ref in enumerate((gate, up, down)):
            part = ref[128 * j : 128 * j + n]
            if n < 128:
                part = jnp.concatenate([part, jnp.zeros((128 - n, 128), F32)], axis=0)
            part = part.T.astype(BF)
            if s < 2:
                part = (part.astype(F32) * gain).astype(BF)
            at = 2 * PAD + 128 * j if s == 2 else 256 * j + 128 * s
            out[:, at : at + 128] = part


def ffn_weights_call(kvg, gate, up, down, behind):
    vmem = pl.BlockSpec(memory_space=pltpu.VMEM)
    return pl.pallas_call(
        ffn_weights_kernel,
        in_specs=[vmem] * 4 + [ANY] * len(behind),
        out_specs=vmem,
        out_shape=shape_of((ROWS, 3 * PAD)),
        compiler_params=params(),
        cost_estimate=cost(0, 2 * MIB),
        name="ffn_weights_kernel",
    )(kvg, gate, up, down, *behind)


def norm_back_kernel(n_through, *refs):
    parts, (x, base), outs = refs[:4], refs[4:6], refs[6 + n_through : len(refs) - n_through]
    v = x[...].astype(F32)
    inv = lax.rsqrt(jnp.mean(v * v, axis=-1, keepdims=True) + EPS)
    unit = v * inv
    u = functools.reduce(jnp.add, [ref[...].astype(F32) for ref in parts])
    out = base[...].astype(F32) + inv * (u - unit * jnp.mean(u * unit, axis=-1, keepdims=True))
    for ref in outs:
        ref[...] = out.astype(ref.dtype)


def norm_back_call(parts, x, base, kinds, through=()):
    vmem = pl.BlockSpec(memory_space=pltpu.VMEM)
    return pl.pallas_call(
        functools.partial(norm_back_kernel, len(through)),
        in_specs=[vmem] * 6 + [ANY] * len(through),
        out_specs=[vmem] * len(kinds) + [ANY] * len(through),
        out_shape=[shape_of((ROWS, D), kind) for kind in kinds]
        + [shape_of(v.shape, v.dtype) for v in through],
        input_output_aliases={6 + i: len(kinds) + i for i in range(len(through))},
        compiler_params=params(),
        cost_estimate=cost(0, 5 * MIB),
        name="norm_back_kernel",
    )(*parts, x, base, *through)


def first_kernel(where, *refs):
    blocks, (w, tcos, tsin, all_out, q_out, kv_out, inv_out, held, sems) = refs[:8], refs[8:]
    x = load_blocks((where[4], 1 - where[4]), blocks, held, sems)[...]
    all_out[...] = x
    y = dot(x, w[...])
    x = x.astype(F32)
    inv = lax.rsqrt(jnp.mean(x * x, axis=-1, keepdims=True) + EPS)
    inv_out[...] = jnp.broadcast_to(inv, inv_out.shape)
    cos, sin = tcos[...] * inv, tsin[...] * inv
    for j in range(2):
        part = y[:, j * 128 : (j + 1) * 128]
        q_out[:, j * 128 : (j + 1) * 128] = (part * cos + swap_halves(part) * sin).astype(BF)
    part = y[:, 256:384]
    is_key = lax.broadcasted_iota(jnp.int32, part.shape, 1) < HD
    kv_out[...] = jnp.where(is_key, part * cos + swap_halves(part) * sin, part * inv).astype(BF)


def first_call(where, blocks, w, tcos, tsin, behind):
    return blocks_call(
        first_kernel,
        where,
        blocks,
        (w, tcos, tsin),
        [pl.BlockSpec((D, AW), lambda i, *_: (0, 0)), by_block(128), by_block(128)],
        [by_block(D), by_block(QW), by_block(128), by_block(128)],
        [
            shape_of((SEQ_LEN, D)),
            shape_of((SEQ_LEN, QW)),
            shape_of((SEQ_LEN, 128)),
            shape_of((SEQ_LEN, 128), F32),
        ],
        2 * SEQ_LEN * D * AW,
        behind,
    )


def put_halves(outs, value, cols=slice(None)):
    outs[0][:, cols] = value[:ROWS]
    outs[1][:, cols] = value[ROWS:]


def middle_kernel(where, *refs):
    blocks, grad_blocks, (w, *refs) = refs[:8], refs[8:16], refs[16:]
    hiddens, grads, (held, sems, grad_held, grad_sems) = refs[:2], refs[2:4], refs[4:]
    x = load_blocks((0, 1), blocks, held, sems)[...]
    c = load_blocks((0, 1), grad_blocks, grad_held, grad_sems)[...]
    for j in range(TILES // 2):
        backs = dot(c, w[:, 2 * PAD + 256 * j : 2 * PAD + 256 * (j + 1)])
        for i in range(2):
            t = 2 * j + i
            y = dot(x, w[:, 256 * t : 256 * (t + 1)])
            gate, up, back = y[:, :128], y[:, 128:], backs[:, 128 * i : 128 * (i + 1)]
            sigma = jax.nn.sigmoid(gate)
            swish = gate * sigma
            put_halves(hiddens, (swish * up).astype(BF), slice(128 * t, 128 * (t + 1)))
            g = (back * up * (sigma * (1.0 + gate * (1.0 - sigma)))).astype(BF)
            put_halves(grads, g, slice(256 * t, 256 * t + 128))
            put_halves(grads, (back * swish).astype(BF), slice(256 * t + 128, 256 * (t + 1)))


def middle_call(where, blocks, grad_blocks, w):
    return blocks_call(
        middle_kernel,
        where,
        blocks,
        (*grad_blocks, w),
        [ANY] * 8 + [whole(D, 3 * PAD)],
        [by_step(PAD)] * 2 + [by_step(2 * PAD)] * 2,
        [shape_of((4 * ROWS, PAD))] * 2 + [shape_of((4 * ROWS, 2 * PAD))] * 2,
        2 * SEQ_LEN * D * 3 * PAD,
        scratch=HELD * 2,
    )


def mixed_grad_kernel(where, *refs):
    blocks, (w, all_out, grad_out, held, sems) = refs[:8], refs[8:]
    x = load_blocks((where[4], 1 - where[4]), blocks, held, sems)[...]
    all_out[...] = x
    grad_out[...] = dot(x, w[...]).astype(BF)


def mixed_grad_call(where, blocks, w):
    return blocks_call(
        mixed_grad_kernel,
        where,
        blocks,
        (w,),
        [whole(D, QW)],
        [by_block(D), by_block(QW)],
        [shape_of((SEQ_LEN, D)), shape_of((SEQ_LEN, QW))],
        2 * SEQ_LEN * D * QW,
    )


def partial_kernel(n_in, n_behind, order, *refs):
    w, across, own = refs[n_in], refs[-2], refs[-1]
    if n_in == 1:
        a = refs[0]
        left = jnp.concatenate(
            [a[pl.ds(pl.multiple_of(order[k] * ROWS, ROWS), ROWS)] for k in range(8)], axis=0
        )
    else:
        left = jnp.concatenate([refs[0][...], refs[1][...]], axis=0)
    y = dot_cols(left, w[...]).astype(BF)
    across[...] = y[: 4 * ROWS]
    own[...] = y[4 * ROWS :]


def partial_call(order, a, w, col, tile, behind=()):
    depth = a[0].shape[1]
    return pl.pallas_call(
        functools.partial(partial_kernel, len(a), len(behind)),
        grid_spec=pltpu.PrefetchScalarGridSpec(
            num_scalar_prefetch=1,
            grid=(D // tile,),
            in_specs=[whole(*v.shape) for v in a]
            + [pl.BlockSpec((tile, depth), lambda i, *_: (i, col))]
            + [ANY] * len(behind),
            out_specs=[pl.BlockSpec((4 * ROWS, tile), lambda i, *_: (0, i))] * 2,
        ),
        out_shape=[shape_of((4 * ROWS, D))] * 2,
        compiler_params=params(),
        cost_estimate=cost(2 * 8 * ROWS * D * depth, 2 * depth * (D + 1024) + 4 * MIB),
        name="partial_kernel",
    )(order, *a, w, *behind)


def add_kernel(n_behind, across, own, *refs):
    for k, ref in enumerate(refs[n_behind:]):
        rows = slice(k * ROWS, (k + 1) * ROWS)
        ref[...] = (across[rows].astype(F32) + own[rows].astype(F32)).astype(BF)


def add_call(across, own, behind=()):
    vmem = pl.BlockSpec(memory_space=pltpu.VMEM)
    return pl.pallas_call(
        functools.partial(add_kernel, len(behind)),
        in_specs=[vmem] * 2 + [ANY] * len(behind),
        out_specs=[vmem] * 4,
        out_shape=[shape_of((ROWS, D))] * 4,
        compiler_params=params(),
        cost_estimate=cost(0, 6 * MIB),
        name="add_kernel",
    )(across, own, *behind)


def scores_of(q, k, diagonal):
    s = dot_cols(q, k)
    if diagonal:
        row = lax.broadcasted_iota(jnp.int32, s.shape, 0) % ROWS
        s = jnp.where(row >= lax.broadcasted_iota(jnp.int32, s.shape, 1), s, -1e30)
    return s


def stack_heads(v):
    return jnp.concatenate([v[:, HD * h : HD * (h + 1)] for h in range(4)], axis=0)


def lay_heads(v):
    return jnp.concatenate([v[ROWS * h : ROWS * (h + 1)] for h in range(4)], axis=1)


def attend_kernel(q, kv, out, lse):
    key, value = kv[:, :HD], kv[:, HD:]
    lane = lax.broadcasted_iota(jnp.int32, (ROWS, 128), 1)
    for b in range(8):
        rows = slice(b * ROWS, (b + 1) * ROWS)
        mine = stack_heads(q[rows] * HD**-0.5)
        pieces = [(scores_of(mine, key[rows], True), value[rows])]
        if b:
            pieces.append((scores_of(mine, key[: b * ROWS], False), value[: b * ROWS]))
        top = functools.reduce(
            jnp.maximum, [jnp.max(s, axis=-1, keepdims=True) for s, _ in pieces]
        )
        total, mixed = 0.0, 0.0
        for s, v in pieces:
            p = jnp.exp(s - top)
            total = total + jnp.sum(p, axis=-1, keepdims=True)
            mixed = mixed + dot(p.astype(BF), v)
        out[rows] = lay_heads(mixed / total).astype(BF)
        log_total = top + jnp.log(total)
        spread_out = jnp.zeros((ROWS, 128), F32)
        for h in range(4):
            spread_out = jnp.where(lane == h, log_total[ROWS * h : ROWS * (h + 1)], spread_out)
        lse[rows] = spread_out


def attend_call(q, kv):
    return pl.pallas_call(
        attend_kernel,
        out_shape=[shape_of((SEQ_LEN, QW)), shape_of((SEQ_LEN, 128), F32)],
        compiler_params=params(),
        cost_estimate=cost(4e9, 2 * MIB, 2 * MIB),
        name="attend_kernel",
    )(q, kv)


def attend_back_kernel(
    q, kv, lse, mixed_grad, tcos, tsin, inv, grad_out, scaled_out, held
):
    key, value = kv[:, :HD], kv[:, HD:]
    held[...] = jnp.zeros_like(held)

    def put(rows, cols, part, turn):
        part = jnp.where(turn, part * tcos[rows] - swap_halves(part) * tsin[rows], part)
        grad_out[rows, cols] = part.astype(BF)
        scaled_out[rows, cols] = (part * inv[rows]).astype(BF)

    for b in range(8):
        rows = slice(b * ROWS, (b + 1) * ROWS)
        mine = stack_heads(q[rows] * HD**-0.5)
        grad = stack_heads(mixed_grad[rows])
        log_total = jnp.concatenate([lse[rows, h : h + 1] for h in range(4)], axis=0)
        pieces = [(rows, True)] + ([(slice(0, b * ROWS), False)] if b else [])
        probs, back = [], []
        inner = 0.0
        for cols, diagonal in pieces:
            p = jnp.exp(scores_of(mine, key[cols], diagonal) - log_total)
            g = dot_cols(grad, value[cols])
            inner = inner + jnp.sum(p * g, axis=-1, keepdims=True)
            probs.append(p)
            back.append(g)
        total = 0.0
        for (cols, _), p, g in zip(pieces, probs, back):
            s_grad = (p * (g - inner)).astype(BF)
            total = total + dot(s_grad, key[cols])
            held[:HD, cols] += dot_rows(mine, s_grad)
            held[HD:, cols] += dot_rows(grad, p.astype(BF))
        wide = lay_heads(total * HD**-0.5)
        for j in range(2):
            put(rows, slice(128 * j, 128 * (j + 1)), wide[:, 128 * j : 128 * (j + 1)], True)
    is_key = lax.broadcasted_iota(jnp.int32, (ROWS, 128), 1) < HD
    for b in range(8):
        rows = slice(b * ROWS, (b + 1) * ROWS)
        put(rows, slice(QW, AW), held[:, rows].T, is_key)


def attend_back_call(q, kv, lse, mixed_grad, tcos, tsin, inv):
    return pl.pallas_call(
        attend_back_kernel,
        out_shape=[shape_of((SEQ_LEN, AW))] * 2,
        scratch_shapes=[pltpu.VMEM((128, SEQ_LEN), F32)],
        compiler_params=params(),
        cost_estimate=cost(8e9, 4 * MIB, 2 * MIB),
        name="attend_back_kernel",
    )(q, kv, lse, mixed_grad, tcos, tsin, inv)


def wgrad_kernel(counts, *refs):
    out = refs[-1]
    at, ref = 0, 0
    for group in counts:
        total = 0.0
        for n in group:
            x = refs[ref : ref + n]
            x = x[0][...] if n == 1 else jnp.concatenate([v[...] for v in x], axis=0)
            total = total + dot_rows(x, refs[ref + n][...])
            ref += n + 1
        out[:, at : at + total.shape[1]] = total.astype(BF)
        at += total.shape[1]


def wgrad_call(tile, *groups, behind=()):
    in_specs, operands, width = [], [], 0
    for group in groups:
        for x, g in group:
            in_specs += [pl.BlockSpec((v.shape[0], tile), lambda i: (0, i)) for v in x]
            in_specs.append(pl.BlockSpec(g.shape, lambda i: (0, 0)))
            operands += [*x, g]
        width += group[0][1].shape[1]
    counts = tuple(tuple(len(x) for x, _ in group) for group in groups)
    return pl.pallas_call(
        functools.partial(wgrad_kernel, counts),
        grid=(D // tile,),
        in_specs=in_specs + [ANY] * len(behind),
        out_specs=pl.BlockSpec((tile, width), lambda i: (i, 0)),
        out_shape=shape_of((D, width)),
        compiler_params=params(),
        cost_estimate=cost(
            2 * SEQ_LEN * D * width, 4 * MIB * len(groups) + 2 * width * (SEQ_LEN + D)
        ),
        name="wgrad_kernel",
    )(*operands, *behind)


WIDE_RATE = 2.0 * D ** (-0.5)
OUT_RATE = 2.0 * max(1, 16 * D // SEQ_LEN) ** (-0.5)
DOWN_RATE = 2.0 * FF ** (-0.5)


def adamw(ins, outs, gradient, rate, decay=DECAY, at=slice(None)):
    weight, first, second = (ref[at] for ref in ins)
    first_new = BETA_ONE * first + (1.0 - BETA_ONE) * gradient
    second_new = BETA_TWO * second + (1.0 - BETA_TWO) * gradient * gradient
    first_hat = first_new / (1.0 - BETA_ONE**STEP)
    second_hat = second_new / (1.0 - BETA_TWO**STEP)
    outs[0][at] = weight - rate * (first_hat / (jnp.sqrt(second_hat) + ADAM_EPS) + decay * weight)
    outs[1][at] = first_new
    outs[2][at] = second_new


def step_call(kernel, operands, states, extra):
    flat = [v for group in states for v in group]
    return pl.pallas_call(
        kernel,
        out_shape=[shape_of(v.shape, F32) for v in flat] + list(extra),
        compiler_params=params(),
        cost_estimate=cost(0, 8 * sum(v.size for v in flat)),
        name=kernel.__name__,
    )(*operands, *flat)


def wide_step_kernel(sums, w, kvg, *refs):
    ins, outs = refs[:9], refs[9:]
    total, gain = 0.0, kvg[:, 129:130].astype(F32)
    for j in range(TILES):
        at = slice(128 * j, min(128 * (j + 1), HID))
        for s in range(3):
            start = 2 * PAD + 128 * j if s == 2 else 256 * j + 128 * s
            cols = slice(start, start + 128)
            g = sums[:, cols].astype(F32)
            if s < 2:
                total = total + g * w[:, cols].astype(F32)
                g = g * gain
            adamw(
                ins[3 * s : 3 * s + 3],
                outs[3 * s : 3 * s + 3],
                g.T[: at.stop - at.start],
                DOWN_RATE if s == 2 else WIDE_RATE,
                at=at,
            )
    outs[9][...] = jnp.sum(total, axis=-1, keepdims=True)


def sum_blocks(parts):
    total = parts[:ROWS].astype(F32)
    for i in range(1, 16):
        total = total + parts[ROWS * i : ROWS * (i + 1)].astype(F32)
    return total


def query_step_kernel(parts, w, gain, gain_two_sum, *refs):
    ins, outs, tail = refs[:6], refs[6:12], refs[12]
    g = sum_blocks(parts)
    adamw(ins[3:], outs[3:], g[:, AW:].T, OUT_RATE)
    g = g[:, :AW]
    gain_one_sum = jnp.sum(g * w[:, :AW].astype(F32), axis=-1, keepdims=True)
    g = g * gain[...]
    adamw(ins[:3], outs[:3], g[:, :QW], WIDE_RATE)
    tail[:, :128] = g[:, QW:]
    lane = lax.broadcasted_iota(jnp.int32, (ROWS, 128), 1)
    tail[:, 128:] = jnp.where(lane == 0, gain_one_sum, gain_two_sum[...])


def last_step_kernel(parts, *refs):
    heads = [parts[2 * h] + parts[2 * h + 1] for h in range(KV_HEADS)]
    key = jnp.concatenate([v[:, :HD] for v in heads], axis=1)
    value = jnp.concatenate([v[:, HD : 2 * HD] for v in heads], axis=1)
    adamw(refs[0:3], refs[6:9], key, WIDE_RATE)
    adamw(refs[3:6], refs[9:12], value, WIDE_RATE)
    refs[12][...] = functools.reduce(jnp.add, [v[:, 128:] for v in heads])


def adamw_step(weight, first, second, gradient, rate, decay):
    first_new = BETA_ONE * first + (1.0 - BETA_ONE) * gradient
    second_new = BETA_TWO * second + (1.0 - BETA_TWO) * gradient * gradient
    first_hat = first_new / (1.0 - BETA_ONE**STEP)
    second_hat = second_new / (1.0 - BETA_TWO**STEP)
    weight_new = weight - rate * (first_hat / (jnp.sqrt(second_hat) + ADAM_EPS) + decay * weight)
    return (weight_new, first_new, second_new)


def rotary():
    positions = jnp.arange(SEQ_LEN).astype(F32)
    frequency = 10000.0 ** (-2.0 * jnp.arange(HD // 2).astype(F32) / HD)
    angles = positions[:, None] * frequency[None, :]
    cos, sin = jnp.cos(angles), jnp.sin(angles)
    return (
        jnp.concatenate([cos] * 4, axis=1),
        jnp.concatenate([-sin, sin, -sin, sin], axis=1),
    )


def shards(
    tokens,
    cotangent,
    w_query,
    query_first,
    query_second,
    w_key,
    key_first,
    key_second,
    w_value,
    value_first,
    value_second,
    w_out,
    out_first,
    out_second,
    w_gate,
    gate_first,
    gate_second,
    w_up,
    up_first,
    up_second,
    w_down,
    down_first,
    down_second,
    norm_gains,
    gains_first,
    gains_second,
):
    z, core = lax.axis_index("z"), lax.axis_index("core")
    dp, ctx = ("y", "x"), ("z", "core")
    back = (z - jnp.arange(4)) % 4
    where = jnp.concatenate([back, core[None]]).astype(jnp.int32)
    order = jnp.concatenate([2 * back + 1 - core, 2 * back + core]).astype(jnp.int32)

    small = jnp.concatenate(
        [
            w_key.astype(BF).reshape(16, 4, HD),
            w_value.astype(BF).reshape(16, 4, HD),
            jnp.broadcast_to(
                jnp.pad(norm_gains.astype(BF).T, ((0, 0), (0, 126)))[:, None, :], (16, 4, 128)
            ),
        ],
        axis=2,
    ).transpose(1, 0, 2)
    small = jnp.broadcast_to(small[:, None], (4, 2, 16, 256)).reshape(ROWS, 256)
    kvg = swap_blocks(small, ctx)
    gain_one = kvg[:, 128:129].astype(F32)

    token_blocks = spread_z(tokens[0])
    grad_blocks = spread_z(cotangent[0])
    w_attend = attend_weights_call(kvg, w_query, w_out)
    near_attend = assemble_call("x", came(w_attend, "x"), token_blocks[1:])
    far_attend = came(near_attend, "y")
    w_ffn = ffn_weights_call(
        kvg, w_gate.T, w_up.T, w_down, far_attend[1:] + grad_blocks[1:]
    )
    all_ffn = lax.all_gather(w_ffn, dp, axis=0, tiled=True)
    all_attend, all_mixed = weights_call(far_attend)
    token_blocks = token_blocks + [other_core(t) for t in token_blocks]

    tcos, tsin = rotary()
    tokens_all, query, key_value, inv_all = first_call(
        where, token_blocks, all_attend, tcos, tsin, ()
    )
    grad_blocks = grad_blocks + [other_core(t) for t in grad_blocks]
    attended, lse = attend_call(query, key_value)

    def reduce_core(a, w, col, tile, behind=()):
        across, own = partial_call(order, a, w, col, tile)
        return add_call(other_core(across), own, behind)

    def reduce_z(parts):
        return [parts[0]] + [ring("z", 4 - k)(parts[k]) for k in (1, 2, 3)]

    def total(parts):
        return functools.reduce(jnp.add, [t.astype(F32) for t in parts])

    mixed_parts = reduce_core((attended,), all_mixed, 0, 1024, grad_blocks[5:])
    middle = tokens[0].astype(F32) + total(reduce_z(mixed_parts))
    inv_second = lax.rsqrt(jnp.mean(middle * middle, axis=-1, keepdims=True) + EPS)
    unit_second = middle * inv_second

    mid_blocks = spread(unit_second.astype(BF))
    hidden0, hidden1, wide0, wide1 = middle_call(where, mid_blocks, grad_blocks, all_ffn)
    wide_parts = reduce_core((wide1, wide0), all_ffn, 0, 512)
    mid_parts = reduce_z(wide_parts)
    ffn_wgrad = wgrad_call(
        256,
        ((mid_blocks[:4], wide0), (mid_blocks[4:], wide1)),
        ((grad_blocks[:4], hidden0), (grad_blocks[4:], hidden1)),
        behind=wide_parts[:1],
    )
    down_sums = partial_call(order, (hidden1, hidden0), all_ffn, 2, 512, wide_parts[:1])
    middle_grad, middle_low, ffn_wgrad, *down_sums = norm_back_call(
        mid_parts, middle, cotangent[0], (F32, BF), (ffn_wgrad, *down_sums)
    )
    ffn_sum = lax.psum_scatter(ffn_wgrad, dp, scatter_dimension=0, tiled=True)
    mid_grad_all, mixed_grad = mixed_grad_call(where, spread(middle_low), all_mixed)
    attend_grad, scaled_grad = attend_back_call(
        query, key_value, lse, mixed_grad, tcos, tsin, inv_all
    )
    attend_wgrad = wgrad_call(
        512, (([tokens_all], scaled_grad),), (([mid_grad_all], attended),)
    )
    attend_parts = swap_blocks(attend_wgrad, dp)
    in_parts = reduce_core((attend_grad,), all_attend, 0, 1024)
    in_parts = reduce_z(in_parts)
    (input_grad,) = norm_back_call(in_parts, tokens[0], middle_grad, (BF,))
    down_parts = add_call(other_core(down_sums[0]), down_sums[1], in_parts[1::2])
    output = middle + total(reduce_z(down_parts))

    *wide_new, gain_two_sum = step_call(
        wide_step_kernel,
        (ffn_sum, w_ffn, kvg),
        (
            (w_gate.T, gate_first.T, gate_second.T),
            (w_up.T, up_first.T, up_second.T),
            (w_down, down_first, down_second),
        ),
        [shape_of((ROWS, 1), F32)],
    )
    wide_new = [v.T for v in wide_new[:6]] + wide_new[6:]
    *query_new, tail = step_call(
        query_step_kernel,
        (attend_parts, w_attend, gain_one, gain_two_sum),
        ((w_query, query_first, query_second), (w_out, out_first, out_second)),
        [shape_of((ROWS, 256), F32)],
    )
    tail = swap_blocks(tail, ctx).reshape(8, 16, 256)
    *kv_new, gains_sum = step_call(
        last_step_kernel,
        (tail,),
        ((w_key, key_first, key_second), (w_value, value_first, value_second)),
        [shape_of((16, 128), F32)],
    )
    gains_sum = gains_sum[:, :2].T / norm_gains.astype(BF).astype(F32)
    gains_new = adamw_step(norm_gains, gains_first, gains_second, gains_sum, 0.3, 0.0)
    return (
        output.astype(BF)[None],
        input_grad[None],
        *query_new[:3],
        *kv_new,
        *query_new[3:],
        *wide_new,
        *gains_new,
    )


def solution(mesh):
    dp, ctx = ("y", "x"), ("z", "core")
    fine = Mesh(mesh.devices.reshape(4, 4, 4, 2), dp + ctx)
    act, col, row = P(dp, ctx, None), P(dp, ctx), P(ctx, dp)
    flat, gains = P(dp + ctx, None), P(None, dp + ctx)
    weights = (col,) * 3 + (flat,) * 6 + (row,) * 3 + (col,) * 6 + (row,) * 3 + (gains,) * 3
    return jax.shard_map(
        shards,
        mesh=fine,
        in_specs=(act, act) + weights,
        out_specs=(act, act) + weights,
        check_vma=False,
    )
```

```python
import functools

import jax
import jax.numpy as jnp
from jax import lax
from jax.experimental import pallas as pl
from jax.experimental.pallas import tpu as pltpu
from jax.sharding import Mesh
from jax.sharding import PartitionSpec as P

D = 2048
HEADS = 32
KV_HEADS = 4
HD = 64
FF = 5632
SEQ_LEN = 1024
STEP = 10

EPS = 1e-05
BETA_ONE = 0.9
BETA_TWO = 0.95
ADAM_EPS = 1e-08
DECAY = 0.1

ROWS = 128
HID = FF // 8
TILES = 6
PAD = TILES * 128
QW = 256
AW = 384
BF = jnp.bfloat16
F32 = jnp.float32
MIB = 2**20


def params(limit=56, **more):
    return pltpu.CompilerParams(vmem_limit_bytes=limit * MIB, **more)


def cost(flops, nbytes, trans=0):
    return pl.CostEstimate(flops=int(flops), bytes_accessed=int(nbytes), transcendentals=int(trans))


def dot(left, right):
    return jnp.dot(left, right, preferred_element_type=F32)


def dot_cols(left, right):
    return lax.dot_general(left, right, (((1,), (1,)), ((), ())), preferred_element_type=F32)


def dot_rows(left, right):
    return lax.dot_general(left, right, (((0,), (0,)), ((), ())), preferred_element_type=F32)


def swap_halves(v):
    width = v.shape[-1]
    lane = lax.broadcasted_iota(jnp.int32, v.shape, v.ndim - 1)
    return jnp.where(
        lane % HD < HD // 2,
        pltpu.roll(v, width - HD // 2, v.ndim - 1),
        pltpu.roll(v, HD // 2, v.ndim - 1),
    )


def ring(axis, k):
    return functools.partial(
        lax.ppermute, axis_name=axis, perm=[(i, (i + k) % 4) for i in range(4)]
    )


def other_core(v):
    return lax.ppermute(v, "core", [(0, 1), (1, 0)])


def spread_z(v):
    return [v, ring("z", 1)(v), ring("z", 2)(v), ring("z", 3)(v)]


def spread(v):
    own = spread_z(v)
    return own + [other_core(t) for t in own]


def came(v, axis):
    return [v] + [ring(axis, k)(v) for k in (1, 2, 3)]


def swap_blocks(v, axes):
    return lax.all_to_all(v, axes, split_axis=0, concat_axis=0, tiled=True)


ANY = pl.BlockSpec(memory_space=pl.ANY)
HELD = [pltpu.VMEM((4, 2 * ROWS, D), BF), pltpu.SemaphoreType.DMA((8,))]


def block_copy(halves, blocks, held, sems, k, half, source=None):
    source = blocks[4 * half + k] if source is None else source
    rows = pl.ds(pl.multiple_of(halves[half] * ROWS, ROWS), ROWS)
    return pltpu.make_async_copy(source, held.at[k, rows], sems.at[4 * half + k])


def start_blocks(halves, blocks, held, sems, at):
    for k in at:
        for half in range(2):
            block_copy(halves, blocks, held, sems, k, half).start()


def wait_blocks(halves, blocks, held, sems):
    step = pl.program_id(0)
    for half in range(2):
        block_copy(halves, blocks, held, sems, step, half, blocks[0]).wait()
    return held.at[step]


def load_blocks(halves, blocks, held, sems):
    @pl.when(pl.program_id(0) == 0)
    def _():
        start_blocks(halves, blocks, held, sems, range(4))

    return wait_blocks(halves, blocks, held, sems)


def by_block(width):
    return pl.BlockSpec((2 * ROWS, width), lambda i, where: (where[i], 0))


def by_step(width):
    return pl.BlockSpec((ROWS, width), lambda i, *_: (i, 0))


def whole(*shape):
    return pl.BlockSpec(shape, lambda i, *_: (0,) * len(shape))


def shape_of(shape, kind=BF):
    return jax.ShapeDtypeStruct(shape, kind)


def blocks_call(
    kernel, where, blocks, operands, in_specs, out_specs, outs, flops, behind=(), through=(), scratch=None
):
    n_in, n_out, n_more = 8 + len(operands), len(outs), len(behind) + len(through)

    def body(where, *refs):
        refs = list(refs)
        del refs[n_in + n_more + n_out : n_in + n_more + n_out + len(through)]
        del refs[n_in : n_in + n_more]
        kernel(where, *refs)

    nbytes = 4 * MIB + sum(o.size * o.dtype.itemsize for o in outs)
    nbytes += sum(o.size * o.dtype.itemsize for o in operands)
    first = 1 + n_in + len(behind)
    return pl.pallas_call(
        body,
        grid_spec=pltpu.PrefetchScalarGridSpec(
            num_scalar_prefetch=1,
            grid=(4,),
            in_specs=[ANY] * 8 + in_specs + [ANY] * n_more,
            out_specs=out_specs + [ANY] * len(through),
            scratch_shapes=scratch or HELD,
        ),
        out_shape=outs + [shape_of(v.shape, v.dtype) for v in through],
        input_output_aliases={first + i: n_out + i for i in range(len(through))},
        compiler_params=params(),
        cost_estimate=cost(flops, nbytes),
        name=kernel.__name__,
    )(where, *blocks, *operands, *behind, *through)


def assemble_call(axis, pieces, behind, through):
    order = ((lax.axis_index(axis) - jnp.arange(4)) % 4).astype(jnp.int32)

    def assemble_kernel(order, *refs):
        for k in range(4):
            refs[-2][order[k]] = refs[k][...]

    shape = pieces[0].shape
    return pl.pallas_call(
        assemble_kernel,
        grid_spec=pltpu.PrefetchScalarGridSpec(
            num_scalar_prefetch=1,
            grid=(1,),
            in_specs=[whole(*shape)] * 4 + [ANY] * (len(behind) + 1),
            out_specs=[whole(4, *shape), ANY],
        ),
        out_shape=[shape_of((4,) + shape), shape_of(through.shape)],
        input_output_aliases={5 + len(behind): 1},
        compiler_params=params(),
        cost_estimate=cost(0, 16 * pieces[0].size),
        name="assemble_kernel",
    )(order, *pieces, *behind, through)


def weights_kernel(order, *refs):
    for k in range(4):
        rows = pl.ds(pl.multiple_of(order[k] * 512, 512), 512)
        piece = refs[k][...].reshape(512, AW + QW)
        refs[-2][rows] = piece[:, :AW]
        refs[-1][rows] = piece[:, AW:]


def weights_call(pieces, behind):
    order = ((lax.axis_index("y") - jnp.arange(4)) % 4).astype(jnp.int32)
    return pl.pallas_call(
        weights_kernel,
        grid_spec=pltpu.PrefetchScalarGridSpec(
            num_scalar_prefetch=1,
            grid=(1,),
            in_specs=[whole(*pieces[0].shape)] * 4 + [ANY] * len(behind),
            out_specs=[whole(D, AW), whole(D, QW)],
        ),
        out_shape=[shape_of((D, AW)), shape_of((D, QW))],
        compiler_params=params(),
        cost_estimate=cost(0, 5 * MIB),
        name="weights_kernel",
    )(order, *pieces, *behind)


def small_kernel(key, value, gains, out):
    cols = gains[...].astype(BF).astype(F32)
    cols = jnp.concatenate([cols, jnp.zeros((6, 16), F32)], axis=0)
    cols = jnp.concatenate([cols, jnp.zeros((8, 112), F32)], axis=1)
    cols = jnp.concatenate([cols, jnp.zeros((120, 128), F32)], axis=0).T[:16].astype(BF)
    for h in range(KV_HEADS):
        at = slice(HD * h, HD * (h + 1))
        block = jnp.concatenate([key[:, at].astype(BF), value[:, at].astype(BF), cols], axis=1)
        out[32 * h : 32 * h + 16] = block
        out[32 * h + 16 : 32 * h + 32] = block


def small_call(key, value, gains):
    return pl.pallas_call(
        small_kernel,
        out_shape=shape_of((ROWS, 256)),
        compiler_params=params(),
        cost_estimate=cost(0, 1 << 17),
        name="small_kernel",
    )(key, value, gains)


def attend_weights_kernel(kvg, query, mixed, out):
    gain = kvg[:, 128:129].astype(F32)
    out[:, :QW] = (query[...].astype(BF).astype(F32) * gain).astype(BF)
    out[:, QW:AW] = (kvg[:, :128].astype(F32) * gain).astype(BF)
    out[:, AW:] = mixed[...].T.astype(BF)


def attend_weights_call(kvg, query, mixed):
    return pl.pallas_call(
        attend_weights_kernel,
        out_shape=shape_of((ROWS, AW + QW)),
        compiler_params=params(),
        cost_estimate=cost(0, MIB),
        name="attend_weights_kernel",
    )(kvg, query, mixed)


def ffn_weights_kernel(kvg, gate, up, down, *refs):
    out = refs[-1]
    gain = kvg[:, 129:130].astype(F32)
    for j in range(TILES):
        n = min(128, HID - 128 * j)
        for s, ref in enumerate((gate, up, down)):
            part = ref[128 * j : 128 * j + n]
            if n < 128:
                part = jnp.concatenate([part, jnp.zeros((128 - n, 128), F32)], axis=0)
            part = part.T.astype(BF)
            if s < 2:
                part = (part.astype(F32) * gain).astype(BF)
            at = 2 * PAD + 128 * j if s == 2 else 256 * j + 128 * s
            out[:, at : at + 128] = part


def ffn_weights_call(kvg, gate, up, down, behind):
    vmem = pl.BlockSpec(memory_space=pltpu.VMEM)
    return pl.pallas_call(
        ffn_weights_kernel,
        in_specs=[vmem] * 4 + [ANY] * len(behind),
        out_specs=vmem,
        out_shape=shape_of((ROWS, 3 * PAD)),
        compiler_params=params(),
        cost_estimate=cost(0, 2 * MIB),
        name="ffn_weights_kernel",
    )(kvg, gate, up, down, *behind)


def norm_back_kernel(n_through, *refs):
    parts, (x, base), outs = refs[:4], refs[4:6], refs[6 + n_through : len(refs) - n_through]
    v = x[...].astype(F32)
    inv = lax.rsqrt(jnp.mean(v * v, axis=-1, keepdims=True) + EPS)
    unit = v * inv
    u = functools.reduce(jnp.add, [ref[...].astype(F32) for ref in parts])
    out = base[...].astype(F32) + inv * (u - unit * jnp.mean(u * unit, axis=-1, keepdims=True))
    for ref in outs:
        ref[...] = out.astype(ref.dtype)


def norm_back_call(parts, x, base, kinds, through=()):
    rows = pl.BlockSpec((ROWS // 2, D), lambda i: (i, 0))
    return pl.pallas_call(
        functools.partial(norm_back_kernel, len(through)),
        grid=(2,),
        in_specs=[rows] * 6 + [ANY] * len(through),
        out_specs=[rows] * len(kinds) + [ANY] * len(through),
        out_shape=[shape_of((ROWS, D), kind) for kind in kinds]
        + [shape_of(v.shape, v.dtype) for v in through],
        input_output_aliases={6 + i: len(kinds) + i for i in range(len(through))},
        compiler_params=params(),
        cost_estimate=cost(0, 5 * MIB),
        name="norm_back_kernel",
    )(*parts, x, base, *through)


def send_products(left, weights, held, sems, outs):
    copies = []
    for t in range(4):
        at, w = weights(t)
        held[t] = dot_cols(left, w).astype(BF)
        half = left.shape[0] // 2
        for i, out in enumerate(outs):
            rows = pl.ds(i * half, half)
            copy = pltpu.make_async_copy(held.at[t, rows], out.at[:, at], sems.at[i, t])
            copy.start()
            copies.append(copy)
    for copy in copies:
        copy.wait()


def pick_rows(ref, order):
    return jnp.concatenate(
        [ref[pl.ds(pl.multiple_of(order[k] * ROWS, ROWS), ROWS)] for k in range(8)], axis=0
    )


SENT = [pltpu.VMEM((4, SEQ_LEN, 512), BF), pltpu.SemaphoreType.DMA((2, 4))]


def front_kernel(order, rows, *refs):
    pieces, (tcos, tsin, q_out, kv_out, inv_out, out, lse, *outs, held, sems) = refs[:4], refs[4:]
    step = pl.program_id(0)
    at = pl.ds(pl.multiple_of(step * 2 * ROWS, 2 * ROWS), 2 * ROWS)

    def piece(k):
        where = pl.ds(pl.multiple_of(order[8 + k] * 512, 512), 512)
        return where, pieces[k][...].reshape(512, AW + QW)

    y = 0.0
    for k in range(4):
        cols, w = piece(k)
        y = y + dot(rows[:, cols], w[:, :AW])
    x = rows[...].astype(F32)
    inv = lax.rsqrt(jnp.mean(x * x, axis=-1, keepdims=True) + EPS)
    inv_out[at] = jnp.broadcast_to(inv, (2 * ROWS, 128))
    cos, sin = tcos[...] * inv, tsin[...] * inv
    for j in range(2):
        part = y[:, j * 128 : (j + 1) * 128]
        q_out[at, j * 128 : (j + 1) * 128] = (part * cos + swap_halves(part) * sin).astype(BF)
    part = y[:, 256:384]
    is_key = lax.broadcasted_iota(jnp.int32, part.shape, 1) < HD
    kv_out[at] = jnp.where(is_key, part * cos + swap_halves(part) * sin, part * inv).astype(BF)

    @pl.when(step == 3)
    def _():
        attend_kernel(q_out, kv_out, out, lse)

        def weights(k):
            cols, w = piece(k)
            return cols, w[:, AW:]

        send_products(pick_rows(out, order), weights, held, sems, outs)


def front_call(order, rows, pieces, tcos, tsin):
    def block(width):
        return pl.BlockSpec((2 * ROWS, width), lambda i, *_: (i, 0))

    shapes = [(QW, BF), (128, BF), (128, F32), (QW, BF), (128, F32)]
    return pl.pallas_call(
        front_kernel,
        grid_spec=pltpu.PrefetchScalarGridSpec(
            num_scalar_prefetch=1,
            grid=(4,),
            in_specs=[block(D)] + [whole(4, ROWS, AW + QW)] * 4 + [block(128)] * 2,
            out_specs=[whole(SEQ_LEN, w) for w, _ in shapes] + [ANY] * 2,
            scratch_shapes=SENT,
        ),
        out_shape=[shape_of((SEQ_LEN, w), t) for w, t in shapes] + [shape_of((4 * ROWS, D))] * 2,
        compiler_params=params(),
        cost_estimate=cost(8e9, 16 * MIB, 2 * MIB),
        name="front_kernel",
    )(order, rows, *pieces, tcos, tsin)


def put_halves(outs, value, cols=slice(None)):
    outs[0][:, cols] = value[:ROWS]
    outs[1][:, cols] = value[ROWS:]


def middle_kernel(where, *refs):
    blocks, grad_all, w, refs = refs[:8], refs[8], refs[9], refs[10:]
    hiddens, grads, outs = refs[:2], refs[2:4], refs[4:6]
    held, sems, grad_held, grad_sems, wide, down, w_sems, both, sent, sent_sems = refs[6:]
    step = pl.program_id(0)
    first = step == 0
    grad_blocks = [
        grad_all.at[pl.ds(pl.multiple_of(where[5 + i] * ROWS, ROWS), ROWS)] for i in range(8)
    ]
    loads = ((0, 1), blocks, held, sems), ((0, 1), grad_blocks, grad_held, grad_sems)

    def w_copies(j):
        return (
            pltpu.make_async_copy(w.at[:, pl.ds(512 * j, 512)], wide.at[j], w_sems.at[0, j]),
            pltpu.make_async_copy(
                w.at[:, pl.ds(2 * PAD + 256 * j, 256)], down.at[j], w_sems.at[1, j]
            ),
        )

    @pl.when(first)
    def _():
        for j in range(4):
            for load in loads:
                start_blocks(*load, (j,))
            if j < TILES // 2:
                for copy in w_copies(j):
                    copy.start()

    x, c = (wait_blocks(*load) for load in loads)
    for j in range(TILES // 2):

        @pl.when(first)
        def _():
            for copy in w_copies(j):
                copy.wait()

        backs = dot(c[...], down[j])
        for i in range(2):
            t = 2 * j + i
            y = dot(x[...], wide[j, :, 256 * i : 256 * (i + 1)])
            gate, up, back = y[:, :128], y[:, 128:], backs[:, 128 * i : 128 * (i + 1)]
            sigma = jax.nn.sigmoid(gate)
            swish = gate * sigma
            put_halves(hiddens, (swish * up).astype(BF), slice(128 * t, 128 * (t + 1)))
            g = (back * up * (sigma * (1.0 + gate * (1.0 - sigma)))).astype(BF)
            g = jnp.concatenate([g, (back * swish).astype(BF)], axis=1)
            cols = slice(256 * t, 256 * (t + 1))
            put_halves(grads, g, cols)
            both[step, :, cols] = g[ROWS:]
            both[4 + step, :, cols] = g[:ROWS]

    @pl.when(step == 3)
    def _():
        left = both[...].reshape(SEQ_LEN, 2 * PAD)
        copies = []
        for t in range(4):
            at = slice(512 * t, 512 * (t + 1))
            y = 0.0
            for j in range(TILES // 2):
                y = y + dot_cols(left[:, 512 * j : 512 * (j + 1)], wide[j, at])
            sent[t] = y.astype(BF)
            for i, out in enumerate(outs):
                copy = pltpu.make_async_copy(
                    sent.at[t, pl.ds(i * 4 * ROWS, 4 * ROWS)],
                    out.at[:, pl.ds(512 * t, 512)],
                    sent_sems.at[i, t],
                )
                copy.start()
                copies.append(copy)
        for copy in copies:
            copy.wait()


def middle_call(where, blocks, grad_all, w):
    return blocks_call(
        middle_kernel,
        where,
        blocks,
        (grad_all, w),
        [ANY] * 2,
        [by_step(PAD)] * 2 + [by_step(2 * PAD)] * 2 + [ANY] * 2,
        [shape_of((4 * ROWS, PAD))] * 2
        + [shape_of((4 * ROWS, 2 * PAD))] * 2
        + [shape_of((4 * ROWS, D))] * 2,
        2 * SEQ_LEN * D * 5 * PAD,
        scratch=HELD * 2
        + [
            pltpu.VMEM((TILES // 2, D, 512), BF),
            pltpu.VMEM((TILES // 2, D, 256), BF),
            pltpu.SemaphoreType.DMA((2, TILES // 2)),
            pltpu.VMEM((8, ROWS, 2 * PAD), BF),
        ]
        + SENT,
    )


def partial_kernel(n_in, n_behind, n_through, order, *refs):
    w, (across, own) = refs[n_in], refs[n_in + 1 + n_behind + n_through :][:2]
    if n_in == 1:
        a = refs[0]
        left = jnp.concatenate(
            [a[pl.ds(pl.multiple_of(order[k] * ROWS, ROWS), ROWS)] for k in range(8)], axis=0
        )
    else:
        left = jnp.concatenate([refs[0][...], refs[1][...]], axis=0)
    y = dot_cols(left, w[...]).astype(BF)
    across[...] = y[: 4 * ROWS]
    own[...] = y[4 * ROWS :]


def partial_call(order, a, w, col, tile, behind=(), through=()):
    depth, first = a[0].shape[1], 2 + len(a) + len(behind)
    return pl.pallas_call(
        functools.partial(partial_kernel, len(a), len(behind), len(through)),
        grid_spec=pltpu.PrefetchScalarGridSpec(
            num_scalar_prefetch=1,
            grid=(D // tile,),
            in_specs=[whole(*v.shape) for v in a]
            + [pl.BlockSpec((tile, depth), lambda i, *_: (i, col))]
            + [ANY] * len(behind + through),
            out_specs=[pl.BlockSpec((4 * ROWS, tile), lambda i, *_: (0, i))] * 2
            + [ANY] * len(through),
        ),
        out_shape=[shape_of((4 * ROWS, D))] * 2 + [shape_of(v.shape, v.dtype) for v in through],
        input_output_aliases={first + i: 2 + i for i in range(len(through))},
        compiler_params=params(),
        cost_estimate=cost(2 * 8 * ROWS * D * depth, 2 * depth * (D + 1024) + 4 * MIB),
        name="partial_kernel",
    )(order, *a, w, *behind, *through)


def add_kernel(n_behind, across, own, *refs):
    n = own.shape[0] // ROWS
    outs, (held, sems) = refs[n_behind : n_behind + n], refs[n_behind + n :]
    loads, stores = [], []
    for k in range(n):
        rows = pl.ds(k * ROWS, ROWS)
        loads.append(
            [
                pltpu.make_async_copy(ref.at[rows], held.at[i, k], sems.at[i, k])
                for i, ref in enumerate((across, own))
            ]
        )
        stores.append(pltpu.make_async_copy(held.at[2, k], outs[k], sems.at[2, k]))
    for pair in loads:
        for copy in pair:
            copy.start()
    for k in range(n):
        for copy in loads[k]:
            copy.wait()
        held[2, k] = (held[0, k].astype(F32) + held[1, k].astype(F32)).astype(BF)
        stores[k].start()
    for copy in stores:
        copy.wait()


def add_call(across, own, behind=()):
    n = own.shape[0] // ROWS
    return pl.pallas_call(
        functools.partial(add_kernel, len(behind)),
        in_specs=[ANY] * (2 + len(behind)),
        out_specs=[ANY] * n,
        out_shape=[shape_of((ROWS, D))] * n,
        scratch_shapes=[pltpu.VMEM((3, n, ROWS, D), BF), pltpu.SemaphoreType.DMA((3, n))],
        compiler_params=params(),
        cost_estimate=cost(0, 6 * own.size),
        name="add_kernel",
    )(across, own, *behind)


def scores_of(q, k, diagonal):
    s = dot_cols(q, k)
    if diagonal:
        row = lax.broadcasted_iota(jnp.int32, s.shape, 0) % ROWS
        s = jnp.where(row >= lax.broadcasted_iota(jnp.int32, s.shape, 1), s, -1e30)
    return s


def stack_heads(v):
    return jnp.concatenate([v[:, HD * h : HD * (h + 1)] for h in range(4)], axis=0)


def lay_heads(v):
    return jnp.concatenate([v[ROWS * h : ROWS * (h + 1)] for h in range(4)], axis=1)


def attend_kernel(q, kv, out, lse):
    key, value = kv[:, :HD], kv[:, HD:]
    lane = lax.broadcasted_iota(jnp.int32, (ROWS, 128), 1)
    for b in range(8):
        rows = slice(b * ROWS, (b + 1) * ROWS)
        mine = stack_heads(q[rows] * HD**-0.5)
        pieces = [(scores_of(mine, key[rows], True), value[rows])]
        if b:
            pieces.append((scores_of(mine, key[: b * ROWS], False), value[: b * ROWS]))
        top = functools.reduce(
            jnp.maximum, [jnp.max(s, axis=-1, keepdims=True) for s, _ in pieces]
        )
        total, mixed = 0.0, 0.0
        for s, v in pieces:
            p = jnp.exp(s - top)
            total = total + jnp.sum(p, axis=-1, keepdims=True)
            mixed = mixed + dot(p.astype(BF), v)
        out[rows] = lay_heads(mixed / total).astype(BF)
        log_total = top + jnp.log(total)
        spread_out = jnp.zeros((ROWS, 128), F32)
        for h in range(4):
            spread_out = jnp.where(lane == h, log_total[ROWS * h : ROWS * (h + 1)], spread_out)
        lse[rows] = spread_out


def attend_back_kernel(
    q, kv, lse, mixed_grad, tcos, tsin, inv, grad_out, scaled_out, held
):
    key, value = kv[:, :HD], kv[:, HD:]
    held[...] = jnp.zeros_like(held)

    def put(rows, cols, part, turn):
        part = jnp.where(turn, part * tcos[rows] - swap_halves(part) * tsin[rows], part)
        grad_out[rows, cols] = part.astype(BF)
        scaled_out[rows, cols] = (part * inv[rows]).astype(BF)

    for b in range(8):
        rows = slice(b * ROWS, (b + 1) * ROWS)
        mine = stack_heads(q[rows] * HD**-0.5)
        grad = stack_heads(mixed_grad[rows])
        log_total = jnp.concatenate([lse[rows, h : h + 1] for h in range(4)], axis=0)
        pieces = [(rows, True)] + ([(slice(0, b * ROWS), False)] if b else [])
        probs, back = [], []
        inner = 0.0
        for cols, diagonal in pieces:
            p = jnp.exp(scores_of(mine, key[cols], diagonal) - log_total)
            g = dot_cols(grad, value[cols])
            inner = inner + jnp.sum(p * g, axis=-1, keepdims=True)
            probs.append(p)
            back.append(g)
        total = 0.0
        for (cols, _), p, g in zip(pieces, probs, back):
            s_grad = (p * (g - inner)).astype(BF)
            total = total + dot(s_grad, key[cols])
            held[:HD, cols] += dot_rows(mine, s_grad)
            held[HD:, cols] += dot_rows(grad, p.astype(BF))
        wide = lay_heads(total * HD**-0.5)
        for j in range(2):
            put(rows, slice(128 * j, 128 * (j + 1)), wide[:, 128 * j : 128 * (j + 1)], True)
    is_key = lax.broadcasted_iota(jnp.int32, (ROWS, 128), 1) < HD
    for b in range(8):
        rows = slice(b * ROWS, (b + 1) * ROWS)
        put(rows, slice(QW, AW), held[:, rows].T, is_key)


def back_kernel(where, *refs):
    blocks, refs = refs[:8], refs[8:]
    w_mixed, w, q, kv, lse, tcos, tsin, inv, all_out, scaled, *outs = refs[:12]
    held, sems, mixed_grad, grad, kv_held, sent, sent_sems = refs[12:]
    step = pl.program_id(0)
    x = load_blocks((where[4], 1 - where[4]), blocks, held, sems)
    all_out[...] = x[...]
    at = pl.ds(pl.multiple_of(where[step] * 2 * ROWS, 2 * ROWS), 2 * ROWS)
    mixed_grad[at] = dot(x[...], w_mixed[...]).astype(BF)

    @pl.when(step == 3)
    def _():
        attend_back_kernel(q, kv, lse, mixed_grad, tcos, tsin, inv, grad, scaled, kv_held)
        left = pick_rows(grad, [where[5 + k] for k in range(8)])
        send_products(
            left,
            lambda t: (pl.ds(512 * t, 512), w[512 * t : 512 * (t + 1)]),
            sent,
            sent_sems,
            outs,
        )


def back_call(where, blocks, *operands):
    widths = [QW, 128, 128, 128, 128, 128]
    return blocks_call(
        back_kernel,
        where,
        blocks,
        operands,
        [whole(D, QW), whole(D, AW)] + [whole(SEQ_LEN, w) for w in widths],
        [by_block(D), whole(SEQ_LEN, AW)] + [ANY] * 2,
        [shape_of((SEQ_LEN, D)), shape_of((SEQ_LEN, AW))] + [shape_of((4 * ROWS, D))] * 2,
        2 * SEQ_LEN * D * (QW + AW) + 8e9,
        scratch=HELD
        + [
            pltpu.VMEM((SEQ_LEN, QW), BF),
            pltpu.VMEM((SEQ_LEN, AW), BF),
            pltpu.VMEM((128, SEQ_LEN), F32),
        ]
        + SENT,
    )


def wgrad_kernel(counts, order, *refs):
    out = refs[-1]
    at, ref = 0, 0
    for group in counts:
        total = 0.0
        for n in group:
            x = refs[ref : ref + n]
            x = x[0][...] if n == 1 else jnp.concatenate([v[...] for v in x], axis=0)
            total = total + dot_rows(x, refs[ref + n][...])
            ref += n + 1
        out[:, at : at + total.shape[1]] = total.astype(BF)
        at += total.shape[1]


def wgrad_call(order, tile, *groups, behind=()):
    in_specs, operands, width = [], [], 0
    for group in groups:
        for i, (x, g) in enumerate(group):
            if isinstance(x, tuple):
                in_specs += [
                    pl.BlockSpec((ROWS, tile), lambda i, order, at=at: (order[at], i))
                    for at in x[1]
                ]
                group[i] = ([x[0]] * len(x[1]), g)
            else:
                in_specs += [pl.BlockSpec((v.shape[0], tile), lambda i, *_: (0, i)) for v in x]
            in_specs.append(whole(*g.shape))
            operands += [*group[i][0], g]
        width += group[0][1].shape[1]
    counts = tuple(tuple(len(x) for x, _ in group) for group in groups)
    return pl.pallas_call(
        functools.partial(wgrad_kernel, counts),
        grid_spec=pltpu.PrefetchScalarGridSpec(
            num_scalar_prefetch=1,
            grid=(D // tile,),
            in_specs=in_specs + [ANY] * len(behind),
            out_specs=pl.BlockSpec((tile, width), lambda i, *_: (i, 0)),
        ),
        out_shape=shape_of((D, width)),
        compiler_params=params(),
        cost_estimate=cost(
            2 * SEQ_LEN * D * width, 4 * MIB * len(groups) + 2 * width * (SEQ_LEN + D)
        ),
        name="wgrad_kernel",
    )(order, *operands, *behind)


WIDE_RATE = 2.0 * D ** (-0.5)
OUT_RATE = 2.0 * max(1, 16 * D // SEQ_LEN) ** (-0.5)
DOWN_RATE = 2.0 * FF ** (-0.5)


def adamw(ins, outs, gradient, rate, decay=DECAY, at=slice(None)):
    weight, first, second = (ref[at] for ref in ins)
    first_new = BETA_ONE * first + (1.0 - BETA_ONE) * gradient
    second_new = BETA_TWO * second + (1.0 - BETA_TWO) * gradient * gradient
    first_hat = first_new / (1.0 - BETA_ONE**STEP)
    second_hat = second_new / (1.0 - BETA_TWO**STEP)
    outs[0][at] = weight - rate * (first_hat / (jnp.sqrt(second_hat) + ADAM_EPS) + decay * weight)
    outs[1][at] = first_new
    outs[2][at] = second_new


def step_call(kernel, operands, states, extra):
    flat = [v for group in states for v in group]
    return pl.pallas_call(
        kernel,
        out_shape=[shape_of(v.shape, F32) for v in flat] + list(extra),
        compiler_params=params(),
        cost_estimate=cost(0, 8 * sum(v.size for v in flat)),
        name=kernel.__name__,
    )(*operands, *flat)


def wide_step_kernel(sums, w, kvg, *refs):
    ins, outs = refs[:9], refs[9:]
    total, gain = 0.0, kvg[:, 129:130].astype(F32)
    for j in range(TILES):
        at = slice(128 * j, min(128 * (j + 1), HID))
        for s in range(3):
            start = 2 * PAD + 128 * j if s == 2 else 256 * j + 128 * s
            cols = slice(start, start + 128)
            g = sums[:, cols].astype(F32)
            if s < 2:
                total = total + g * w[:, cols].astype(F32)
                g = g * gain
            adamw(
                ins[3 * s : 3 * s + 3],
                outs[3 * s : 3 * s + 3],
                g.T[: at.stop - at.start],
                DOWN_RATE if s == 2 else WIDE_RATE,
                at=at,
            )
    outs[9][...] = jnp.sum(total, axis=-1, keepdims=True)


def sum_blocks(parts):
    total = parts[:ROWS].astype(F32)
    for i in range(1, 16):
        total = total + parts[ROWS * i : ROWS * (i + 1)].astype(F32)
    return total


def query_step_kernel(parts, w, gain, gain_two_sum, *refs):
    ins, outs, tail = refs[:6], refs[6:12], refs[12]
    g = sum_blocks(parts)
    adamw(ins[3:], outs[3:], g[:, AW:].T, OUT_RATE)
    g = g[:, :AW]
    gain_one_sum = jnp.sum(g * w[:, :AW].astype(F32), axis=-1, keepdims=True)
    g = g * gain[...]
    adamw(ins[:3], outs[:3], g[:, :QW], WIDE_RATE)
    tail[:, :128] = g[:, QW:]
    lane = lax.broadcasted_iota(jnp.int32, (ROWS, 128), 1)
    tail[:, 128:] = jnp.where(lane == 0, gain_one_sum, gain_two_sum[...])


def last_step_kernel(parts, *refs):
    heads = [parts[2 * h] + parts[2 * h + 1] for h in range(KV_HEADS)]
    key = jnp.concatenate([v[:, :HD] for v in heads], axis=1)
    value = jnp.concatenate([v[:, HD : 2 * HD] for v in heads], axis=1)
    adamw(refs[0:3], refs[9:12], key, WIDE_RATE)
    adamw(refs[3:6], refs[12:15], value, WIDE_RATE)
    sums = functools.reduce(jnp.add, [v[:, 128:] for v in heads])
    sums = jnp.concatenate([sums, jnp.zeros((112, 128), F32)], axis=0).T[:2, :16]
    sums = sums / refs[6][...].astype(BF).astype(F32)
    adamw(refs[6:9], refs[15:18], sums, 0.3, 0.0)


def rotary():
    positions = jnp.arange(SEQ_LEN).astype(F32)
    frequency = 10000.0 ** (-2.0 * jnp.arange(HD // 2).astype(F32) / HD)
    angles = positions[:, None] * frequency[None, :]
    cos, sin = jnp.cos(angles), jnp.sin(angles)
    return (
        jnp.concatenate([cos] * 4, axis=1),
        jnp.concatenate([-sin, sin, -sin, sin], axis=1),
    )


def shards(
    tokens,
    cotangent,
    w_query,
    query_first,
    query_second,
    w_key,
    key_first,
    key_second,
    w_value,
    value_first,
    value_second,
    w_out,
    out_first,
    out_second,
    w_gate,
    gate_first,
    gate_second,
    w_up,
    up_first,
    up_second,
    w_down,
    down_first,
    down_second,
    norm_gains,
    gains_first,
    gains_second,
):
    z, core = lax.axis_index("z"), lax.axis_index("core")
    dp, ctx = ("y", "x"), ("z", "core")
    back = (z - jnp.arange(4)) % 4
    y_back = (lax.axis_index("y") - jnp.arange(4)) % 4
    order = jnp.concatenate([2 * back + 1 - core, 2 * back + core, y_back]).astype(jnp.int32)
    where = jnp.concatenate([back, core[None], order[4:8], order[:4]]).astype(jnp.int32)
    back_where = jnp.concatenate([back, core[None], order[:8]]).astype(jnp.int32)

    small = small_call(w_key, w_value, norm_gains)
    kvg = swap_blocks(small, ctx)
    gain_one = kvg[:, 128:129].astype(F32)

    tcos, tsin = rotary()
    tokens_all = lax.all_gather(tokens[0], ctx, axis=0, tiled=True)
    grad_all = lax.all_gather(cotangent[0], ctx, axis=0, tiled=True)
    w_attend = attend_weights_call(kvg, w_query, w_out)
    w_ffn = ffn_weights_call(kvg, w_gate.T, w_up.T, w_down, (w_attend,))
    near_attend, w_ffn = assemble_call("x", came(w_attend, "x"), (tcos, tsin), w_ffn)
    far_attend = came(near_attend, "y")
    query, key_value, inv_all, attended, lse, *mixed_parts = front_call(
        order, tokens_all, far_attend, tcos, tsin
    )
    all_ffn = lax.all_gather(w_ffn, dp, axis=0, tiled=True)

    def reduce_core(partials, behind=()):
        return add_call(other_core(partials[0]), partials[1], behind)

    def reduce_z(parts):
        return [parts[0]] + [ring("z", 4 - k)(parts[k]) for k in (1, 2, 3)]

    def total(parts):
        return functools.reduce(jnp.add, [t.astype(F32) for t in parts])

    mixed_parts = reduce_core(mixed_parts)
    all_attend, all_mixed = weights_call(far_attend, mixed_parts[:1])
    middle = tokens[0].astype(F32) + total(reduce_z(mixed_parts))
    inv_second = lax.rsqrt(jnp.mean(middle * middle, axis=-1, keepdims=True) + EPS)
    unit_second = middle * inv_second

    mid_blocks = spread(unit_second.astype(BF))
    hidden0, hidden1, wide0, wide1, *wide_parts = middle_call(
        where, mid_blocks, grad_all, all_ffn
    )
    wide_parts = reduce_core(wide_parts, (all_mixed,))
    mid_parts = reduce_z(wide_parts)
    ffn_wgrad = wgrad_call(
        order,
        256,
        [(mid_blocks[:4], wide0), (mid_blocks[4:], wide1)],
        [((grad_all, range(4, 8)), hidden0), ((grad_all, range(4)), hidden1)],
        behind=wide_parts[:1],
    )
    down_sums = partial_call(order, (hidden1, hidden0), all_ffn, 2, 512, wide_parts[:1])
    middle_grad, middle_low, ffn_wgrad, *down_sums = norm_back_call(
        mid_parts, middle, cotangent[0], (F32, BF), (ffn_wgrad, *down_sums)
    )
    ffn_sum = lax.psum_scatter(ffn_wgrad, dp, scatter_dimension=0, tiled=True)
    mid_grad_blocks = spread(middle_low)
    mid_grad_all, scaled_grad, *in_parts = back_call(
        back_where, mid_grad_blocks, all_mixed, all_attend, query, key_value, lse, tcos, tsin, inv_all
    )
    attend_wgrad = wgrad_call(
        order, 512, [([tokens_all], scaled_grad)], [([mid_grad_all], attended)]
    )
    in_parts = reduce_core(in_parts, (attend_wgrad,))
    attend_parts = swap_blocks(attend_wgrad, dp)
    in_parts = reduce_z(in_parts)
    (input_grad,) = norm_back_call(in_parts, tokens[0], middle_grad, (BF,))
    down_parts = add_call(other_core(down_sums[0]), down_sums[1], in_parts[1:2])
    output = middle + total(reduce_z(down_parts))

    *wide_new, gain_two_sum = step_call(
        wide_step_kernel,
        (ffn_sum, w_ffn, kvg),
        (
            (w_gate.T, gate_first.T, gate_second.T),
            (w_up.T, up_first.T, up_second.T),
            (w_down, down_first, down_second),
        ),
        [shape_of((ROWS, 1), F32)],
    )
    wide_new = [v.T for v in wide_new[:6]] + wide_new[6:]
    *query_new, tail = step_call(
        query_step_kernel,
        (attend_parts, w_attend, gain_one, gain_two_sum),
        ((w_query, query_first, query_second), (w_out, out_first, out_second)),
        [shape_of((ROWS, 256), F32)],
    )
    tail = swap_blocks(tail, ctx).reshape(8, 16, 256)
    last_new = step_call(
        last_step_kernel,
        (tail,),
        (
            (w_key, key_first, key_second),
            (w_value, value_first, value_second),
            (norm_gains, gains_first, gains_second),
        ),
        [],
    )
    return (
        output.astype(BF)[None],
        input_grad[None],
        *query_new[:3],
        *last_new[:6],
        *query_new[3:],
        *wide_new,
        *last_new[6:],
    )


def solution(mesh):
    dp, ctx = ("y", "x"), ("z", "core")
    fine = Mesh(mesh.devices.reshape(4, 4, 4, 2), dp + ctx)
    act, col, row = P(dp, ctx, None), P(dp, ctx), P(ctx, dp)
    flat, gains = P(dp + ctx, None), P(None, dp + ctx)
    weights = (col,) * 3 + (flat,) * 6 + (row,) * 3 + (col,) * 6 + (row,) * 3 + (gains,) * 3
    return jax.shard_map(
        shards,
        mesh=fine,
        in_specs=(act, act) + weights,
        out_specs=(act, act) + weights,
        check_vma=False,
    )
```

```python
import functools

import jax
import jax.numpy as jnp
from jax import lax
from jax.experimental import pallas as pl
from jax.experimental.pallas import tpu as pltpu
from jax.sharding import Mesh
from jax.sharding import PartitionSpec as P

D = 2048
HEADS = 32
KV_HEADS = 4
HD = 64
FF = 5632
SEQ_LEN = 1024
STEP = 10

EPS = 1e-05
BETA_ONE = 0.9
BETA_TWO = 0.95
ADAM_EPS = 1e-08
DECAY = 0.1

ROWS = 128
HID = FF // 8
TILES = 6
PAD = TILES * 128
QW = 256
AW = 384
BF = jnp.bfloat16
F32 = jnp.float32
MIB = 2**20


def params(limit=56, **more):
    return pltpu.CompilerParams(vmem_limit_bytes=limit * MIB, **more)


def cost(flops, nbytes, trans=0):
    return pl.CostEstimate(flops=int(flops), bytes_accessed=int(nbytes), transcendentals=int(trans))


def dot(left, right):
    return jnp.dot(left, right, preferred_element_type=F32)


def dot_cols(left, right):
    return lax.dot_general(left, right, (((1,), (1,)), ((), ())), preferred_element_type=F32)


def dot_rows(left, right):
    return lax.dot_general(left, right, (((0,), (0,)), ((), ())), preferred_element_type=F32)


def swap_halves(v):
    width = v.shape[-1]
    lane = lax.broadcasted_iota(jnp.int32, v.shape, v.ndim - 1)
    return jnp.where(
        lane % HD < HD // 2,
        pltpu.roll(v, width - HD // 2, v.ndim - 1),
        pltpu.roll(v, HD // 2, v.ndim - 1),
    )


def ring(axis, k):
    return functools.partial(
        lax.ppermute, axis_name=axis, perm=[(i, (i + k) % 4) for i in range(4)]
    )


def other_core(v):
    return lax.ppermute(v, "core", [(0, 1), (1, 0)])


def spread_z(v):
    return [v, ring("z", 1)(v), ring("z", 2)(v), ring("z", 3)(v)]


def spread(v):
    own = spread_z(v)
    return own + [other_core(t) for t in own]


def swap_blocks(v, axes):
    return lax.all_to_all(v, axes, split_axis=0, concat_axis=0, tiled=True)


ANY = pl.BlockSpec(memory_space=pltpu.HBM)
HELD = [pltpu.VMEM((4, 2 * ROWS, D), BF), pltpu.SemaphoreType.DMA((8,))]


def block_copy(halves, blocks, held, sems, k, half, source=None):
    source = blocks[4 * half + k] if source is None else source
    rows = pl.ds(pl.multiple_of(halves[half] * ROWS, ROWS), ROWS)
    return pltpu.make_async_copy(source, held.at[k, rows], sems.at[4 * half + k])


def start_blocks(halves, blocks, held, sems, at):
    for k in at:
        for half in range(2):
            block_copy(halves, blocks, held, sems, k, half).start()


def wait_blocks(halves, blocks, held, sems):
    step = pl.program_id(0)
    for half in range(2):
        block_copy(halves, blocks, held, sems, step, half, blocks[0]).wait()
    return held.at[step]


def load_blocks(halves, blocks, held, sems):
    @pl.when(pl.program_id(0) == 0)
    def _():
        start_blocks(halves, blocks, held, sems, range(4))

    return wait_blocks(halves, blocks, held, sems)


def by_block(width):
    return pl.BlockSpec((2 * ROWS, width), lambda i, where: (where[i], 0))


def by_step(width):
    return pl.BlockSpec((ROWS, width), lambda i, *_: (i, 0))


def whole(*shape):
    return pl.BlockSpec(shape, lambda i, *_: (0,) * len(shape))


def shape_of(shape, kind=BF):
    return jax.ShapeDtypeStruct(shape, kind)


def blocks_call(
    kernel, where, blocks, operands, in_specs, out_specs, outs, flops, behind=(), through=(), scratch=None
):
    n_in, n_out, n_more = 8 + len(operands), len(outs), len(behind) + len(through)

    def body(where, *refs):
        refs = list(refs)
        del refs[n_in + n_more + n_out : n_in + n_more + n_out + len(through)]
        del refs[n_in : n_in + n_more]
        kernel(where, *refs)

    nbytes = 4 * MIB + sum(o.size * o.dtype.itemsize for o in outs)
    nbytes += sum(o.size * o.dtype.itemsize for o in operands)
    first = 1 + n_in + len(behind)
    return pl.pallas_call(
        body,
        grid_spec=pltpu.PrefetchScalarGridSpec(
            num_scalar_prefetch=1,
            grid=(4,),
            in_specs=[ANY] * 8 + in_specs + [ANY] * n_more,
            out_specs=out_specs + [ANY] * len(through),
            scratch_shapes=scratch or HELD,
        ),
        out_shape=outs + [shape_of(v.shape, v.dtype) for v in through],
        input_output_aliases={first + i: n_out + i for i in range(len(through))},
        compiler_params=params(),
        cost_estimate=cost(flops, nbytes),
        name=kernel.__name__,
    )(where, *blocks, *operands, *behind, *through)


def small_kernel(key, value, gains, out):
    cols = gains[...].astype(BF).astype(F32)
    cols = jnp.concatenate([cols, jnp.zeros((6, 16), F32)], axis=0)
    cols = jnp.concatenate([cols, jnp.zeros((8, 112), F32)], axis=1)
    cols = jnp.concatenate([cols, jnp.zeros((120, 128), F32)], axis=0).T[:16].astype(BF)
    for h in range(KV_HEADS):
        at = slice(HD * h, HD * (h + 1))
        block = jnp.concatenate([key[:, at].astype(BF), value[:, at].astype(BF), cols], axis=1)
        out[32 * h : 32 * h + 16] = block
        out[32 * h + 16 : 32 * h + 32] = block


def small_call(key, value, gains):
    return pl.pallas_call(
        small_kernel,
        out_shape=shape_of((ROWS, 256)),
        compiler_params=params(),
        cost_estimate=cost(0, 1 << 17),
        name="small_kernel",
    )(key, value, gains)


def weights_kernel(kvg, query, mixed, gate, up, down, attend_out, copies, ffn_out):
    gain = kvg[:, 128:129].astype(F32)
    attend_out[:, :QW] = (query[...].astype(BF).astype(F32) * gain).astype(BF)
    attend_out[:, QW:AW] = (kvg[:, :128].astype(F32) * gain).astype(BF)
    attend_out[:, AW:] = mixed[...].T.astype(BF)
    for i in range(16):
        copies[ROWS * i : ROWS * (i + 1)] = attend_out[...]
    gain = kvg[:, 129:130].astype(F32)
    for j in range(TILES):
        n = min(128, HID - 128 * j)
        for s, ref in enumerate((gate, up, down)):
            part = ref[128 * j : 128 * j + n]
            if n < 128:
                part = jnp.concatenate([part, jnp.zeros((128 - n, 128), F32)], axis=0)
            part = part.T.astype(BF)
            if s < 2:
                part = (part.astype(F32) * gain).astype(BF)
            at = 2 * PAD + 128 * j if s == 2 else 256 * j + 128 * s
            ffn_out[:, at : at + 128] = part


def weights_call(*operands):
    return pl.pallas_call(
        weights_kernel,
        out_shape=[
            shape_of((ROWS, AW + QW)),
            shape_of((D, AW + QW)),
            shape_of((ROWS, 3 * PAD)),
        ],
        compiler_params=params(),
        cost_estimate=cost(0, 5 * MIB),
        name="weights_kernel",
    )(*operands)


def norm_back_kernel(n_through, *refs):
    parts, (x, base), outs = refs[:4], refs[4:6], refs[6 + n_through : len(refs) - n_through]
    v = x[...].astype(F32)
    inv = lax.rsqrt(jnp.mean(v * v, axis=-1, keepdims=True) + EPS)
    unit = v * inv
    u = functools.reduce(jnp.add, [ref[...].astype(F32) for ref in parts])
    out = base[...].astype(F32) + inv * (u - unit * jnp.mean(u * unit, axis=-1, keepdims=True))
    for ref in outs:
        ref[...] = out.astype(ref.dtype)


def norm_back_call(parts, x, base, kinds, through=()):
    rows = pl.BlockSpec((ROWS // 2, D), lambda i: (i, 0))
    return pl.pallas_call(
        functools.partial(norm_back_kernel, len(through)),
        grid=(2,),
        in_specs=[rows] * 6 + [ANY] * len(through),
        out_specs=[rows] * len(kinds) + [ANY] * len(through),
        out_shape=[shape_of((ROWS, D), kind) for kind in kinds]
        + [shape_of(v.shape, v.dtype) for v in through],
        input_output_aliases={6 + i: len(kinds) + i for i in range(len(through))},
        compiler_params=params(),
        cost_estimate=cost(0, 5 * MIB),
        name="norm_back_kernel",
    )(*parts, x, base, *through)


def send_products(left, w, start, end, held, sems, outs):
    copies = []
    half = left.shape[0] // 2
    for t in range(4):
        held[t] = dot_cols(left, w[512 * t : 512 * (t + 1), start:end]).astype(BF)
        for i, out in enumerate(outs):
            copy = pltpu.make_async_copy(
                held.at[t, pl.ds(i * half, half)], out.at[:, pl.ds(512 * t, 512)], sems.at[i, t]
            )
            copy.start()
            copies.append(copy)
    for copy in copies:
        copy.wait()


def pick_rows(ref, order):
    return jnp.concatenate(
        [ref[pl.ds(pl.multiple_of(order[k] * ROWS, ROWS), ROWS)] for k in range(8)], axis=0
    )


SENT = [pltpu.VMEM((4, SEQ_LEN, 512), BF), pltpu.SemaphoreType.DMA((2, 4))]


def front_kernel(order, rows, *refs):
    w, tcos, tsin, q_out, kv_out, inv_out, out, lse, *outs, held, sems = refs
    step = pl.program_id(0)
    at = pl.ds(pl.multiple_of(step * 2 * ROWS, 2 * ROWS), 2 * ROWS)

    y = dot(rows[...], w[:, :AW])
    x = rows[...].astype(F32)
    inv = lax.rsqrt(jnp.mean(x * x, axis=-1, keepdims=True) + EPS)
    inv_out[at] = jnp.broadcast_to(inv, (2 * ROWS, 128))
    cos, sin = tcos[...] * inv, tsin[...] * inv
    for j in range(2):
        part = y[:, j * 128 : (j + 1) * 128]
        q_out[at, j * 128 : (j + 1) * 128] = (part * cos + swap_halves(part) * sin).astype(BF)
    part = y[:, 256:384]
    is_key = lax.broadcasted_iota(jnp.int32, part.shape, 1) < HD
    kv_out[at] = jnp.where(is_key, part * cos + swap_halves(part) * sin, part * inv).astype(BF)

    @pl.when(step == 3)
    def _():
        attend_kernel(q_out, kv_out, out, lse)
        send_products(pick_rows(out, order), w, AW, AW + QW, held, sems, outs)


def front_call(order, rows, w, tcos, tsin):
    def block(width):
        return pl.BlockSpec((2 * ROWS, width), lambda i, *_: (i, 0))

    shapes = [(QW, BF), (128, BF), (128, F32), (QW, BF), (128, F32)]
    return pl.pallas_call(
        front_kernel,
        grid_spec=pltpu.PrefetchScalarGridSpec(
            num_scalar_prefetch=1,
            grid=(4,),
            in_specs=[block(D), whole(D, AW + QW)] + [block(128)] * 2,
            out_specs=[whole(SEQ_LEN, w) for w, _ in shapes] + [ANY] * 2,
            scratch_shapes=SENT,
        ),
        out_shape=[shape_of((SEQ_LEN, w), t) for w, t in shapes] + [shape_of((4 * ROWS, D))] * 2,
        compiler_params=params(),
        cost_estimate=cost(8e9, 16 * MIB, 2 * MIB),
        name="front_kernel",
    )(order, rows, w, tcos, tsin)


def put_halves(outs, value, cols=slice(None)):
    outs[0][:, cols] = value[:ROWS]
    outs[1][:, cols] = value[ROWS:]


def middle_kernel(where, *refs):
    blocks, grad_all, w, refs = refs[:8], refs[8], refs[9], refs[10:]
    hiddens, grads, outs = refs[:2], refs[2:4], refs[4:6]
    held, sems, grad_held, grad_sems, wide, down, w_sems, both, sent, sent_sems = refs[6:]
    step = pl.program_id(0)
    first = step == 0
    grad_blocks = [
        grad_all.at[pl.ds(pl.multiple_of(where[5 + i] * ROWS, ROWS), ROWS)] for i in range(8)
    ]
    loads = ((0, 1), blocks, held, sems), ((0, 1), grad_blocks, grad_held, grad_sems)

    def w_copies(j):
        return (
            pltpu.make_async_copy(w.at[:, pl.ds(512 * j, 512)], wide.at[j], w_sems.at[0, j]),
            pltpu.make_async_copy(
                w.at[:, pl.ds(2 * PAD + 256 * j, 256)], down.at[j], w_sems.at[1, j]
            ),
        )

    @pl.when(first)
    def _():
        for j in range(4):
            for load in loads:
                start_blocks(*load, (j,))
            if j < TILES // 2:
                for copy in w_copies(j):
                    copy.start()

    x, c = (wait_blocks(*load) for load in loads)
    for j in range(TILES // 2):

        @pl.when(first)
        def _():
            for copy in w_copies(j):
                copy.wait()

        backs = dot(c[...], down[j])
        for i in range(2):
            t = 2 * j + i
            y = dot(x[...], wide[j, :, 256 * i : 256 * (i + 1)])
            gate, up, back = y[:, :128], y[:, 128:], backs[:, 128 * i : 128 * (i + 1)]
            sigma = jax.nn.sigmoid(gate)
            swish = gate * sigma
            put_halves(hiddens, (swish * up).astype(BF), slice(128 * t, 128 * (t + 1)))
            g = (back * up * (sigma * (1.0 + gate * (1.0 - sigma)))).astype(BF)
            g = jnp.concatenate([g, (back * swish).astype(BF)], axis=1)
            cols = slice(256 * t, 256 * (t + 1))
            put_halves(grads, g, cols)
            both[step, :, cols] = g[ROWS:]
            both[4 + step, :, cols] = g[:ROWS]

    @pl.when(step == 3)
    def _():
        left = both[...].reshape(SEQ_LEN, 2 * PAD)
        copies = []
        for t in range(4):
            at = slice(512 * t, 512 * (t + 1))
            y = 0.0
            for j in range(TILES // 2):
                y = y + dot_cols(left[:, 512 * j : 512 * (j + 1)], wide[j, at])
            sent[t] = y.astype(BF)
            for i, out in enumerate(outs):
                copy = pltpu.make_async_copy(
                    sent.at[t, pl.ds(i * 4 * ROWS, 4 * ROWS)],
                    out.at[:, pl.ds(512 * t, 512)],
                    sent_sems.at[i, t],
                )
                copy.start()
                copies.append(copy)
        for copy in copies:
            copy.wait()


def middle_call(where, blocks, grad_all, w):
    return blocks_call(
        middle_kernel,
        where,
        blocks,
        (grad_all, w),
        [ANY] * 2,
        [by_step(PAD)] * 2 + [by_step(2 * PAD)] * 2 + [ANY] * 2,
        [shape_of((4 * ROWS, PAD))] * 2
        + [shape_of((4 * ROWS, 2 * PAD))] * 2
        + [shape_of((4 * ROWS, D))] * 2,
        2 * SEQ_LEN * D * 5 * PAD,
        scratch=HELD * 2
        + [
            pltpu.VMEM((TILES // 2, D, 512), BF),
            pltpu.VMEM((TILES // 2, D, 256), BF),
            pltpu.SemaphoreType.DMA((2, TILES // 2)),
            pltpu.VMEM((8, ROWS, 2 * PAD), BF),
        ]
        + SENT,
    )


def partial_kernel(n_in, n_behind, n_through, order, *refs):
    w, (across, own) = refs[n_in], refs[n_in + 1 + n_behind + n_through :][:2]
    if n_in == 1:
        a = refs[0]
        left = jnp.concatenate(
            [a[pl.ds(pl.multiple_of(order[k] * ROWS, ROWS), ROWS)] for k in range(8)], axis=0
        )
    else:
        left = jnp.concatenate([refs[0][...], refs[1][...]], axis=0)
    y = dot_cols(left, w[...]).astype(BF)
    across[...] = y[: 4 * ROWS]
    own[...] = y[4 * ROWS :]


def partial_call(order, a, w, col, tile, behind=(), through=()):
    depth, first = a[0].shape[1], 2 + len(a) + len(behind)
    return pl.pallas_call(
        functools.partial(partial_kernel, len(a), len(behind), len(through)),
        grid_spec=pltpu.PrefetchScalarGridSpec(
            num_scalar_prefetch=1,
            grid=(D // tile,),
            in_specs=[whole(*v.shape) for v in a]
            + [pl.BlockSpec((tile, depth), lambda i, *_: (i, col))]
            + [ANY] * (len(behind) + len(through)),
            out_specs=[pl.BlockSpec((4 * ROWS, tile), lambda i, *_: (0, i))] * 2
            + [ANY] * len(through),
        ),
        out_shape=[shape_of((4 * ROWS, D))] * 2 + [shape_of(v.shape, v.dtype) for v in through],
        input_output_aliases={first + i: 2 + i for i in range(len(through))},
        compiler_params=params(),
        cost_estimate=cost(2 * 8 * ROWS * D * depth, 2 * depth * (D + 1024) + 4 * MIB),
        name="partial_kernel",
    )(order, *a, w, *behind, *through)


def add_kernel(n_behind, across, own, *refs):
    n = own.shape[0] // ROWS
    outs, (held, sems) = refs[n_behind : n_behind + n], refs[n_behind + n :]
    loads, stores = [], []
    for k in range(n):
        rows = pl.ds(k * ROWS, ROWS)
        loads.append(
            [
                pltpu.make_async_copy(ref.at[rows], held.at[i, k], sems.at[i, k])
                for i, ref in enumerate((across, own))
            ]
        )
        stores.append(pltpu.make_async_copy(held.at[2, k], outs[k], sems.at[2, k]))
    for pair in loads:
        for copy in pair:
            copy.start()
    for k in range(n):
        for copy in loads[k]:
            copy.wait()
        held[2, k] = (held[0, k].astype(F32) + held[1, k].astype(F32)).astype(BF)
        stores[k].start()
    for copy in stores:
        copy.wait()


def add_call(across, own, behind=()):
    n = own.shape[0] // ROWS
    return pl.pallas_call(
        functools.partial(add_kernel, len(behind)),
        in_specs=[ANY] * (2 + len(behind)),
        out_specs=[ANY] * n,
        out_shape=[shape_of((ROWS, D))] * n,
        scratch_shapes=[pltpu.VMEM((3, n, ROWS, D), BF), pltpu.SemaphoreType.DMA((3, n))],
        compiler_params=params(),
        cost_estimate=cost(0, 6 * own.size),
        name="add_kernel",
    )(across, own, *behind)


def scores_of(q, k, diagonal):
    s = dot_cols(q, k)
    if diagonal:
        row = lax.broadcasted_iota(jnp.int32, s.shape, 0) % ROWS
        s = jnp.where(row >= lax.broadcasted_iota(jnp.int32, s.shape, 1), s, -1e30)
    return s


def stack_heads(v):
    return jnp.concatenate([v[:, HD * h : HD * (h + 1)] for h in range(4)], axis=0)


def lay_heads(v):
    return jnp.concatenate([v[ROWS * h : ROWS * (h + 1)] for h in range(4)], axis=1)


def attend_kernel(q, kv, out, lse):
    key, value = kv[:, :HD], kv[:, HD:]
    lane = lax.broadcasted_iota(jnp.int32, (ROWS, 128), 1)
    for b in range(8):
        rows = slice(b * ROWS, (b + 1) * ROWS)
        mine = stack_heads(q[rows] * HD**-0.5)
        pieces = [(scores_of(mine, key[rows], True), value[rows])]
        if b:
            pieces.append((scores_of(mine, key[: b * ROWS], False), value[: b * ROWS]))
        top = functools.reduce(
            jnp.maximum, [jnp.max(s, axis=-1, keepdims=True) for s, _ in pieces]
        )
        total, mixed = 0.0, 0.0
        for s, v in pieces:
            p = jnp.exp(s - top)
            total = total + jnp.sum(p, axis=-1, keepdims=True)
            mixed = mixed + dot(p.astype(BF), v)
        out[rows] = lay_heads(mixed / total).astype(BF)
        log_total = top + jnp.log(total)
        spread_out = jnp.zeros((ROWS, 128), F32)
        for h in range(4):
            spread_out = jnp.where(lane == h, log_total[ROWS * h : ROWS * (h + 1)], spread_out)
        lse[rows] = spread_out


def attend_back_kernel(
    q, kv, lse, mixed_grad, tcos, tsin, inv, grad_out, scaled_out, held
):
    key, value = kv[:, :HD], kv[:, HD:]
    held[...] = jnp.zeros_like(held)

    def put(rows, cols, part, turn):
        part = jnp.where(turn, part * tcos[rows] - swap_halves(part) * tsin[rows], part)
        grad_out[rows, cols] = part.astype(BF)
        scaled_out[rows, cols] = (part * inv[rows]).astype(BF)

    for b in range(8):
        rows = slice(b * ROWS, (b + 1) * ROWS)
        mine = stack_heads(q[rows] * HD**-0.5)
        grad = stack_heads(mixed_grad[rows])
        log_total = jnp.concatenate([lse[rows, h : h + 1] for h in range(4)], axis=0)
        pieces = [(rows, True)] + ([(slice(0, b * ROWS), False)] if b else [])
        probs, back = [], []
        inner = 0.0
        for cols, diagonal in pieces:
            p = jnp.exp(scores_of(mine, key[cols], diagonal) - log_total)
            g = dot_cols(grad, value[cols])
            inner = inner + jnp.sum(p * g, axis=-1, keepdims=True)
            probs.append(p)
            back.append(g)
        total = 0.0
        for (cols, _), p, g in zip(pieces, probs, back):
            s_grad = (p * (g - inner)).astype(BF)
            total = total + dot(s_grad, key[cols])
            held[:HD, cols] += dot_rows(mine, s_grad)
            held[HD:, cols] += dot_rows(grad, p.astype(BF))
        wide = lay_heads(total * HD**-0.5)
        for j in range(2):
            put(rows, slice(128 * j, 128 * (j + 1)), wide[:, 128 * j : 128 * (j + 1)], True)
    is_key = lax.broadcasted_iota(jnp.int32, (ROWS, 128), 1) < HD
    for b in range(8):
        rows = slice(b * ROWS, (b + 1) * ROWS)
        put(rows, slice(QW, AW), held[:, rows].T, is_key)


def back_kernel(where, *refs):
    blocks, refs = refs[:8], refs[8:]
    w, q, kv, lse, tcos, tsin, inv, all_out, scaled, *outs = refs[:11]
    held, sems, mixed_grad, grad, kv_held, sent, sent_sems = refs[11:]
    step = pl.program_id(0)
    x = load_blocks((where[4], 1 - where[4]), blocks, held, sems)
    all_out[...] = x[...]
    at = pl.ds(pl.multiple_of(where[step] * 2 * ROWS, 2 * ROWS), 2 * ROWS)
    mixed_grad[at] = dot(x[...], w[:, AW:]).astype(BF)

    @pl.when(step == 3)
    def _():
        attend_back_kernel(q, kv, lse, mixed_grad, tcos, tsin, inv, grad, scaled, kv_held)
        left = pick_rows(grad, [where[5 + k] for k in range(8)])
        send_products(left, w, 0, AW, sent, sent_sems, outs)


BACK_COST = 1.54e11


def back_call(where, blocks, operands):
    widths = [QW, 128, 128, 128, 128, 128]
    return blocks_call(
        back_kernel,
        where,
        blocks,
        operands,
        [whole(D, AW + QW)] + [whole(SEQ_LEN, w) for w in widths],
        [by_block(D), whole(SEQ_LEN, AW)] + [ANY] * 2,
        [shape_of((SEQ_LEN, D)), shape_of((SEQ_LEN, AW))] + [shape_of((4 * ROWS, D))] * 2,
        BACK_COST,
        scratch=HELD
        + [
            pltpu.VMEM((SEQ_LEN, QW), BF),
            pltpu.VMEM((SEQ_LEN, AW), BF),
            pltpu.VMEM((128, SEQ_LEN), F32),
        ]
        + SENT,
    )


def wgrad_kernel(counts, order, *refs):
    out = refs[-1]
    at, ref = 0, 0
    for group in counts:
        total = 0.0
        for n in group:
            x = refs[ref : ref + n]
            x = x[0][...] if n == 1 else jnp.concatenate([v[...] for v in x], axis=0)
            total = total + dot_rows(x, refs[ref + n][...])
            ref += n + 1
        out[:, at : at + total.shape[1]] = total.astype(BF)
        at += total.shape[1]


def wgrad_call(order, tile, *groups, behind=()):
    in_specs, operands, width = [], [], 0
    for group in groups:
        for i, (x, g) in enumerate(group):
            if isinstance(x, tuple):
                in_specs += [
                    pl.BlockSpec((ROWS, tile), lambda i, order, at=at: (order[at], i))
                    for at in x[1]
                ]
                group[i] = ([x[0]] * len(x[1]), g)
            else:
                in_specs += [pl.BlockSpec((v.shape[0], tile), lambda i, *_: (0, i)) for v in x]
            in_specs.append(whole(*g.shape))
            operands += [*group[i][0], g]
        width += group[0][1].shape[1]
    counts = tuple(tuple(len(x) for x, _ in group) for group in groups)
    return pl.pallas_call(
        functools.partial(wgrad_kernel, counts),
        grid_spec=pltpu.PrefetchScalarGridSpec(
            num_scalar_prefetch=1,
            grid=(D // tile,),
            in_specs=in_specs + [ANY] * len(behind),
            out_specs=pl.BlockSpec((tile, width), lambda i, *_: (i, 0)),
        ),
        out_shape=shape_of((D, width)),
        compiler_params=params(),
        cost_estimate=cost(
            2 * SEQ_LEN * D * width, 4 * MIB * len(groups) + 2 * width * (SEQ_LEN + D)
        ),
        name="wgrad_kernel",
    )(order, *operands, *behind)


WIDE_RATE = 2.0 * D ** (-0.5)
OUT_RATE = 2.0 * max(1, 16 * D // SEQ_LEN) ** (-0.5)
DOWN_RATE = 2.0 * FF ** (-0.5)


def adamw(ins, outs, gradient, rate, decay=DECAY, at=slice(None)):
    weight, first, second = (ref[at] for ref in ins)
    first_new = BETA_ONE * first + (1.0 - BETA_ONE) * gradient
    second_new = BETA_TWO * second + (1.0 - BETA_TWO) * gradient * gradient
    first_hat = first_new / (1.0 - BETA_ONE**STEP)
    second_hat = second_new / (1.0 - BETA_TWO**STEP)
    outs[0][at] = weight - rate * (first_hat / (jnp.sqrt(second_hat) + ADAM_EPS) + decay * weight)
    outs[1][at] = first_new
    outs[2][at] = second_new


def step_call(kernel, operands, states, extra):
    flat = [v for group in states for v in group]
    return pl.pallas_call(
        kernel,
        out_shape=[shape_of(v.shape, F32) for v in flat] + list(extra),
        compiler_params=params(),
        cost_estimate=cost(0, 8 * sum(v.size for v in flat)),
        name=kernel.__name__,
    )(*operands, *flat)


def wide_step_kernel(sums, kvg, *refs):
    ins, outs = refs[:9], refs[9:]
    gain = kvg[:, 129:130].astype(F32)
    for j in range(TILES):
        at = slice(128 * j, min(128 * (j + 1), HID))
        for s in range(3):
            start = 2 * PAD + 128 * j if s == 2 else 256 * j + 128 * s
            cols = slice(start, start + 128)
            g = sums[:, cols].astype(F32)
            if s < 2:
                g = g * gain
            adamw(
                ins[3 * s : 3 * s + 3],
                outs[3 * s : 3 * s + 3],
                g.T[: at.stop - at.start],
                DOWN_RATE if s == 2 else WIDE_RATE,
                at=at,
            )


def sum_blocks(parts):
    total = parts[:ROWS].astype(F32)
    for i in range(1, 16):
        total = total + parts[ROWS * i : ROWS * (i + 1)].astype(F32)
    return total


def query_step_kernel(parts, w, kvg, wide_sums, w_wide, *refs):
    ins, outs, tail = refs[:6], refs[6:12], refs[12]
    g = sum_blocks(parts)
    adamw(ins[3:], outs[3:], g[:, AW:].T, OUT_RATE)
    g = g[:, :AW]
    gain_one_sum = jnp.sum(g * w[:, :AW].astype(F32), axis=-1, keepdims=True)
    wide = wide_sums[:, : 2 * PAD].astype(F32) * w_wide[:, : 2 * PAD].astype(F32)
    gain_two_sum = jnp.sum(wide, axis=-1, keepdims=True)
    g = g * kvg[:, 128:129].astype(F32)
    adamw(ins[:3], outs[:3], g[:, :QW], WIDE_RATE)
    tail[:, :128] = g[:, QW:]
    lane = lax.broadcasted_iota(jnp.int32, (ROWS, 128), 1)
    tail[:, 128:] = jnp.where(lane == 0, gain_one_sum, gain_two_sum)


def last_step_kernel(parts, *refs):
    heads = [parts[2 * h] + parts[2 * h + 1] for h in range(KV_HEADS)]
    key = jnp.concatenate([v[:, :HD] for v in heads], axis=1)
    value = jnp.concatenate([v[:, HD : 2 * HD] for v in heads], axis=1)
    adamw(refs[0:3], refs[9:12], key, WIDE_RATE)
    adamw(refs[3:6], refs[12:15], value, WIDE_RATE)
    sums = functools.reduce(jnp.add, [v[:, 128:] for v in heads])
    sums = jnp.concatenate([sums, jnp.zeros((112, 128), F32)], axis=0).T[:2, :16]
    sums = sums / refs[6][...].astype(BF).astype(F32)
    adamw(refs[6:9], refs[15:18], sums, 0.3, 0.0)


def rotary():
    positions = jnp.arange(SEQ_LEN).astype(F32)
    frequency = 10000.0 ** (-2.0 * jnp.arange(HD // 2).astype(F32) / HD)
    angles = positions[:, None] * frequency[None, :]
    cos, sin = jnp.cos(angles), jnp.sin(angles)
    return (
        jnp.concatenate([cos] * 4, axis=1),
        jnp.concatenate([-sin, sin, -sin, sin], axis=1),
    )


def shards(
    tokens,
    cotangent,
    w_query,
    query_first,
    query_second,
    w_key,
    key_first,
    key_second,
    w_value,
    value_first,
    value_second,
    w_out,
    out_first,
    out_second,
    w_gate,
    gate_first,
    gate_second,
    w_up,
    up_first,
    up_second,
    w_down,
    down_first,
    down_second,
    norm_gains,
    gains_first,
    gains_second,
):
    z, core = lax.axis_index("z"), lax.axis_index("core")
    dp, ctx = ("y", "x"), ("z", "core")
    back = (z - jnp.arange(4)) % 4
    order = jnp.concatenate([2 * back + 1 - core, 2 * back + core]).astype(jnp.int32)
    where = jnp.concatenate([back, core[None], order[4:8], order[:4]]).astype(jnp.int32)
    back_where = jnp.concatenate([back, core[None], order[:8]]).astype(jnp.int32)

    small = small_call(w_key, w_value, norm_gains)
    kvg = swap_blocks(small, ctx)

    tcos, tsin = rotary()
    tokens_all = lax.all_gather(tokens[0], ctx, axis=0, tiled=True)
    grad_all = lax.all_gather(cotangent[0], ctx, axis=0, tiled=True)
    w_attend, copies, w_ffn = weights_call(kvg, w_query, w_out, w_gate.T, w_up.T, w_down)
    all_attend = swap_blocks(copies, dp)
    all_ffn = lax.all_gather(w_ffn, dp, axis=0, tiled=True)
    query, key_value, inv_all, attended, lse, *mixed_parts = front_call(
        order, tokens_all, all_attend, tcos, tsin
    )
    all_ffn = lax.all_gather(w_ffn, dp, axis=0, tiled=True)

    def reduce_core(partials):
        across = other_core(partials[0])
        at = [slice(k * ROWS, (k + 1) * ROWS) for k in range(4)]
        return [(across[a].astype(F32) + partials[1][a].astype(F32)).astype(BF) for a in at]

    def reduce_z(parts):
        return [parts[0]] + [ring("z", 4 - k)(parts[k]) for k in (1, 2, 3)]

    def total(parts):
        return functools.reduce(jnp.add, [t.astype(F32) for t in parts])

    mixed_parts = reduce_core(mixed_parts)
    middle = tokens[0].astype(F32) + total(reduce_z(mixed_parts))
    inv_second = lax.rsqrt(jnp.mean(middle * middle, axis=-1, keepdims=True) + EPS)
    unit_second = middle * inv_second

    mid_blocks = spread(unit_second.astype(BF))
    hidden0, hidden1, wide0, wide1, *wide_parts = middle_call(
        where, mid_blocks, grad_all, all_ffn
    )
    wide_parts = reduce_core(wide_parts)
    mid_parts = reduce_z(wide_parts)
    ffn_wgrad = wgrad_call(
        order,
        256,
        [(mid_blocks[:4], wide0), (mid_blocks[4:], wide1)],
        [((grad_all, range(4, 8)), hidden0), ((grad_all, range(4)), hidden1)],
        behind=wide_parts[:1],
    )
    down_sums = partial_call(order, (hidden1, hidden0), all_ffn, 2, 512, wide_parts[:1])
    middle_grad, middle_low, *down_sums = norm_back_call(
        mid_parts, middle, cotangent[0], (F32, BF), down_sums
    )
    ffn_sum = lax.psum_scatter(ffn_wgrad, dp, scatter_dimension=0, tiled=True)
    mid_grad_blocks = spread(middle_low)
    mid_grad_all, scaled_grad, *in_parts = back_call(
        back_where, mid_grad_blocks, (all_attend, query, key_value, lse, tcos, tsin, inv_all)
    )
    attend_wgrad = wgrad_call(
        order, 512, [([tokens_all], scaled_grad)], [([mid_grad_all], attended)]
    )
    in_parts = add_call(other_core(in_parts[0]), in_parts[1], (attend_wgrad,))
    attend_parts = swap_blocks(attend_wgrad, dp)
    in_parts = reduce_z(in_parts)
    (input_grad,) = norm_back_call(in_parts, tokens[0], middle_grad, (BF,))
    down_parts = add_call(other_core(down_sums[0]), down_sums[1], in_parts[1:2])
    output = middle + total(reduce_z(down_parts))

    wide_new = step_call(
        wide_step_kernel,
        (ffn_sum, kvg),
        (
            (w_gate.T, gate_first.T, gate_second.T),
            (w_up.T, up_first.T, up_second.T),
            (w_down, down_first, down_second),
        ),
        [],
    )
    wide_new = [v.T for v in wide_new[:6]] + list(wide_new[6:])
    *query_new, tail = step_call(
        query_step_kernel,
        (attend_parts, w_attend, kvg, ffn_sum, w_ffn),
        ((w_query, query_first, query_second), (w_out, out_first, out_second)),
        [shape_of((ROWS, 256), F32)],
    )
    tail = swap_blocks(tail, ctx).reshape(8, 16, 256)
    last_new = step_call(
        last_step_kernel,
        (tail,),
        (
            (w_key, key_first, key_second),
            (w_value, value_first, value_second),
            (norm_gains, gains_first, gains_second),
        ),
        [],
    )
    return (
        output.astype(BF)[None],
        input_grad[None],
        *query_new[:3],
        *last_new[:6],
        *query_new[3:],
        *wide_new,
        *last_new[6:],
    )


def solution(mesh):
    dp, ctx = ("y", "x"), ("z", "core")
    fine = Mesh(mesh.devices.reshape(4, 4, 4, 2), dp + ctx)
    act, col, row = P(dp, ctx, None), P(dp, ctx), P(ctx, dp)
    flat, gains = P(dp + ctx, None), P(None, dp + ctx)
    weights = (col,) * 3 + (flat,) * 6 + (row,) * 3 + (col,) * 6 + (row,) * 3 + (gains,) * 3
    return jax.shard_map(
        shards,
        mesh=fine,
        in_specs=(act, act) + weights,
        out_specs=(act, act) + weights,
        check_vma=False,
    )
```

```python
import functools

import jax
import jax.numpy as jnp
from jax import lax
from jax.experimental import pallas as pl
from jax.experimental.pallas import tpu as pltpu
from jax.sharding import Mesh
from jax.sharding import PartitionSpec as P

D = 2048
HEADS = 32
KV_HEADS = 4
HD = 64
FF = 5632
SEQ_LEN = 1024
STEP = 10

EPS = 1e-05
BETA_ONE = 0.9
BETA_TWO = 0.95
ADAM_EPS = 1e-08
DECAY = 0.1

ROWS = 128
HID = FF // 8
TILES = 6
PAD = TILES * 128
WIDE = 2 * HID
QW = 256
AW = 384
BF = jnp.bfloat16
F32 = jnp.float32
MIB = 2**20


def params(limit=56, **more):
    return pltpu.CompilerParams(vmem_limit_bytes=limit * MIB, **more)


def cost(flops, nbytes, trans=0):
    return pl.CostEstimate(flops=int(flops), bytes_accessed=int(nbytes), transcendentals=int(trans))


def dot(left, right):
    return jnp.dot(left, right, preferred_element_type=F32)


def dot_cols(left, right):
    return lax.dot_general(left, right, (((1,), (1,)), ((), ())), preferred_element_type=F32)


def dot_rows(left, right):
    return lax.dot_general(left, right, (((0,), (0,)), ((), ())), preferred_element_type=F32)


def swap_halves(v):
    width = v.shape[-1]
    lane = lax.broadcasted_iota(jnp.int32, v.shape, v.ndim - 1)
    return jnp.where(
        lane % HD < HD // 2,
        pltpu.roll(v, width - HD // 2, v.ndim - 1),
        pltpu.roll(v, HD // 2, v.ndim - 1),
    )


def ring(axis, k):
    return functools.partial(
        lax.ppermute, axis_name=axis, perm=[(i, (i + k) % 4) for i in range(4)]
    )


def other_core(v):
    return lax.ppermute(v, "core", [(0, 1), (1, 0)])


def spread_z(v):
    return [v, ring("z", 1)(v), ring("z", 2)(v), ring("z", 3)(v)]


def spread(v):
    own = spread_z(v)
    return own + [other_core(t) for t in own]


def swap_blocks(v, axes):
    return lax.all_to_all(v, axes, split_axis=0, concat_axis=0, tiled=True)


ANY = pl.BlockSpec(memory_space=pltpu.HBM)
HELD = [pltpu.VMEM((4, 2 * ROWS, D), BF), pltpu.SemaphoreType.DMA((8,))]


def block_copy(halves, blocks, held, sems, k, half, source=None):
    source = blocks[4 * half + k] if source is None else source
    rows = pl.ds(pl.multiple_of(halves[half] * ROWS, ROWS), ROWS)
    return pltpu.make_async_copy(source, held.at[k, rows], sems.at[4 * half + k])


def start_blocks(halves, blocks, held, sems, at):
    for k in at:
        for half in range(2):
            block_copy(halves, blocks, held, sems, k, half).start()


def wait_blocks(halves, blocks, held, sems):
    step = pl.program_id(0)
    for half in range(2):
        block_copy(halves, blocks, held, sems, step, half, blocks[0]).wait()
    return held.at[step]


def load_blocks(halves, blocks, held, sems):
    @pl.when(pl.program_id(0) == 0)
    def _():
        start_blocks(halves, blocks, held, sems, range(4))

    return wait_blocks(halves, blocks, held, sems)


def by_block(width):
    return pl.BlockSpec((2 * ROWS, width), lambda i, where: (where[i], 0))


def by_step(width):
    return pl.BlockSpec((ROWS, width), lambda i, *_: (i, 0))


def whole(*shape):
    return pl.BlockSpec(shape, lambda i, *_: (0,) * len(shape))


def shape_of(shape, kind=BF):
    return jax.ShapeDtypeStruct(shape, kind)


def blocks_call(
    kernel, where, blocks, operands, in_specs, out_specs, outs, flops, behind=(), through=(), scratch=None
):
    n_in, n_out, n_more = 8 + len(operands), len(outs), len(behind) + len(through)

    def body(where, *refs):
        refs = list(refs)
        del refs[n_in + n_more + n_out : n_in + n_more + n_out + len(through)]
        del refs[n_in : n_in + n_more]
        kernel(where, *refs)

    nbytes = 4 * MIB + sum(o.size * o.dtype.itemsize for o in outs)
    nbytes += sum(o.size * o.dtype.itemsize for o in operands)
    first = 1 + n_in + len(behind)
    return pl.pallas_call(
        body,
        grid_spec=pltpu.PrefetchScalarGridSpec(
            num_scalar_prefetch=1,
            grid=(4,),
            in_specs=[ANY] * 8 + in_specs + [ANY] * n_more,
            out_specs=out_specs + [ANY] * len(through),
            scratch_shapes=scratch or HELD,
        ),
        out_shape=outs + [shape_of(v.shape, v.dtype) for v in through],
        input_output_aliases={first + i: n_out + i for i in range(len(through))},
        compiler_params=params(),
        cost_estimate=cost(flops, nbytes),
        name=kernel.__name__,
    )(where, *blocks, *operands, *behind, *through)


def small_kernel(key, value, gains, out):
    cols = gains[...].astype(BF).astype(F32)
    cols = jnp.concatenate([cols, jnp.zeros((6, 16), F32)], axis=0)
    cols = jnp.concatenate([cols, jnp.zeros((8, 112), F32)], axis=1)
    cols = jnp.concatenate([cols, jnp.zeros((120, 128), F32)], axis=0).T[:16].astype(BF)
    for h in range(KV_HEADS):
        at = slice(HD * h, HD * (h + 1))
        block = jnp.concatenate([key[:, at].astype(BF), value[:, at].astype(BF), cols], axis=1)
        out[32 * h : 32 * h + 16] = block
        out[32 * h + 16 : 32 * h + 32] = block


def small_call(key, value, gains):
    return pl.pallas_call(
        small_kernel,
        out_shape=shape_of((ROWS, 256)),
        compiler_params=params(),
        cost_estimate=cost(0, 1 << 17),
        name="small_kernel",
    )(key, value, gains)


def weights_kernel(kvg, query, mixed, gate, up, down, attend_out, copies, ffn_out):
    gain = kvg[:, 128:129].astype(F32)
    attend_out[:, :QW] = (query[...].astype(BF).astype(F32) * gain).astype(BF)
    attend_out[:, QW:AW] = (kvg[:, :128].astype(F32) * gain).astype(BF)
    attend_out[:, AW:] = mixed[...].T.astype(BF)
    for i in range(16):
        copies[ROWS * i : ROWS * (i + 1)] = attend_out[...]
    gain = kvg[:, 129:130].astype(F32)
    for j in range(TILES):
        rows = slice(128 * j, min(128 * (j + 1), HID))
        parts = [ref[rows] for ref in (gate, up)]
        if j == TILES - 1:
            parts = [jnp.concatenate(parts, axis=0)]
        for s, part in enumerate(parts):
            at = PAD + 256 * j + 128 * s
            part = part.T.astype(BF).astype(F32) * gain
            ffn_out[:, at : at + 128] = part.astype(BF)
        part = down[rows]
        if j == TILES - 1:
            part = jnp.concatenate([part, jnp.zeros((PAD - HID, 128), F32)], axis=0)
        ffn_out[:, 128 * j : 128 * (j + 1)] = part.T.astype(BF)


def weights_call(*operands):
    return pl.pallas_call(
        weights_kernel,
        out_shape=[
            shape_of((ROWS, AW + QW)),
            shape_of((D, AW + QW)),
            shape_of((ROWS, PAD + WIDE)),
        ],
        compiler_params=params(),
        cost_estimate=cost(0, 5 * MIB),
        name="weights_kernel",
    )(*operands)


def norm_back_kernel(n_through, *refs):
    parts, (x, base), outs = refs[:4], refs[4:6], refs[6 + n_through : len(refs) - n_through]
    v = x[...].astype(F32)
    inv = lax.rsqrt(jnp.mean(v * v, axis=-1, keepdims=True) + EPS)
    unit = v * inv
    u = functools.reduce(jnp.add, [ref[...].astype(F32) for ref in parts])
    out = base[...].astype(F32) + inv * (u - unit * jnp.mean(u * unit, axis=-1, keepdims=True))
    for ref in outs:
        ref[...] = out.astype(ref.dtype)


def norm_back_call(parts, x, base, kinds, through=()):
    rows = pl.BlockSpec((ROWS // 2, D), lambda i: (i, 0))
    return pl.pallas_call(
        functools.partial(norm_back_kernel, len(through)),
        grid=(2,),
        in_specs=[rows] * 6 + [ANY] * len(through),
        out_specs=[rows] * len(kinds) + [ANY] * len(through),
        out_shape=[shape_of((ROWS, D), kind) for kind in kinds]
        + [shape_of(v.shape, v.dtype) for v in through],
        input_output_aliases={6 + i: len(kinds) + i for i in range(len(through))},
        compiler_params=params(),
        cost_estimate=cost(0, 5 * MIB),
        name="norm_back_kernel",
    )(*parts, x, base, *through)


def send_products(left, w, start, end, held, sems, outs):
    copies = []
    half = left.shape[0] // 2
    for t in range(4):
        held[t] = dot_cols(left, w[512 * t : 512 * (t + 1), start:end]).astype(BF)
        for i, out in enumerate(outs):
            copy = pltpu.make_async_copy(
                held.at[t, pl.ds(i * half, half)], out.at[:, pl.ds(512 * t, 512)], sems.at[i, t]
            )
            copy.start()
            copies.append(copy)
    for copy in copies:
        copy.wait()


def pick_rows(ref, order):
    return jnp.concatenate(
        [ref[pl.ds(pl.multiple_of(order[k] * ROWS, ROWS), ROWS)] for k in range(8)], axis=0
    )


SENT = [pltpu.VMEM((4, SEQ_LEN, 512), BF), pltpu.SemaphoreType.DMA((2, 4))]


def front_kernel(order, rows, *refs):
    w, tcos, tsin, q_out, kv_out, inv_out, out, lse, *outs, held, sems = refs
    step = pl.program_id(0)
    at = pl.ds(pl.multiple_of(step * 2 * ROWS, 2 * ROWS), 2 * ROWS)

    y = dot(rows[...], w[:, :AW])
    x = rows[...].astype(F32)
    inv = lax.rsqrt(jnp.mean(x * x, axis=-1, keepdims=True) + EPS)
    inv_out[at] = jnp.broadcast_to(inv, (2 * ROWS, 128))
    cos, sin = tcos[...] * inv, tsin[...] * inv
    for j in range(2):
        part = y[:, j * 128 : (j + 1) * 128]
        q_out[at, j * 128 : (j + 1) * 128] = (part * cos + swap_halves(part) * sin).astype(BF)
    part = y[:, 256:384]
    is_key = lax.broadcasted_iota(jnp.int32, part.shape, 1) < HD
    kv_out[at] = jnp.where(is_key, part * cos + swap_halves(part) * sin, part * inv).astype(BF)

    @pl.when(step == 3)
    def _():
        attend_kernel(q_out, kv_out, out, lse)
        send_products(pick_rows(out, order), w, AW, AW + QW, held, sems, outs)


def front_call(order, rows, w, tcos, tsin):
    def block(width):
        return pl.BlockSpec((2 * ROWS, width), lambda i, *_: (i, 0))

    shapes = [(QW, BF), (128, BF), (128, F32), (QW, BF), (128, F32)]
    return pl.pallas_call(
        front_kernel,
        grid_spec=pltpu.PrefetchScalarGridSpec(
            num_scalar_prefetch=1,
            grid=(4,),
            in_specs=[block(D), whole(D, AW + QW)] + [block(128)] * 2,
            out_specs=[whole(SEQ_LEN, w) for w, _ in shapes] + [ANY] * 2,
            scratch_shapes=SENT,
        ),
        out_shape=[shape_of((SEQ_LEN, w), t) for w, t in shapes] + [shape_of((4 * ROWS, D))] * 2,
        compiler_params=params(),
        cost_estimate=cost(8e9, 16 * MIB, 2 * MIB),
        name="front_kernel",
    )(order, rows, w, tcos, tsin)


def put_halves(outs, value, cols=slice(None)):
    outs[0][:, cols] = value[:ROWS]
    outs[1][:, cols] = value[ROWS:]


def middle_kernel(where, *refs):
    blocks, grad_all, w, refs = refs[:8], refs[8], refs[9], refs[10:]
    hiddens, grads, outs = refs[:2], refs[2:4], refs[4:6]
    held, sems, grad_held, grad_sems, wide, down, w_sems, both, sent, sent_sems = refs[6:]
    step = pl.program_id(0)
    first = step == 0
    grad_blocks = [
        grad_all.at[pl.ds(pl.multiple_of(where[5 + i] * ROWS, ROWS), ROWS)] for i in range(8)
    ]
    loads = ((0, 1), blocks, held, sems), ((0, 1), grad_blocks, grad_held, grad_sems)

    def w_copies(j):
        n = min(512, WIDE - 512 * j)
        return (
            pltpu.make_async_copy(
                w.at[:, pl.ds(PAD + 512 * j, n)], wide.at[j, :, pl.ds(0, n)], w_sems.at[0, j]
            ),
            pltpu.make_async_copy(w.at[:, pl.ds(256 * j, 256)], down.at[j], w_sems.at[1, j]),
        )

    @pl.when(first)
    def _():
        for j in range(4):
            for load in loads:
                start_blocks(*load, (j,))
            if j < TILES // 2:
                for copy in w_copies(j):
                    copy.start()

    x, c = (wait_blocks(*load) for load in loads)
    for j in range(TILES // 2):

        @pl.when(first)
        def _():
            for copy in w_copies(j):
                copy.wait()

        backs = dot(c[...], down[j])
        for i in range(2):
            t = 2 * j + i
            last = t == TILES - 1
            n = 128 if last else 256
            y = dot(x[...], wide[j, :, 256 * i : 256 * i + n])
            gate, up = y[:, :128], pltpu.roll(y, HD, 1) if last else y[:, 128:]
            back = backs[:, 128 * i : 128 * (i + 1)]
            sigma = jax.nn.sigmoid(gate)
            swish = gate * sigma
            hidden = swish * up
            g = back * up * (sigma * (1.0 + gate * (1.0 - sigma)))
            u = back * swish
            if last:
                valid = lax.broadcasted_iota(jnp.int32, g.shape, 1) < HD
                hidden = jnp.where(valid, hidden, 0.0)
                g = jnp.where(valid, g, pltpu.roll(u, HD, 1)).astype(BF)
            else:
                g = jnp.concatenate([g.astype(BF), u.astype(BF)], axis=1)
            put_halves(hiddens, hidden.astype(BF), slice(128 * t, 128 * (t + 1)))
            cols = slice(256 * t, 256 * t + n)
            put_halves(grads, g, cols)
            both[step, :, cols] = g[ROWS:]
            both[4 + step, :, cols] = g[:ROWS]

    @pl.when(step == 3)
    def _():
        left = both[...].reshape(SEQ_LEN, WIDE)
        copies = []
        for t in range(4):
            at = slice(512 * t, 512 * (t + 1))
            y = 0.0
            for j in range(TILES // 2):
                n = min(512, WIDE - 512 * j)
                y = y + dot_cols(left[:, 512 * j : 512 * j + n], wide[j, at, :n])
            sent[t] = y.astype(BF)
            for i, out in enumerate(outs):
                copy = pltpu.make_async_copy(
                    sent.at[t, pl.ds(i * 4 * ROWS, 4 * ROWS)],
                    out.at[:, pl.ds(512 * t, 512)],
                    sent_sems.at[i, t],
                )
                copy.start()
                copies.append(copy)
        for copy in copies:
            copy.wait()


def middle_call(where, blocks, grad_all, w):
    return blocks_call(
        middle_kernel,
        where,
        blocks,
        (grad_all, w),
        [ANY] * 2,
        [by_step(PAD)] * 2 + [by_step(WIDE)] * 2 + [ANY] * 2,
        [shape_of((4 * ROWS, PAD))] * 2
        + [shape_of((4 * ROWS, WIDE))] * 2
        + [shape_of((4 * ROWS, D))] * 2,
        2 * SEQ_LEN * D * 5 * PAD,
        scratch=HELD * 2
        + [
            pltpu.VMEM((TILES // 2, D, 512), BF),
            pltpu.VMEM((TILES // 2, D, 256), BF),
            pltpu.SemaphoreType.DMA((2, TILES // 2)),
            pltpu.VMEM((8, ROWS, WIDE), BF),
        ]
        + SENT,
    )


def partial_kernel(n_in, n_behind, n_through, order, *refs):
    w, (across, own) = refs[n_in], refs[n_in + 1 + n_behind + n_through :][:2]
    if n_in == 1:
        a = refs[0]
        left = jnp.concatenate(
            [a[pl.ds(pl.multiple_of(order[k] * ROWS, ROWS), ROWS)] for k in range(8)], axis=0
        )
    else:
        left = jnp.concatenate([refs[0][...], refs[1][...]], axis=0)
    y = dot_cols(left, w[...]).astype(BF)
    across[...] = y[: 4 * ROWS]
    own[...] = y[4 * ROWS :]


def partial_call(order, a, w, col, tile, behind=(), through=()):
    depth, first = a[0].shape[1], 2 + len(a) + len(behind)
    return pl.pallas_call(
        functools.partial(partial_kernel, len(a), len(behind), len(through)),
        grid_spec=pltpu.PrefetchScalarGridSpec(
            num_scalar_prefetch=1,
            grid=(D // tile,),
            in_specs=[whole(*v.shape) for v in a]
            + [pl.BlockSpec((tile, depth), lambda i, *_: (i, col))]
            + [ANY] * (len(behind) + len(through)),
            out_specs=[pl.BlockSpec((4 * ROWS, tile), lambda i, *_: (0, i))] * 2
            + [ANY] * len(through),
        ),
        out_shape=[shape_of((4 * ROWS, D))] * 2 + [shape_of(v.shape, v.dtype) for v in through],
        input_output_aliases={first + i: 2 + i for i in range(len(through))},
        compiler_params=params(),
        cost_estimate=cost(2 * 8 * ROWS * D * depth, 2 * depth * (D + 1024) + 4 * MIB),
        name="partial_kernel",
    )(order, *a, w, *behind, *through)


def add_kernel(n_behind, across, own, *refs):
    n = own.shape[0] // ROWS
    outs, (held, sems) = refs[n_behind : n_behind + n], refs[n_behind + n :]
    loads, stores = [], []
    for k in range(n):
        rows = pl.ds(k * ROWS, ROWS)
        loads.append(
            [
                pltpu.make_async_copy(ref.at[rows], held.at[i, k], sems.at[i, k])
                for i, ref in enumerate((across, own))
            ]
        )
        stores.append(pltpu.make_async_copy(held.at[2, k], outs[k], sems.at[2, k]))
    for pair in loads:
        for copy in pair:
            copy.start()
    for k in range(n):
        for copy in loads[k]:
            copy.wait()
        held[2, k] = (held[0, k].astype(F32) + held[1, k].astype(F32)).astype(BF)
        stores[k].start()
    for copy in stores:
        copy.wait()


def add_call(across, own, behind=()):
    n = own.shape[0] // ROWS
    return pl.pallas_call(
        functools.partial(add_kernel, len(behind)),
        in_specs=[ANY] * (2 + len(behind)),
        out_specs=[ANY] * n,
        out_shape=[shape_of((ROWS, D))] * n,
        scratch_shapes=[pltpu.VMEM((3, n, ROWS, D), BF), pltpu.SemaphoreType.DMA((3, n))],
        compiler_params=params(),
        cost_estimate=cost(0, 6 * own.size),
        name="add_kernel",
    )(across, own, *behind)


def scores_of(q, k, diagonal):
    s = dot_cols(q, k)
    if diagonal:
        row = lax.broadcasted_iota(jnp.int32, s.shape, 0) % ROWS
        s = jnp.where(row >= lax.broadcasted_iota(jnp.int32, s.shape, 1), s, -1e30)
    return s


def stack_heads(v):
    return jnp.concatenate([v[:, HD * h : HD * (h + 1)] for h in range(4)], axis=0)


def lay_heads(v):
    return jnp.concatenate([v[ROWS * h : ROWS * (h + 1)] for h in range(4)], axis=1)


def attend_kernel(q, kv, out, lse):
    key, value = kv[:, :HD], kv[:, HD:]
    lane = lax.broadcasted_iota(jnp.int32, (ROWS, 128), 1)
    for b in range(8):
        rows = slice(b * ROWS, (b + 1) * ROWS)
        mine = stack_heads(q[rows] * HD**-0.5)
        pieces = [(scores_of(mine, key[rows], True), value[rows])]
        if b:
            pieces.append((scores_of(mine, key[: b * ROWS], False), value[: b * ROWS]))
        top = functools.reduce(
            jnp.maximum, [jnp.max(s, axis=-1, keepdims=True) for s, _ in pieces]
        )
        total, mixed = 0.0, 0.0
        for s, v in pieces:
            p = jnp.exp(s - top)
            total = total + jnp.sum(p, axis=-1, keepdims=True)
            mixed = mixed + dot(p.astype(BF), v)
        out[rows] = lay_heads(mixed / total).astype(BF)
        log_total = top + jnp.log(total)
        spread_out = jnp.zeros((ROWS, 128), F32)
        for h in range(4):
            spread_out = jnp.where(lane == h, log_total[ROWS * h : ROWS * (h + 1)], spread_out)
        lse[rows] = spread_out


def attend_back_kernel(
    q, kv, lse, mixed_grad, tcos, tsin, inv, grad_out, scaled_out, held
):
    key, value = kv[:, :HD], kv[:, HD:]
    held[...] = jnp.zeros_like(held)

    def put(rows, cols, part, turn):
        part = jnp.where(turn, part * tcos[rows] - swap_halves(part) * tsin[rows], part)
        grad_out[rows, cols] = part.astype(BF)
        scaled_out[rows, cols] = (part * inv[rows]).astype(BF)

    for b in range(8):
        rows = slice(b * ROWS, (b + 1) * ROWS)
        mine = stack_heads(q[rows] * HD**-0.5)
        grad = stack_heads(mixed_grad[rows])
        log_total = jnp.concatenate([lse[rows, h : h + 1] for h in range(4)], axis=0)
        pieces = [(rows, True)] + ([(slice(0, b * ROWS), False)] if b else [])
        probs, back = [], []
        inner = 0.0
        for cols, diagonal in pieces:
            p = jnp.exp(scores_of(mine, key[cols], diagonal) - log_total)
            g = dot_cols(grad, value[cols])
            inner = inner + jnp.sum(p * g, axis=-1, keepdims=True)
            probs.append(p)
            back.append(g)
        total = 0.0
        for (cols, _), p, g in zip(pieces, probs, back):
            s_grad = (p * (g - inner)).astype(BF)
            total = total + dot(s_grad, key[cols])
            held[:HD, cols] += dot_rows(mine, s_grad)
            held[HD:, cols] += dot_rows(grad, p.astype(BF))
        wide = lay_heads(total * HD**-0.5)
        for j in range(2):
            put(rows, slice(128 * j, 128 * (j + 1)), wide[:, 128 * j : 128 * (j + 1)], True)
    is_key = lax.broadcasted_iota(jnp.int32, (ROWS, 128), 1) < HD
    for b in range(8):
        rows = slice(b * ROWS, (b + 1) * ROWS)
        put(rows, slice(QW, AW), held[:, rows].T, is_key)


def back_kernel(where, *refs):
    blocks, refs = refs[:8], refs[8:]
    w, q, kv, lse, tcos, tsin, inv, attended, rows, scaled, *outs, wgrad_out = refs[:13]
    held, sems, mixed_grad, grad, kv_held, rows_held, rows_sem, wgrad, wgrad_sems = refs[13:22]
    sent, sent_sems = refs[22:]
    step = pl.program_id(0)
    rows_copy = pltpu.make_async_copy(rows, rows_held, rows_sem)
    x = load_blocks((where[4], 1 - where[4]), blocks, held, sems)

    @pl.when(step == 0)
    def _():
        rows_copy.start()

    def place(k):
        return pl.ds(pl.multiple_of(where[k] * 2 * ROWS, 2 * ROWS), 2 * ROWS)

    mixed_grad[place(step)] = dot(x[...], w[:, AW:]).astype(BF)

    @pl.when(step == 3)
    def _():
        attend_back_kernel(q, kv, lse, mixed_grad, tcos, tsin, inv, grad, scaled, kv_held)
        rows_copy.wait()
        copies = []
        for t in range(4):
            cols = slice(512 * t, 512 * (t + 1))
            wgrad[t, :, :AW] = dot_rows(rows_held[:, cols], scaled[...]).astype(BF)
            y = 0.0
            for k in range(4):
                y = y + dot_rows(held[k, :, cols], attended[place(k)])
            wgrad[t, :, AW:] = y.astype(BF)
            copy = pltpu.make_async_copy(
                wgrad.at[t], wgrad_out.at[pl.ds(512 * t, 512)], wgrad_sems.at[t]
            )
            copy.start()
            copies.append(copy)
        left = pick_rows(grad, [where[5 + k] for k in range(8)])
        send_products(left, w, 0, AW, sent, sent_sems, outs)
        for copy in copies:
            copy.wait()


BACK_COST = 1.43e11


def back_call(where, blocks, operands, rows):
    widths = [QW, 128, 128, 128, 128, 128, QW]
    return blocks_call(
        back_kernel,
        where,
        blocks,
        (*operands, rows),
        [whole(D, AW + QW)] + [whole(SEQ_LEN, w) for w in widths] + [ANY],
        [whole(SEQ_LEN, AW)] + [ANY] * 3,
        [shape_of((SEQ_LEN, AW))] + [shape_of((4 * ROWS, D))] * 2 + [shape_of((D, AW + QW))],
        BACK_COST,
        scratch=HELD
        + [
            pltpu.VMEM((SEQ_LEN, QW), BF),
            pltpu.VMEM((SEQ_LEN, AW), BF),
            pltpu.VMEM((128, SEQ_LEN), F32),
            pltpu.VMEM((SEQ_LEN, D), BF),
            pltpu.SemaphoreType.DMA(()),
            pltpu.VMEM((4, 512, AW + QW), BF),
            pltpu.SemaphoreType.DMA((4,)),
        ]
        + SENT,
    )


def wgrad_kernel(counts, order, *refs):
    out = refs[-1]
    at, ref = 0, 0
    for group in counts:
        total = 0.0
        for n in group:
            x = refs[ref : ref + n]
            x = x[0][...] if n == 1 else jnp.concatenate([v[...] for v in x], axis=0)
            total = total + dot_rows(x, refs[ref + n][...])
            ref += n + 1
        out[:, at : at + total.shape[1]] = total.astype(BF)
        at += total.shape[1]


def wgrad_call(order, tile, *groups, behind=()):
    in_specs, operands, width = [], [], 0
    for group in groups:
        for i, (x, g) in enumerate(group):
            if isinstance(x, tuple):
                in_specs += [
                    pl.BlockSpec((ROWS, tile), lambda i, order, at=at: (order[at], i))
                    for at in x[1]
                ]
                group[i] = ([x[0]] * len(x[1]), g)
            else:
                in_specs += [pl.BlockSpec((v.shape[0], tile), lambda i, *_: (0, i)) for v in x]
            in_specs.append(whole(*g.shape))
            operands += [*group[i][0], g]
        width += group[0][1].shape[1]
    counts = tuple(tuple(len(x) for x, _ in group) for group in groups)
    return pl.pallas_call(
        functools.partial(wgrad_kernel, counts),
        grid_spec=pltpu.PrefetchScalarGridSpec(
            num_scalar_prefetch=1,
            grid=(D // tile,),
            in_specs=in_specs + [ANY] * len(behind),
            out_specs=pl.BlockSpec((tile, width), lambda i, *_: (i, 0)),
        ),
        out_shape=shape_of((D, width)),
        compiler_params=params(),
        cost_estimate=cost(
            2 * SEQ_LEN * D * width, 4 * MIB * len(groups) + 2 * width * (SEQ_LEN + D)
        ),
        name="wgrad_kernel",
    )(order, *operands, *behind)


WIDE_RATE = 2.0 * D ** (-0.5)
OUT_RATE = 2.0 * max(1, 16 * D // SEQ_LEN) ** (-0.5)
DOWN_RATE = 2.0 * FF ** (-0.5)


def adamw(ins, outs, gradient, rate, decay=DECAY, at=slice(None)):
    weight, first, second = (ref[at] for ref in ins)
    first_new = BETA_ONE * first + (1.0 - BETA_ONE) * gradient
    second_new = BETA_TWO * second + (1.0 - BETA_TWO) * gradient * gradient
    first_hat = first_new / (1.0 - BETA_ONE**STEP)
    second_hat = second_new / (1.0 - BETA_TWO**STEP)
    outs[0][at] = weight - rate * (first_hat / (jnp.sqrt(second_hat) + ADAM_EPS) + decay * weight)
    outs[1][at] = first_new
    outs[2][at] = second_new


def step_call(kernel, operands, states, extra):
    flat = [v for group in states for v in group]
    return pl.pallas_call(
        kernel,
        out_shape=[shape_of(v.shape, F32) for v in flat] + list(extra),
        compiler_params=params(),
        cost_estimate=cost(0, 8 * sum(v.size for v in flat)),
        name=kernel.__name__,
    )(*operands, *flat)


def wide_step_kernel(sums, kvg, *refs):
    ins, outs = refs[:9], refs[9:]
    gain = kvg[:, 129:130].astype(F32)
    for j in range(TILES):
        at = slice(128 * j, min(128 * (j + 1), HID))
        n = at.stop - at.start
        g = [sums[:, PAD + 256 * j : PAD + 256 * j + 128].astype(F32) * gain]
        if j < TILES - 1:
            g.append(sums[:, PAD + 256 * j + 128 : PAD + 256 * (j + 1)].astype(F32) * gain)
        g = [v.T for v in g]
        if j == TILES - 1:
            g = [g[0][:n], g[0][n:]]
        g.append(sums[:, 128 * j : 128 * (j + 1)].astype(F32).T[:n])
        for s, rate in enumerate((WIDE_RATE, WIDE_RATE, DOWN_RATE)):
            adamw(ins[3 * s : 3 * s + 3], outs[3 * s : 3 * s + 3], g[s], rate, at=at)


def sum_blocks(parts):
    total = parts[:ROWS].astype(F32)
    for i in range(1, 16):
        total = total + parts[ROWS * i : ROWS * (i + 1)].astype(F32)
    return total


def query_step_kernel(parts, w, kvg, wide_sums, w_wide, *refs):
    ins, outs, tail = refs[:6], refs[6:12], refs[12]
    g = sum_blocks(parts)
    adamw(ins[3:], outs[3:], g[:, AW:].T, OUT_RATE)
    g = g[:, :AW]
    gain_one_sum = jnp.sum(g * w[:, :AW].astype(F32), axis=-1, keepdims=True)
    wide = wide_sums[:, PAD:].astype(F32) * w_wide[:, PAD:].astype(F32)
    gain_two_sum = jnp.sum(wide, axis=-1, keepdims=True)
    g = g * kvg[:, 128:129].astype(F32)
    adamw(ins[:3], outs[:3], g[:, :QW], WIDE_RATE)
    tail[:, :128] = g[:, QW:]
    lane = lax.broadcasted_iota(jnp.int32, (ROWS, 128), 1)
    tail[:, 128:] = jnp.where(lane == 0, gain_one_sum, gain_two_sum)


def last_step_kernel(parts, *refs):
    heads = [parts[2 * h] + parts[2 * h + 1] for h in range(KV_HEADS)]
    key = jnp.concatenate([v[:, :HD] for v in heads], axis=1)
    value = jnp.concatenate([v[:, HD : 2 * HD] for v in heads], axis=1)
    adamw(refs[0:3], refs[9:12], key, WIDE_RATE)
    adamw(refs[3:6], refs[12:15], value, WIDE_RATE)
    sums = functools.reduce(jnp.add, [v[:, 128:] for v in heads])
    sums = jnp.concatenate([sums, jnp.zeros((112, 128), F32)], axis=0).T[:2, :16]
    sums = sums / refs[6][...].astype(BF).astype(F32)
    adamw(refs[6:9], refs[15:18], sums, 0.3, 0.0)


def rotary():
    positions = jnp.arange(SEQ_LEN).astype(F32)
    frequency = 10000.0 ** (-2.0 * jnp.arange(HD // 2).astype(F32) / HD)
    angles = positions[:, None] * frequency[None, :]
    cos, sin = jnp.cos(angles), jnp.sin(angles)
    return (
        jnp.concatenate([cos] * 4, axis=1),
        jnp.concatenate([-sin, sin, -sin, sin], axis=1),
    )


def shards(
    tokens,
    cotangent,
    w_query,
    query_first,
    query_second,
    w_key,
    key_first,
    key_second,
    w_value,
    value_first,
    value_second,
    w_out,
    out_first,
    out_second,
    w_gate,
    gate_first,
    gate_second,
    w_up,
    up_first,
    up_second,
    w_down,
    down_first,
    down_second,
    norm_gains,
    gains_first,
    gains_second,
):
    z, core = lax.axis_index("z"), lax.axis_index("core")
    dp, ctx = ("y", "x"), ("z", "core")
    back = (z - jnp.arange(4)) % 4
    order = jnp.concatenate([2 * back + 1 - core, 2 * back + core]).astype(jnp.int32)
    where = jnp.concatenate([back, core[None], order[4:8], order[:4]]).astype(jnp.int32)
    back_where = jnp.concatenate([back, core[None], order[:8]]).astype(jnp.int32)

    small = small_call(w_key, w_value, norm_gains)
    kvg = swap_blocks(small, ctx)

    tcos, tsin = rotary()
    tokens_all = lax.all_gather(tokens[0], ctx, axis=0, tiled=True)
    grad_all = lax.all_gather(cotangent[0], ctx, axis=0, tiled=True)
    w_attend, copies, w_ffn = weights_call(kvg, w_query, w_out, w_gate.T, w_up.T, w_down)
    all_attend = swap_blocks(copies, dp)
    all_ffn = lax.all_gather(w_ffn, dp, axis=0, tiled=True)
    query, key_value, inv_all, attended, lse, *mixed_parts = front_call(
        order, tokens_all, all_attend, tcos, tsin
    )
    all_ffn = lax.all_gather(w_ffn, dp, axis=0, tiled=True)

    def reduce_core(partials):
        across = other_core(partials[0])
        at = [slice(k * ROWS, (k + 1) * ROWS) for k in range(4)]
        return [(across[a].astype(F32) + partials[1][a].astype(F32)).astype(BF) for a in at]

    def reduce_z(parts):
        return [parts[0]] + [ring("z", 4 - k)(parts[k]) for k in (1, 2, 3)]

    def total(parts):
        return functools.reduce(jnp.add, [t.astype(F32) for t in parts])

    mixed_parts = reduce_core(mixed_parts)
    middle = tokens[0].astype(F32) + total(reduce_z(mixed_parts))
    inv_second = lax.rsqrt(jnp.mean(middle * middle, axis=-1, keepdims=True) + EPS)
    unit_second = middle * inv_second

    mid_blocks = spread(unit_second.astype(BF))
    hidden0, hidden1, wide0, wide1, *wide_parts = middle_call(
        where, mid_blocks, grad_all, all_ffn
    )
    wide_parts = reduce_core(wide_parts)
    mid_parts = reduce_z(wide_parts)
    ffn_wgrad = wgrad_call(
        order,
        256,
        [((grad_all, range(4, 8)), hidden0), ((grad_all, range(4)), hidden1)],
        [(mid_blocks[:4], wide0), (mid_blocks[4:], wide1)],
        behind=wide_parts[:1],
    )
    down_sums = partial_call(order, (hidden1, hidden0), all_ffn, 0, 512, wide_parts[:1])
    middle_grad, middle_low, *down_sums = norm_back_call(
        mid_parts, middle, cotangent[0], (F32, BF), down_sums
    )
    ffn_sum = lax.psum_scatter(ffn_wgrad, dp, scatter_dimension=0, tiled=True)
    mid_grad_blocks = spread(middle_low)
    _, *in_parts, attend_wgrad = back_call(
        back_where,
        mid_grad_blocks,
        (all_attend, query, key_value, lse, tcos, tsin, inv_all, attended),
        tokens_all,
    )
    attend_parts = swap_blocks(attend_wgrad, dp)
    in_parts = add_call(other_core(in_parts[0]), in_parts[1])
    in_parts = reduce_z(in_parts)
    (input_grad,) = norm_back_call(in_parts, tokens[0], middle_grad, (BF,))
    down_parts = add_call(other_core(down_sums[0]), down_sums[1], in_parts[1:2])
    output = middle + total(reduce_z(down_parts))

    wide_new = step_call(
        wide_step_kernel,
        (ffn_sum, kvg),
        (
            (w_gate.T, gate_first.T, gate_second.T),
            (w_up.T, up_first.T, up_second.T),
            (w_down, down_first, down_second),
        ),
        [],
    )
    wide_new = [v.T for v in wide_new[:6]] + list(wide_new[6:])
    *query_new, tail = step_call(
        query_step_kernel,
        (attend_parts, w_attend, kvg, ffn_sum, w_ffn),
        ((w_query, query_first, query_second), (w_out, out_first, out_second)),
        [shape_of((ROWS, 256), F32)],
    )
    tail = swap_blocks(tail, ctx).reshape(8, 16, 256)
    last_new = step_call(
        last_step_kernel,
        (tail,),
        (
            (w_key, key_first, key_second),
            (w_value, value_first, value_second),
            (norm_gains, gains_first, gains_second),
        ),
        [],
    )
    return (
        output.astype(BF)[None],
        input_grad[None],
        *query_new[:3],
        *last_new[:6],
        *query_new[3:],
        *wide_new,
        *last_new[6:],
    )


def solution(mesh):
    dp, ctx = ("y", "x"), ("z", "core")
    fine = Mesh(mesh.devices.reshape(4, 4, 4, 2), dp + ctx)
    act, col, row = P(dp, ctx, None), P(dp, ctx), P(ctx, dp)
    flat, gains = P(dp + ctx, None), P(None, dp + ctx)
    weights = (col,) * 3 + (flat,) * 6 + (row,) * 3 + (col,) * 6 + (row,) * 3 + (gains,) * 3
    return jax.shard_map(
        shards,
        mesh=fine,
        in_specs=(act, act) + weights,
        out_specs=(act, act) + weights,
        check_vma=False,
    )
```

```python
import functools

import jax
import jax.numpy as jnp
from jax import lax
from jax.experimental import pallas as pl
from jax.experimental.pallas import tpu as pltpu
from jax.sharding import Mesh
from jax.sharding import PartitionSpec as P

D = 2048
HEADS = 32
KV_HEADS = 4
HD = 64
FF = 5632
SEQ_LEN = 1024
STEP = 10

EPS = 1e-05
BETA_ONE = 0.9
BETA_TWO = 0.95
ADAM_EPS = 1e-08
DECAY = 0.1

ROWS = 128
HID = FF // 8
TILES = 6
PAD = TILES * 128
WIDE = 2 * HID
QW = 256
AW = 384
BF = jnp.bfloat16
F32 = jnp.float32
MIB = 2**20


def params(limit=56, **more):
    return pltpu.CompilerParams(vmem_limit_bytes=limit * MIB, **more)


def cost(flops, nbytes, trans=0):
    return pl.CostEstimate(flops=int(flops), bytes_accessed=int(nbytes), transcendentals=int(trans))


def dot(left, right):
    return jnp.dot(left, right, preferred_element_type=F32)


def dot_cols(left, right):
    return lax.dot_general(left, right, (((1,), (1,)), ((), ())), preferred_element_type=F32)


def dot_rows(left, right):
    return lax.dot_general(left, right, (((0,), (0,)), ((), ())), preferred_element_type=F32)


def swap_halves(v):
    width = v.shape[-1]
    lane = lax.broadcasted_iota(jnp.int32, v.shape, v.ndim - 1)
    return jnp.where(
        lane % HD < HD // 2,
        pltpu.roll(v, width - HD // 2, v.ndim - 1),
        pltpu.roll(v, HD // 2, v.ndim - 1),
    )


def ring(axis, k):
    return functools.partial(
        lax.ppermute, axis_name=axis, perm=[(i, (i + k) % 4) for i in range(4)]
    )


def other_core(v):
    return lax.ppermute(v, "core", [(0, 1), (1, 0)])


def spread_z(v):
    return [v, ring("z", 1)(v), ring("z", 2)(v), ring("z", 3)(v)]


def spread(v):
    own = spread_z(v)
    return own + [other_core(t) for t in own]


def swap_blocks(v, axes):
    return lax.all_to_all(v, axes, split_axis=0, concat_axis=0, tiled=True)


ANY = pl.BlockSpec(memory_space=pltpu.HBM)
HELD = [pltpu.VMEM((4, 2 * ROWS, D), BF), pltpu.SemaphoreType.DMA((8,))]


def block_copy(halves, blocks, held, sems, k, half, source=None):
    source = blocks[4 * half + k] if source is None else source
    rows = pl.ds(pl.multiple_of(halves[half] * ROWS, ROWS), ROWS)
    return pltpu.make_async_copy(source, held.at[k, rows], sems.at[4 * half + k])


def start_blocks(halves, blocks, held, sems, at):
    for k in at:
        for half in range(2):
            block_copy(halves, blocks, held, sems, k, half).start()


def wait_blocks(halves, blocks, held, sems):
    step = pl.program_id(0)
    for half in range(2):
        block_copy(halves, blocks, held, sems, step, half, blocks[0]).wait()
    return held.at[step]


def load_blocks(halves, blocks, held, sems):
    @pl.when(pl.program_id(0) == 0)
    def _():
        start_blocks(halves, blocks, held, sems, range(4))

    return wait_blocks(halves, blocks, held, sems)


def by_block(width):
    return pl.BlockSpec((2 * ROWS, width), lambda i, where: (where[i], 0))


def by_step(width):
    return pl.BlockSpec((ROWS, width), lambda i, *_: (i, 0))


def whole(*shape):
    return pl.BlockSpec(shape, lambda i, *_: (0,) * len(shape))


def shape_of(shape, kind=BF):
    return jax.ShapeDtypeStruct(shape, kind)


def blocks_call(
    kernel, where, blocks, operands, in_specs, out_specs, outs, flops, behind=(), through=(), scratch=None
):
    n_in, n_out, n_more = 8 + len(operands), len(outs), len(behind) + len(through)

    def body(where, *refs):
        refs = list(refs)
        del refs[n_in + n_more + n_out : n_in + n_more + n_out + len(through)]
        del refs[n_in : n_in + n_more]
        kernel(where, *refs)

    nbytes = 4 * MIB + sum(o.size * o.dtype.itemsize for o in outs)
    nbytes += sum(o.size * o.dtype.itemsize for o in operands)
    first = 1 + n_in + len(behind)
    return pl.pallas_call(
        body,
        grid_spec=pltpu.PrefetchScalarGridSpec(
            num_scalar_prefetch=1,
            grid=(4,),
            in_specs=[ANY] * 8 + in_specs + [ANY] * n_more,
            out_specs=out_specs + [ANY] * len(through),
            scratch_shapes=scratch or HELD,
        ),
        out_shape=outs + [shape_of(v.shape, v.dtype) for v in through],
        input_output_aliases={first + i: n_out + i for i in range(len(through))},
        compiler_params=params(),
        cost_estimate=cost(flops, nbytes),
        name=kernel.__name__,
    )(where, *blocks, *operands, *behind, *through)


def small_kernel(key, value, gains, out):
    cols = gains[...].astype(BF).astype(F32)
    cols = jnp.concatenate([cols, jnp.zeros((6, 16), F32)], axis=0)
    cols = jnp.concatenate([cols, jnp.zeros((8, 112), F32)], axis=1)
    cols = jnp.concatenate([cols, jnp.zeros((120, 128), F32)], axis=0).T[:16].astype(BF)
    for h in range(KV_HEADS):
        at = slice(HD * h, HD * (h + 1))
        block = jnp.concatenate([key[:, at].astype(BF), value[:, at].astype(BF), cols], axis=1)
        out[32 * h : 32 * h + 16] = block
        out[32 * h + 16 : 32 * h + 32] = block


def small_call(key, value, gains):
    return pl.pallas_call(
        small_kernel,
        out_shape=shape_of((ROWS, 256)),
        compiler_params=params(),
        cost_estimate=cost(0, 1 << 17),
        name="small_kernel",
    )(key, value, gains)


def weights_kernel(kvg, query, mixed, gate, up, down, attend_out, copies, ffn_out):
    gain = kvg[:, 128:129].astype(F32)
    attend_out[:, :QW] = (query[...].astype(BF).astype(F32) * gain).astype(BF)
    attend_out[:, QW:AW] = (kvg[:, :128].astype(F32) * gain).astype(BF)
    attend_out[:, AW:] = mixed[...].T.astype(BF)
    for i in range(16):
        copies[ROWS * i : ROWS * (i + 1)] = attend_out[...]
    gain = kvg[:, 129:130].astype(F32)
    for j in range(TILES):
        rows = slice(128 * j, min(128 * (j + 1), HID))
        parts = [ref[rows] for ref in (gate, up)]
        if j == TILES - 1:
            parts = [jnp.concatenate(parts, axis=0)]
        for s, part in enumerate(parts):
            at = PAD + 256 * j + 128 * s
            part = part.T.astype(BF).astype(F32) * gain
            ffn_out[:, at : at + 128] = part.astype(BF)
        part = down[rows]
        if j == TILES - 1:
            part = jnp.concatenate([part, jnp.zeros((PAD - HID, 128), F32)], axis=0)
        ffn_out[:, 128 * j : 128 * (j + 1)] = part.T.astype(BF)


def weights_call(*operands):
    return pl.pallas_call(
        weights_kernel,
        out_shape=[
            shape_of((ROWS, AW + QW)),
            shape_of((D, AW + QW)),
            shape_of((ROWS, PAD + WIDE)),
        ],
        compiler_params=params(),
        cost_estimate=cost(0, 5 * MIB),
        name="weights_kernel",
    )(*operands)


def norm_back_kernel(n_through, *refs):
    parts, (x, base), outs = refs[:4], refs[4:6], refs[6 + n_through : len(refs) - n_through]
    v = x[...].astype(F32)
    inv = lax.rsqrt(jnp.mean(v * v, axis=-1, keepdims=True) + EPS)
    unit = v * inv
    u = functools.reduce(jnp.add, [ref[...].astype(F32) for ref in parts])
    out = base[...].astype(F32) + inv * (u - unit * jnp.mean(u * unit, axis=-1, keepdims=True))
    for ref in outs:
        ref[...] = out.astype(ref.dtype)


def norm_back_call(parts, x, base, kinds, through=()):
    rows = pl.BlockSpec((ROWS // 2, D), lambda i: (i, 0))
    return pl.pallas_call(
        functools.partial(norm_back_kernel, len(through)),
        grid=(2,),
        in_specs=[rows] * 6 + [ANY] * len(through),
        out_specs=[rows] * len(kinds) + [ANY] * len(through),
        out_shape=[shape_of((ROWS, D), kind) for kind in kinds]
        + [shape_of(v.shape, v.dtype) for v in through],
        input_output_aliases={6 + i: len(kinds) + i for i in range(len(through))},
        compiler_params=params(),
        cost_estimate=cost(0, 5 * MIB),
        name="norm_back_kernel",
    )(*parts, x, base, *through)


def send_products(left, w, start, end, held, sems, outs):
    copies = []
    half = left.shape[0] // 2
    for t in range(4):
        held[t] = dot_cols(left, w[512 * t : 512 * (t + 1), start:end]).astype(BF)
        for i, out in enumerate(outs):
            copy = pltpu.make_async_copy(
                held.at[t, pl.ds(i * half, half)], out.at[:, pl.ds(512 * t, 512)], sems.at[i, t]
            )
            copy.start()
            copies.append(copy)
    for copy in copies:
        copy.wait()


def pick_rows(ref, order):
    return jnp.concatenate(
        [ref[pl.ds(pl.multiple_of(order[k] * ROWS, ROWS), ROWS)] for k in range(8)], axis=0
    )


SENT = [pltpu.VMEM((4, SEQ_LEN, 512), BF), pltpu.SemaphoreType.DMA((2, 4))]


def front_kernel(order, rows, *refs):
    w, tcos, tsin, q_out, kv_out, inv_out, out, lse, *outs, held, sems = refs
    step = pl.program_id(0)
    at = pl.ds(pl.multiple_of(step * 2 * ROWS, 2 * ROWS), 2 * ROWS)

    y = dot(rows[...], w[:, :AW])
    x = rows[...].astype(F32)
    inv = lax.rsqrt(jnp.mean(x * x, axis=-1, keepdims=True) + EPS)
    inv_out[at] = jnp.broadcast_to(inv, (2 * ROWS, 128))
    cos, sin = tcos[...] * inv, tsin[...] * inv
    for j in range(2):
        part = y[:, j * 128 : (j + 1) * 128]
        q_out[at, j * 128 : (j + 1) * 128] = (part * cos + swap_halves(part) * sin).astype(BF)
    part = y[:, 256:384]
    is_key = lax.broadcasted_iota(jnp.int32, part.shape, 1) < HD
    kv_out[at] = jnp.where(is_key, part * cos + swap_halves(part) * sin, part * inv).astype(BF)

    @pl.when(step == 3)
    def _():
        attend_kernel(q_out, kv_out, out, lse)
        send_products(pick_rows(out, order), w, AW, AW + QW, held, sems, outs)


def front_call(order, rows, w, tcos, tsin):
    def block(width):
        return pl.BlockSpec((2 * ROWS, width), lambda i, *_: (i, 0))

    shapes = [(QW, BF), (128, BF), (128, F32), (QW, BF), (128, F32)]
    return pl.pallas_call(
        front_kernel,
        grid_spec=pltpu.PrefetchScalarGridSpec(
            num_scalar_prefetch=1,
            grid=(4,),
            in_specs=[block(D), whole(D, AW + QW)] + [block(128)] * 2,
            out_specs=[whole(SEQ_LEN, w) for w, _ in shapes] + [ANY] * 2,
            scratch_shapes=SENT,
        ),
        out_shape=[shape_of((SEQ_LEN, w), t) for w, t in shapes] + [shape_of((4 * ROWS, D))] * 2,
        compiler_params=params(),
        cost_estimate=cost(8e9, 16 * MIB, 2 * MIB),
        name="front_kernel",
    )(order, rows, w, tcos, tsin)


def put_halves(outs, value, cols=slice(None)):
    outs[0][:, cols] = value[:ROWS]
    outs[1][:, cols] = value[ROWS:]


def middle_kernel(where, *refs):
    blocks, grad_all, w, refs = refs[:8], refs[8], refs[9], refs[10:]
    hiddens, grads, outs = refs[:2], refs[2:4], refs[4:6]
    held, sems, grad_held, grad_sems, wide, down, w_sems, both, sent, sent_sems = refs[6:]
    step = pl.program_id(0)
    first = step == 0
    grad_blocks = [
        grad_all.at[pl.ds(pl.multiple_of(where[5 + i] * ROWS, ROWS), ROWS)] for i in range(8)
    ]
    loads = ((0, 1), blocks, held, sems), ((0, 1), grad_blocks, grad_held, grad_sems)

    def w_copies(j):
        n = min(512, WIDE - 512 * j)
        return (
            pltpu.make_async_copy(
                w.at[:, pl.ds(PAD + 512 * j, n)], wide.at[j, :, pl.ds(0, n)], w_sems.at[0, j]
            ),
            pltpu.make_async_copy(w.at[:, pl.ds(256 * j, 256)], down.at[j], w_sems.at[1, j]),
        )

    @pl.when(first)
    def _():
        for j in range(4):
            for load in loads:
                start_blocks(*load, (j,))
            if j < TILES // 2:
                for copy in w_copies(j):
                    copy.start()

    x, c = (wait_blocks(*load) for load in loads)
    for j in range(TILES // 2):

        @pl.when(first)
        def _():
            for copy in w_copies(j):
                copy.wait()

        backs = dot(c[...], down[j])
        for i in range(2):
            t = 2 * j + i
            last = t == TILES - 1
            n = 128 if last else 256
            y = dot(x[...], wide[j, :, 256 * i : 256 * i + n])
            gate, up = y[:, :128], pltpu.roll(y, HD, 1) if last else y[:, 128:]
            back = backs[:, 128 * i : 128 * (i + 1)]
            sigma = jax.nn.sigmoid(gate)
            swish = gate * sigma
            hidden = swish * up
            g = back * up * (sigma * (1.0 + gate * (1.0 - sigma)))
            u = back * swish
            if last:
                valid = lax.broadcasted_iota(jnp.int32, g.shape, 1) < HD
                hidden = jnp.where(valid, hidden, 0.0)
                g = jnp.where(valid, g, pltpu.roll(u, HD, 1)).astype(BF)
            else:
                g = jnp.concatenate([g.astype(BF), u.astype(BF)], axis=1)
            put_halves(hiddens, hidden.astype(BF), slice(128 * t, 128 * (t + 1)))
            cols = slice(256 * t, 256 * t + n)
            put_halves(grads, g, cols)
            both[step, :, cols] = g[ROWS:]
            both[4 + step, :, cols] = g[:ROWS]

    @pl.when(step == 3)
    def _():
        left = both[...].reshape(SEQ_LEN, WIDE)
        copies = []
        for t in range(4):
            at = slice(512 * t, 512 * (t + 1))
            y = 0.0
            for j in range(TILES // 2):
                n = min(512, WIDE - 512 * j)
                y = y + dot_cols(left[:, 512 * j : 512 * j + n], wide[j, at, :n])
            sent[t] = y.astype(BF)
            for i, out in enumerate(outs):
                copy = pltpu.make_async_copy(
                    sent.at[t, pl.ds(i * 4 * ROWS, 4 * ROWS)],
                    out.at[:, pl.ds(512 * t, 512)],
                    sent_sems.at[i, t],
                )
                copy.start()
                copies.append(copy)
        for copy in copies:
            copy.wait()


def middle_call(where, blocks, grad_all, w):
    return blocks_call(
        middle_kernel,
        where,
        blocks,
        (grad_all, w),
        [ANY] * 2,
        [by_step(PAD)] * 2 + [by_step(WIDE)] * 2 + [ANY] * 2,
        [shape_of((4 * ROWS, PAD))] * 2
        + [shape_of((4 * ROWS, WIDE))] * 2
        + [shape_of((4 * ROWS, D))] * 2,
        2 * SEQ_LEN * D * 5 * PAD,
        scratch=HELD * 2
        + [
            pltpu.VMEM((TILES // 2, D, 512), BF),
            pltpu.VMEM((TILES // 2, D, 256), BF),
            pltpu.SemaphoreType.DMA((2, TILES // 2)),
            pltpu.VMEM((8, ROWS, WIDE), BF),
        ]
        + SENT,
    )


def partial_kernel(n_in, n_behind, n_through, order, *refs):
    w, (across, own) = refs[n_in], refs[n_in + 1 + n_behind + n_through :][:2]
    if n_in == 1:
        a = refs[0]
        left = jnp.concatenate(
            [a[pl.ds(pl.multiple_of(order[k] * ROWS, ROWS), ROWS)] for k in range(8)], axis=0
        )
    else:
        left = jnp.concatenate([refs[0][...], refs[1][...]], axis=0)
    y = dot_cols(left, w[...]).astype(BF)
    across[...] = y[: 4 * ROWS]
    own[...] = y[4 * ROWS :]


def partial_call(order, a, w, col, tile, behind=(), through=()):
    depth, first = a[0].shape[1], 2 + len(a) + len(behind)
    return pl.pallas_call(
        functools.partial(partial_kernel, len(a), len(behind), len(through)),
        grid_spec=pltpu.PrefetchScalarGridSpec(
            num_scalar_prefetch=1,
            grid=(D // tile,),
            in_specs=[whole(*v.shape) for v in a]
            + [pl.BlockSpec((tile, depth), lambda i, *_: (i, col))]
            + [ANY] * (len(behind) + len(through)),
            out_specs=[pl.BlockSpec((4 * ROWS, tile), lambda i, *_: (0, i))] * 2
            + [ANY] * len(through),
        ),
        out_shape=[shape_of((4 * ROWS, D))] * 2 + [shape_of(v.shape, v.dtype) for v in through],
        input_output_aliases={first + i: 2 + i for i in range(len(through))},
        compiler_params=params(),
        cost_estimate=cost(2 * 8 * ROWS * D * depth, 2 * depth * (D + 1024) + 4 * MIB),
        name="partial_kernel",
    )(order, *a, w, *behind, *through)


def add_kernel(n_behind, across, own, *refs):
    n = own.shape[0] // ROWS
    outs, (held, sems) = refs[n_behind : n_behind + n], refs[n_behind + n :]
    loads, stores = [], []
    for k in range(n):
        rows = pl.ds(k * ROWS, ROWS)
        loads.append(
            [
                pltpu.make_async_copy(ref.at[rows], held.at[i, k], sems.at[i, k])
                for i, ref in enumerate((across, own))
            ]
        )
        stores.append(pltpu.make_async_copy(held.at[2, k], outs[k], sems.at[2, k]))
    for pair in loads:
        for copy in pair:
            copy.start()
    for k in range(n):
        for copy in loads[k]:
            copy.wait()
        held[2, k] = (held[0, k].astype(F32) + held[1, k].astype(F32)).astype(BF)
        stores[k].start()
    for copy in stores:
        copy.wait()


def add_call(across, own, behind=()):
    n = own.shape[0] // ROWS
    return pl.pallas_call(
        functools.partial(add_kernel, len(behind)),
        in_specs=[ANY] * (2 + len(behind)),
        out_specs=[ANY] * n,
        out_shape=[shape_of((ROWS, D))] * n,
        scratch_shapes=[pltpu.VMEM((3, n, ROWS, D), BF), pltpu.SemaphoreType.DMA((3, n))],
        compiler_params=params(),
        cost_estimate=cost(0, 6 * own.size),
        name="add_kernel",
    )(across, own, *behind)


def scores_of(q, k, diagonal):
    s = dot_cols(q, k)
    if diagonal:
        row = lax.broadcasted_iota(jnp.int32, s.shape, 0) % ROWS
        s = jnp.where(row >= lax.broadcasted_iota(jnp.int32, s.shape, 1), s, -1e30)
    return s


def stack_heads(v):
    return jnp.concatenate([v[:, HD * h : HD * (h + 1)] for h in range(4)], axis=0)


def lay_heads(v):
    return jnp.concatenate([v[ROWS * h : ROWS * (h + 1)] for h in range(4)], axis=1)


def attend_kernel(q, kv, out, lse):
    key, value = kv[:, :HD], kv[:, HD:]
    lane = lax.broadcasted_iota(jnp.int32, (ROWS, 128), 1)
    for b in range(8):
        rows = slice(b * ROWS, (b + 1) * ROWS)
        mine = stack_heads(q[rows] * HD**-0.5)
        pieces = [(scores_of(mine, key[rows], True), value[rows])]
        if b:
            pieces.append((scores_of(mine, key[: b * ROWS], False), value[: b * ROWS]))
        top = functools.reduce(
            jnp.maximum, [jnp.max(s, axis=-1, keepdims=True) for s, _ in pieces]
        )
        total, mixed = 0.0, 0.0
        for s, v in pieces:
            p = jnp.exp(s - top)
            total = total + jnp.sum(p, axis=-1, keepdims=True)
            mixed = mixed + dot(p.astype(BF), v)
        out[rows] = lay_heads(mixed / total).astype(BF)
        log_total = top + jnp.log(total)
        spread_out = jnp.zeros((ROWS, 128), F32)
        for h in range(4):
            spread_out = jnp.where(lane == h, log_total[ROWS * h : ROWS * (h + 1)], spread_out)
        lse[rows] = spread_out


def attend_back_kernel(
    q, kv, lse, mixed_grad, tcos, tsin, inv, grad_out, scaled_out, held
):
    key, value = kv[:, :HD], kv[:, HD:]
    held[...] = jnp.zeros_like(held)

    def put(rows, cols, part, turn):
        part = jnp.where(turn, part * tcos[rows] - swap_halves(part) * tsin[rows], part)
        grad_out[rows, cols] = part.astype(BF)
        scaled_out[rows, cols] = (part * inv[rows]).astype(BF)

    for b in range(8):
        rows = slice(b * ROWS, (b + 1) * ROWS)
        mine = stack_heads(q[rows] * HD**-0.5)
        grad = stack_heads(mixed_grad[rows])
        log_total = jnp.concatenate([lse[rows, h : h + 1] for h in range(4)], axis=0)
        pieces = [(rows, True)] + ([(slice(0, b * ROWS), False)] if b else [])
        probs, back = [], []
        inner = 0.0
        for cols, diagonal in pieces:
            p = jnp.exp(scores_of(mine, key[cols], diagonal) - log_total)
            g = dot_cols(grad, value[cols])
            inner = inner + jnp.sum(p * g, axis=-1, keepdims=True)
            probs.append(p)
            back.append(g)
        total = 0.0
        for (cols, _), p, g in zip(pieces, probs, back):
            s_grad = (p * (g - inner)).astype(BF)
            total = total + dot(s_grad, key[cols])
            held[:HD, cols] += dot_rows(mine, s_grad)
            held[HD:, cols] += dot_rows(grad, p.astype(BF))
        wide = lay_heads(total * HD**-0.5)
        for j in range(2):
            put(rows, slice(128 * j, 128 * (j + 1)), wide[:, 128 * j : 128 * (j + 1)], True)
    is_key = lax.broadcasted_iota(jnp.int32, (ROWS, 128), 1) < HD
    for b in range(8):
        rows = slice(b * ROWS, (b + 1) * ROWS)
        put(rows, slice(QW, AW), held[:, rows].T, is_key)


def back_kernel(where, *refs):
    blocks, refs = refs[:8], refs[8:]
    w, q, kv, lse, tcos, tsin, inv, attended, rows, scaled, *outs, wgrad_out = refs[:13]
    held, sems, mixed_grad, grad, kv_held, rows_held, rows_sem, wgrad, wgrad_sems = refs[13:22]
    sent, sent_sems = refs[22:]
    step = pl.program_id(0)
    rows_copy = pltpu.make_async_copy(rows, rows_held, rows_sem)
    x = load_blocks((where[4], 1 - where[4]), blocks, held, sems)

    @pl.when(step == 0)
    def _():
        rows_copy.start()

    def place(k):
        return pl.ds(pl.multiple_of(where[k] * 2 * ROWS, 2 * ROWS), 2 * ROWS)

    mixed_grad[place(step)] = dot(x[...], w[:, AW:]).astype(BF)

    @pl.when(step == 3)
    def _():
        attend_back_kernel(q, kv, lse, mixed_grad, tcos, tsin, inv, grad, scaled, kv_held)
        rows_copy.wait()
        copies = []
        for t in range(4):
            cols = slice(512 * t, 512 * (t + 1))
            wgrad[t, :, :AW] = dot_rows(rows_held[:, cols], scaled[...]).astype(BF)
            y = 0.0
            for k in range(4):
                y = y + dot_rows(held[k, :, cols], attended[place(k)])
            wgrad[t, :, AW:] = y.astype(BF)
            copy = pltpu.make_async_copy(
                wgrad.at[t], wgrad_out.at[pl.ds(512 * t, 512)], wgrad_sems.at[t]
            )
            copy.start()
            copies.append(copy)
        left = pick_rows(grad, [where[5 + k] for k in range(8)])
        send_products(left, w, 0, AW, sent, sent_sems, outs)
        for copy in copies:
            copy.wait()


BACK_COST = 1.43e11


def back_call(where, blocks, operands, rows):
    widths = [QW, 128, 128, 128, 128, 128, QW]
    return blocks_call(
        back_kernel,
        where,
        blocks,
        (*operands, rows),
        [whole(D, AW + QW)] + [whole(SEQ_LEN, w) for w in widths] + [ANY],
        [whole(SEQ_LEN, AW)] + [ANY] * 3,
        [shape_of((SEQ_LEN, AW))] + [shape_of((4 * ROWS, D))] * 2 + [shape_of((D, AW + QW))],
        BACK_COST,
        scratch=HELD
        + [
            pltpu.VMEM((SEQ_LEN, QW), BF),
            pltpu.VMEM((SEQ_LEN, AW), BF),
            pltpu.VMEM((128, SEQ_LEN), F32),
            pltpu.VMEM((SEQ_LEN, D), BF),
            pltpu.SemaphoreType.DMA(()),
            pltpu.VMEM((4, 512, AW + QW), BF),
            pltpu.SemaphoreType.DMA((4,)),
        ]
        + SENT,
    )


def wgrad_kernel(counts, order, *refs):
    out = refs[-1]
    at, ref = 0, 0
    for group in counts:
        total = 0.0
        for n in group:
            x = refs[ref : ref + n]
            x = x[0][...] if n == 1 else jnp.concatenate([v[...] for v in x], axis=0)
            total = total + dot_rows(x, refs[ref + n][...])
            ref += n + 1
        out[:, at : at + total.shape[1]] = total.astype(BF)
        at += total.shape[1]


def wgrad_call(order, tile, *groups, behind=()):
    in_specs, operands, width = [], [], 0
    for group in groups:
        for i, (x, g) in enumerate(group):
            if isinstance(x, tuple):
                in_specs += [
                    pl.BlockSpec((ROWS, tile), lambda i, order, at=at: (order[at], i))
                    for at in x[1]
                ]
                group[i] = ([x[0]] * len(x[1]), g)
            else:
                in_specs += [pl.BlockSpec((v.shape[0], tile), lambda i, *_: (0, i)) for v in x]
            in_specs.append(whole(*g.shape))
            operands += [*group[i][0], g]
        width += group[0][1].shape[1]
    counts = tuple(tuple(len(x) for x, _ in group) for group in groups)
    return pl.pallas_call(
        functools.partial(wgrad_kernel, counts),
        grid_spec=pltpu.PrefetchScalarGridSpec(
            num_scalar_prefetch=1,
            grid=(D // tile,),
            in_specs=in_specs + [ANY] * len(behind),
            out_specs=pl.BlockSpec((tile, width), lambda i, *_: (i, 0)),
        ),
        out_shape=shape_of((D, width)),
        compiler_params=params(),
        cost_estimate=cost(
            2 * SEQ_LEN * D * width, 4 * MIB * len(groups) + 2 * width * (SEQ_LEN + D)
        ),
        name="wgrad_kernel",
    )(order, *operands, *behind)


WIDE_RATE = 2.0 * D ** (-0.5)
OUT_RATE = 2.0 * max(1, 16 * D // SEQ_LEN) ** (-0.5)
DOWN_RATE = 2.0 * FF ** (-0.5)


def adamw(ins, outs, gradient, rate, decay=DECAY, at=slice(None)):
    weight, first, second = (ref[at] for ref in ins)
    first_new = BETA_ONE * first + (1.0 - BETA_ONE) * gradient
    second_new = BETA_TWO * second + (1.0 - BETA_TWO) * gradient * gradient
    first_hat = first_new / (1.0 - BETA_ONE**STEP)
    second_hat = second_new / (1.0 - BETA_TWO**STEP)
    outs[0][at] = weight - rate * (first_hat / (jnp.sqrt(second_hat) + ADAM_EPS) + decay * weight)
    outs[1][at] = first_new
    outs[2][at] = second_new


def step_call(kernel, operands, states, extra):
    flat = [v for group in states for v in group]
    return pl.pallas_call(
        kernel,
        out_shape=[shape_of(v.shape, F32) for v in flat] + list(extra),
        compiler_params=params(),
        cost_estimate=cost(0, 8 * sum(v.size for v in flat)),
        name=kernel.__name__,
    )(*operands, *flat)


def wide_step_kernel(sums, kvg, *refs):
    ins, outs = refs[:9], refs[9:]
    gain = kvg[:, 129:130].astype(F32)
    for j in range(TILES):
        at = slice(128 * j, min(128 * (j + 1), HID))
        n = at.stop - at.start
        g = [sums[:, PAD + 256 * j : PAD + 256 * j + 128].astype(F32) * gain]
        if j < TILES - 1:
            g.append(sums[:, PAD + 256 * j + 128 : PAD + 256 * (j + 1)].astype(F32) * gain)
        g = [v.T for v in g]
        if j == TILES - 1:
            g = [g[0][:n], g[0][n:]]
        g.append(sums[:, 128 * j : 128 * (j + 1)].astype(F32).T[:n])
        for s, rate in enumerate((WIDE_RATE, WIDE_RATE, DOWN_RATE)):
            adamw(ins[3 * s : 3 * s + 3], outs[3 * s : 3 * s + 3], g[s], rate, at=at)


def sum_blocks(parts):
    total = parts[:ROWS].astype(F32)
    for i in range(1, 16):
        total = total + parts[ROWS * i : ROWS * (i + 1)].astype(F32)
    return total


def query_step_kernel(parts, kvg, _, *refs):
    ins, outs = refs[:6], refs[6:12]
    g = sum_blocks(parts)
    adamw(ins[3:], outs[3:], g[:, AW:].T, OUT_RATE)
    adamw(ins[:3], outs[:3], g[:, :QW] * kvg[:, 128:129].astype(F32), WIDE_RATE)


def tail_kernel(parts, w, kvg, wide_sums, w_wide, _, tail):
    g = sum_blocks(parts)
    gain_one_sum = jnp.sum(g * w[:, :AW].astype(F32), axis=-1, keepdims=True)
    wide = wide_sums[:, PAD:].astype(F32) * w_wide[:, PAD:].astype(F32)
    gain_two_sum = jnp.sum(wide, axis=-1, keepdims=True)
    tail[:, :128] = g[:, QW:] * kvg[:, 128:129].astype(F32)
    lane = lax.broadcasted_iota(jnp.int32, (ROWS, 128), 1)
    tail[:, 128:] = jnp.where(lane == 0, gain_one_sum, gain_two_sum)


def tail_call(parts, w, kvg, wide_sums, w_wide, behind):
    return pl.pallas_call(
        tail_kernel,
        grid=(1,),
        in_specs=[whole(D, AW)]
        + [whole(*v.shape) for v in (w, kvg, wide_sums, w_wide)]
        + [ANY],
        out_specs=whole(ROWS, 256),
        out_shape=shape_of((ROWS, 256), F32),
        compiler_params=params(),
        cost_estimate=cost(0, 3 * MIB),
        name="tail_kernel",
    )(parts, w, kvg, wide_sums, w_wide, behind)


def last_step_kernel(parts, *refs):
    heads = [parts[2 * h] + parts[2 * h + 1] for h in range(KV_HEADS)]
    key = jnp.concatenate([v[:, :HD] for v in heads], axis=1)
    value = jnp.concatenate([v[:, HD : 2 * HD] for v in heads], axis=1)
    adamw(refs[0:3], refs[9:12], key, WIDE_RATE)
    adamw(refs[3:6], refs[12:15], value, WIDE_RATE)
    sums = functools.reduce(jnp.add, [v[:, 128:] for v in heads])
    sums = jnp.concatenate([sums, jnp.zeros((112, 128), F32)], axis=0).T[:2, :16]
    sums = sums / refs[6][...].astype(BF).astype(F32)
    adamw(refs[6:9], refs[15:18], sums, 0.3, 0.0)


def rotary():
    positions = jnp.arange(SEQ_LEN).astype(F32)
    frequency = 10000.0 ** (-2.0 * jnp.arange(HD // 2).astype(F32) / HD)
    angles = positions[:, None] * frequency[None, :]
    cos, sin = jnp.cos(angles), jnp.sin(angles)
    return (
        jnp.concatenate([cos] * 4, axis=1),
        jnp.concatenate([-sin, sin, -sin, sin], axis=1),
    )


def shards(
    tokens,
    cotangent,
    w_query,
    query_first,
    query_second,
    w_key,
    key_first,
    key_second,
    w_value,
    value_first,
    value_second,
    w_out,
    out_first,
    out_second,
    w_gate,
    gate_first,
    gate_second,
    w_up,
    up_first,
    up_second,
    w_down,
    down_first,
    down_second,
    norm_gains,
    gains_first,
    gains_second,
):
    z, core = lax.axis_index("z"), lax.axis_index("core")
    dp, ctx = ("y", "x"), ("z", "core")
    back = (z - jnp.arange(4)) % 4
    order = jnp.concatenate([2 * back + 1 - core, 2 * back + core]).astype(jnp.int32)
    where = jnp.concatenate([back, core[None], order[4:8], order[:4]]).astype(jnp.int32)
    back_where = jnp.concatenate([back, core[None], order[:8]]).astype(jnp.int32)

    small = small_call(w_key, w_value, norm_gains)
    kvg = swap_blocks(small, ctx)

    tcos, tsin = rotary()
    tokens_all = lax.all_gather(tokens[0], ctx, axis=0, tiled=True)
    grad_all = lax.all_gather(cotangent[0], ctx, axis=0, tiled=True)
    w_attend, copies, w_ffn = weights_call(kvg, w_query, w_out, w_gate.T, w_up.T, w_down)
    all_attend = swap_blocks(copies, dp)
    all_ffn = lax.all_gather(w_ffn, dp, axis=0, tiled=True)
    query, key_value, inv_all, attended, lse, *mixed_parts = front_call(
        order, tokens_all, all_attend, tcos, tsin
    )
    all_ffn = lax.all_gather(w_ffn, dp, axis=0, tiled=True)

    def reduce_core(partials):
        across = other_core(partials[0])
        at = [slice(k * ROWS, (k + 1) * ROWS) for k in range(4)]
        return [(across[a].astype(F32) + partials[1][a].astype(F32)).astype(BF) for a in at]

    def reduce_z(parts):
        return [parts[0]] + [ring("z", 4 - k)(parts[k]) for k in (1, 2, 3)]

    def total(parts):
        return functools.reduce(jnp.add, [t.astype(F32) for t in parts])

    mixed_parts = reduce_core(mixed_parts)
    middle = tokens[0].astype(F32) + total(reduce_z(mixed_parts))
    inv_second = lax.rsqrt(jnp.mean(middle * middle, axis=-1, keepdims=True) + EPS)
    unit_second = middle * inv_second

    mid_blocks = spread(unit_second.astype(BF))
    hidden0, hidden1, wide0, wide1, *wide_parts = middle_call(
        where, mid_blocks, grad_all, all_ffn
    )
    wide_parts = reduce_core(wide_parts)
    mid_parts = reduce_z(wide_parts)
    ffn_wgrad = wgrad_call(
        order,
        256,
        [((grad_all, range(4, 8)), hidden0), ((grad_all, range(4)), hidden1)],
        [(mid_blocks[:4], wide0), (mid_blocks[4:], wide1)],
        behind=wide_parts[:1],
    )
    down_sums = partial_call(order, (hidden1, hidden0), all_ffn, 0, 512, wide_parts[:1])
    middle_grad, middle_low, *down_sums = norm_back_call(
        mid_parts, middle, cotangent[0], (F32, BF), down_sums
    )
    ffn_sum = lax.psum_scatter(ffn_wgrad, dp, scatter_dimension=0, tiled=True)
    mid_grad_blocks = spread(middle_low)
    _, *in_parts, attend_wgrad = back_call(
        back_where,
        mid_grad_blocks,
        (all_attend, query, key_value, lse, tcos, tsin, inv_all, attended),
        tokens_all,
    )
    attend_parts = swap_blocks(attend_wgrad, dp)
    in_parts = add_call(other_core(in_parts[0]), in_parts[1])
    in_parts = reduce_z(in_parts)
    (input_grad,) = norm_back_call(in_parts, tokens[0], middle_grad, (BF,))
    down_parts = add_call(other_core(down_sums[0]), down_sums[1], in_parts[1:2])
    output = middle + total(reduce_z(down_parts))

    wide_new = step_call(
        wide_step_kernel,
        (ffn_sum, kvg),
        (
            (w_gate.T, gate_first.T, gate_second.T),
            (w_up.T, up_first.T, up_second.T),
            (w_down, down_first, down_second),
        ),
        [],
    )
    wide_new = [v.T for v in wide_new[:6]] + list(wide_new[6:])
    tail = tail_call(attend_parts, w_attend, kvg, ffn_sum, w_ffn, wide_new[6])
    query_new = step_call(
        query_step_kernel,
        (attend_parts, kvg, tail),
        ((w_query, query_first, query_second), (w_out, out_first, out_second)),
        [],
    )
    tail = swap_blocks(tail, ctx).reshape(8, 16, 256)
    last_new = step_call(
        last_step_kernel,
        (tail,),
        (
            (w_key, key_first, key_second),
            (w_value, value_first, value_second),
            (norm_gains, gains_first, gains_second),
        ),
        [],
    )
    return (
        output.astype(BF)[None],
        input_grad[None],
        *query_new[:3],
        *last_new[:6],
        *query_new[3:],
        *wide_new,
        *last_new[6:],
    )


def solution(mesh):
    dp, ctx = ("y", "x"), ("z", "core")
    fine = Mesh(mesh.devices.reshape(4, 4, 4, 2), dp + ctx)
    act, col, row = P(dp, ctx, None), P(dp, ctx), P(ctx, dp)
    flat, gains = P(dp + ctx, None), P(None, dp + ctx)
    weights = (col,) * 3 + (flat,) * 6 + (row,) * 3 + (col,) * 6 + (row,) * 3 + (gains,) * 3
    return jax.shard_map(
        shards,
        mesh=fine,
        in_specs=(act, act) + weights,
        out_specs=(act, act) + weights,
        check_vma=False,
    )
```
